256 devices in a mesh: half: 2 (over x_hi), gx: 16 (over z, x_lo), gy: 8 (over y, core).
Axes of the slice: x: 4 (x_hi: 2, x_lo: 2; x = x_hi * 2 + x_lo), y: 4, z: 8, core: 2. Of those that a mesh axis runs over, the one named last changes fastest.
Arguments:
- grid_state: float32 [2, 4, 8, 256, 2048], P('half', None, None, 'gx', 'gy'), may hold values from 0.1 to 1.5
- materials: int32 [2, 8, 256, 2048], P('half', None, 'gx', 'gy'), may hold values from 0 to 3
- contacts: int32 [256, 2048], P('gx', 'gy'), may hold values 0 or 1
- received_sheets: float32 [2, 256, 2048], P('half', 'gx', 'gy'), may hold values from 0 to 2
Outputs:
- final_state: float32 [2, 4, 8, 256, 2048], P('half', None, None, 'gx', 'gy')
- outgoing: float32 [2, 256, 2048], P('half', 'gx', 'gy')
The draws below stay inside these ranges and needn't reach their ends.
All inputs are finite; a program needn't handle non-finite values. No bound on the sum of `contacts` on one device may be relied on, other than what follows from the above.
Results may differ from the reference program's by a relative error of at most 0.0001.
Values sent between devices are 32-bit elements; how exact they have to be, the bound alone decides.
No kernel may reach another device: no remote copies, remote signals or barrier semaphores. Data moves between devices by JAX's collectives and lax.ppermute only.
A program may use at most 64 MiB of HBM per device.

```python
import jax
import jax.numpy as jnp

LAYERS = 8
NEWTON = 1
RELAX = 1
STEPS = 2
NX = 256
NY = 2048


def place_ends(result, stream_key, low, top_value):
    longest = result.shape.index(max(result.shape))
    spots = []
    for shift in (0, 1):
        where = [jax.random.randint(jax.random.fold_in(stream_key, axis), (), 0, length) for axis, length in enumerate(result.shape)]
        where[longest] = (where[longest] + shift) % result.shape[longest]
        spots.append(tuple(where))
    return result.at[spots[0]].set(low).at[spots[1]].set(top_value)


def steps_of(stream_key, extent, cuts, smallest, high):
    loudness = 1.0
    for dim, shards_of in cuts:
        steps = jax.random.uniform(jax.random.fold_in(jax.random.fold_in(stream_key, 6), dim), (shards_of,), jnp.float32, smallest / len(cuts), high / len(cuts))
        loudness = loudness * jnp.repeat(jnp.exp(steps), extent[dim] // shards_of).reshape((-1,) + (1,) * (len(extent) - 1 - dim))
    return loudness


def setup_inputs(seed: int = 0) -> dict:
    keys = jax.random.split(jax.random.key(seed), 5)
    grid_state = jnp.clip(0.1 + 1.4 * jax.random.uniform(keys[0], (2, 4, LAYERS, NX, NY), jnp.float32) ** steps_of(keys[0], (2, 4, LAYERS, NX, NY), ((0, 2), (3, 16), (4, 8)), -0.2, 0.2), 0.1, 1.5)
    materials = place_ends(jax.random.randint(keys[1], (2, LAYERS, NX, NY), 0, 4), jax.random.fold_in(keys[1], 1), 0, 3).astype(jnp.int32)
    contacts = place_ends((jax.random.randint(keys[2], (NX, NY), 0, 4) < 1).astype(jnp.int32), jax.random.fold_in(keys[2], 1), 0, 1)
    received_sheets = jnp.clip(2.0 * jax.random.uniform(keys[3], (2, NX, NY), jnp.float32) ** steps_of(keys[3], (2, NX, NY), ((0, 2), (1, 16), (2, 8)), -0.2, 0.2), 0.0, 2.0)
    return dict(grid_state=grid_state, materials=materials, contacts=contacts, received_sheets=received_sheets)


OVERSHOOT = 0.8
OMEGA_HEAT = 0.9
POISSON = 0.7
RATE = 0.3
HEATING = 0.05
WARMTH_DIFFUSE = 0.5
DECAY_TIME = 2.0
SPEED_DROP = 0.3
HEAT_GAIN = 0.5
DOPING = (1.5, -1.5, 0.6, -0.6)
MOB_ELEC = (1.0, 0.35, 0.7, 0.5)
MOB_HOLE = (0.4, 0.8, 0.3, 0.6)
CONDUCT = (1.0, 0.15, 2.5, 0.5)
CAPACITY = (0.6, 1.2, 0.4, 0.9)


def lookup(material, table):
    summed = jnp.zeros(material.shape, jnp.float32)
    for code_value in range(4):
        summed = summed + jnp.where(material == code_value, table[code_value], 0.0)
    return summed


def layer_faces(layers):
    layer_index = jnp.arange(layers)[:, None, None]
    has_above = (layer_index > 0).astype(jnp.float32)
    has_below = (layer_index < layers - 1).astype(jnp.float32)
    return layer_index, has_above, has_below


def semiconductor_pass(padded_mesh, linearized_pass, crystal_warmth, impurity_density, negative_drift_speed, positive_drift_speed, locked_flags, baseline_solution):
    layers = padded_mesh.shape[1]
    layer_index, has_above, has_below = layer_faces(layers)
    middle_cell = padded_mesh[:, :, 1:-1, 1:-1]
    electrostatic_field = middle_cell[0]
    negative_charges = middle_cell[1]
    positive_charge_density = middle_cell[2]
    charge_warmth = middle_cell[3]
    neighbours = [
        (padded_mesh[:, :, :-2, 1:-1], 1.0),
        (padded_mesh[:, :, 2:, 1:-1], 1.0),
        (padded_mesh[:, :, 1:-1, :-2], 1.0),
        (padded_mesh[:, :, 1:-1, 2:], 1.0),
        (jnp.concatenate([middle_cell[:, :1], middle_cell[:, :-1]], axis=1), has_above),
        (jnp.concatenate([middle_cell[:, 1:], middle_cell[:, -1:]], axis=1), has_below),
    ]
    summed_coefficient = 4.0 + has_above + has_below
    if linearized_pass:
        laplace = jnp.zeros_like(electrostatic_field)
        for adjacent_cells, interface_coefficient in neighbours:
            laplace = laplace + interface_coefficient * (adjacent_cells[0] - electrostatic_field)
        equation_mismatch = laplace + POISSON * (positive_charge_density - negative_charges + impurity_density)
        jacobian_diagonal = summed_coefficient + POISSON * (jnp.abs(negative_charges) + jnp.abs(positive_charge_density))
        refreshed_state = jnp.stack([electrostatic_field + OVERSHOOT * equation_mismatch / jacobian_diagonal, negative_charges, positive_charge_density, charge_warmth])
        warming_sheet = jnp.zeros(crystal_warmth.shape, jnp.float32)
    else:
        warming_factor = jnp.exp(-SPEED_DROP * crystal_warmth)[None]
        mobility_elec = negative_drift_speed * warming_factor
        mobility_hole = positive_drift_speed * warming_factor
        flux_elec = jnp.zeros_like(electrostatic_field)
        flux_hole = jnp.zeros_like(electrostatic_field)
        diag_elec = jnp.zeros_like(electrostatic_field)
        diag_hole = jnp.zeros_like(electrostatic_field)
        warmth_curvature = jnp.zeros_like(electrostatic_field)
        dissipated_power = jnp.zeros_like(electrostatic_field)
        for adjacent_cells, interface_coefficient in neighbours:
            drift_term = jnp.tanh(adjacent_cells[0] - electrostatic_field)
            current_elec = (adjacent_cells[1] - negative_charges) - 0.5 * (negative_charges + adjacent_cells[1]) * drift_term
            current_hole = (adjacent_cells[2] - positive_charge_density) + 0.5 * (positive_charge_density + adjacent_cells[2]) * drift_term
            flux_elec = flux_elec + interface_coefficient * current_elec
            flux_hole = flux_hole + interface_coefficient * current_hole
            diag_elec = diag_elec + interface_coefficient * (1.0 + 0.5 * drift_term)
            diag_hole = diag_hole + interface_coefficient * (1.0 - 0.5 * drift_term)
            warmth_curvature = warmth_curvature + interface_coefficient * (adjacent_cells[3] - charge_warmth)
            moving_elec = mobility_elec * current_elec
            moving_hole = mobility_hole * current_hole
            dissipated_power = dissipated_power + interface_coefficient * (moving_elec * moving_elec + moving_hole * moving_hole)
        dissipated_power = HEATING * dissipated_power
        recombine = RATE * (negative_charges * positive_charge_density - 1.0) / (negative_charges * negative_charges + positive_charge_density * positive_charge_density + 2.0)
        next_elec = negative_charges + OVERSHOOT * (mobility_elec * flux_elec - recombine) / (mobility_elec * diag_elec)
        next_hole = positive_charge_density + OVERSHOOT * (mobility_hole * flux_hole - recombine) / (mobility_hole * diag_hole)
        damping_enabled = (charge_warmth - crystal_warmth[None]) / DECAY_TIME
        upcoming_warmth = charge_warmth + OVERSHOOT * (WARMTH_DIFFUSE * warmth_curvature + dissipated_power - damping_enabled) / (WARMTH_DIFFUSE * summed_coefficient + 1.0 / DECAY_TIME)
        refreshed_state = jnp.stack([electrostatic_field, next_elec, next_hole, upcoming_warmth])
        warming_sheet = jnp.sum(dissipated_power, axis=0)
    refreshed_state = jnp.where(locked_flags[None] > 0.5, baseline_solution, refreshed_state)
    return refreshed_state, warming_sheet


def warming_pass(padded_mesh, diffusive_coefficient, specific_warmth, resistive_sheet, baseline_solution):
    layers = padded_mesh.shape[1]
    layer_index, has_above, has_below = layer_faces(layers)
    on_top = (layer_index == 0).astype(jnp.float32)
    source = HEAT_GAIN * resistive_sheet[None] * on_top
    planes = []
    for subcell in range(4):
        offset_x = subcell // 2
        offset_y = subcell % 2
        middle_cell = padded_mesh[subcell, :, 1:-1, 1:-1]
        across_x = 2 * (1 - offset_x) + offset_y
        across_y = 2 * offset_x + (1 - offset_y)
        if offset_x == 0:
            west_cell = padded_mesh[across_x, :, :-2, 1:-1]
            east_cell = padded_mesh[across_x, :, 1:-1, 1:-1]
        else:
            west_cell = padded_mesh[across_x, :, 1:-1, 1:-1]
            east_cell = padded_mesh[across_x, :, 2:, 1:-1]
        if offset_y == 0:
            south_cell = padded_mesh[across_y, :, 1:-1, :-2]
            north_cell = padded_mesh[across_y, :, 1:-1, 1:-1]
        else:
            south_cell = padded_mesh[across_y, :, 1:-1, 1:-1]
            north_cell = padded_mesh[across_y, :, 1:-1, 2:]
        above_cell = jnp.concatenate([middle_cell[:1], middle_cell[:-1]], axis=0)
        below_cell = jnp.concatenate([middle_cell[1:], jnp.zeros_like(middle_cell[:1])], axis=0)
        laplace = west_cell + east_cell + south_cell + north_cell - 4.0 * middle_cell
        laplace = laplace + has_above * (above_cell - middle_cell) + (below_cell - middle_cell)
        weights = 5.0 + has_above
        change = diffusive_coefficient * laplace + source - specific_warmth * (middle_cell - baseline_solution[subcell])
        planes.append(middle_cell + OMEGA_HEAT * change / (diffusive_coefficient * weights + specific_warmth))
    refreshed_state = jnp.stack(planes)
    return refreshed_state, 0.25 * jnp.sum(refreshed_state[:, 0], axis=0)


def margin_sheet(fields):
    return jnp.pad(fields, ((0, 0), (0, 0), (1, 1), (1, 1)))


def reference(grid_state, materials, contacts, received_sheets):
    layers = grid_state.shape[2]
    semiconductor_fields = grid_state[0]
    warming_fields = grid_state[1]
    impurity_density = lookup(materials[0], DOPING)
    negative_drift_speed = lookup(materials[0], MOB_ELEC)
    positive_drift_speed = lookup(materials[0], MOB_HOLE)
    diffusive_coefficient = lookup(materials[1], CONDUCT)
    specific_warmth = lookup(materials[1], CAPACITY)
    layer_index = jnp.arange(layers)[:, None, None]
    locked_flags = jnp.where((layer_index == 0) & (contacts[None] == 1), 1.0, 0.0).astype(jnp.float32)
    crystal_warmth = received_sheets[0]
    resistive_sheet = received_sheets[1]
    initial_guess = semiconductor_fields
    warming_sheet = jnp.zeros(crystal_warmth.shape, jnp.float32)
    warmth_sheet = jnp.zeros(crystal_warmth.shape, jnp.float32)
    for time_step in range(STEPS):
        interval_opening = warming_fields
        for newton_pass in range(NEWTON):
            for sweep_counter in range(RELAX + 1):
                semiconductor_fields, warming_sheet = semiconductor_pass(margin_sheet(semiconductor_fields), sweep_counter == 0, crystal_warmth, impurity_density, negative_drift_speed, positive_drift_speed, locked_flags, initial_guess)
                warming_fields, warmth_sheet = warming_pass(margin_sheet(warming_fields), diffusive_coefficient, specific_warmth, resistive_sheet, interval_opening)
        crystal_warmth = warmth_sheet
        resistive_sheet = warming_sheet
    return jnp.stack([semiconductor_fields, warming_fields]), jnp.stack([warming_sheet, warmth_sheet])
```

```python
import jax
import jax.numpy as jnp
from jax import lax
from jax.experimental import pallas as pl
from jax.experimental.pallas import tpu as pltpu
from jax.sharding import PartitionSpec as P

F32 = jnp.float32
LAYERS = 8
TX = 16
LANES = 128
TILES = 3
HALO = 3
ROWS = TX + 2 * HALO
FIRST = HALO

DOPING = (1.5, -1.5, 0.6, -0.6)
MOB_ELEC = (1.0, 0.35, 0.7, 0.5)
MOB_HOLE = (0.4, 0.8, 0.3, 0.6)
CONDUCT = (1.0, 0.15, 2.5, 0.5)
CAPACITY = (0.6, 1.2, 0.4, 0.9)
INV_ELEC = tuple(1.0 / m for m in MOB_ELEC)
INV_HOLE = tuple(1.0 / m for m in MOB_HOLE)
SPREAD_TOP = tuple(0.9 * k / (5.0 * k + c) for k, c in zip(CONDUCT, CAPACITY))
SPREAD_IN = tuple(0.9 * k / (6.0 * k + c) for k, c in zip(CONDUCT, CAPACITY))
KEEP_TOP = tuple(0.9 * c / (5.0 * k + c) for k, c in zip(CONDUCT, CAPACITY))
KEEP_IN = tuple(0.9 * c / (6.0 * k + c) for k, c in zip(CONDUCT, CAPACITY))
SOURCE_TOP = tuple(0.45 / (5.0 * k + c) for k, c in zip(CONDUCT, CAPACITY))

CODE, SHEET = 4, 5
WIDTH = (3, 2, 2, 2, 2, 2)
SLOT = (0, 3, 5, 7, 9, 11)
LOW = [(f, r) for f in range(6) for r in range(WIDTH[f])]
HIGH = [(f, TX - WIDTH[f] + r) for f in range(6) for r in range(WIDTH[f])]
ITEMS = len(LOW)
VMEM = pl.BlockSpec(memory_space=pltpu.VMEM)
HBM = pl.BlockSpec(memory_space=pltpu.HBM)
SHEET_SHAPE = (24, TILES * LANES)


def call(kernel, outs, ins, specs=None, out_specs=None, scratch=(), aliases=None, flops=0):
    return pl.pallas_call(
        kernel,
        out_shape=[jax.ShapeDtypeStruct(s, F32) for s in outs],
        in_specs=specs or [VMEM] * len(ins),
        out_specs=out_specs or [VMEM] * len(outs),
        scratch_shapes=list(scratch),
        input_output_aliases=aliases or {},
        compiler_params=pltpu.CompilerParams(vmem_limit_bytes=12 << 20),
        cost_estimate=pl.CostEstimate(flops=flops, bytes_accessed=1 << 20, transcendentals=0),
    )(*ins)


def lane_index():
    return lax.broadcasted_iota(jnp.int32, (LAYERS, LANES), 1)


def layer_index(width):
    return lax.broadcasted_iota(jnp.int32, (LAYERS, width), 0)


def pick(code, table):
    low = jnp.where(code < 0.5, table[0], table[1])
    high = jnp.where(code < 2.5, table[2], table[3])
    return jnp.where(code < 1.5, low, high)


def wide(ref, f, i):
    return jnp.concatenate([ref[f, i, t] for t in range(TILES)], axis=1)


def put(ref, f, i, value):
    for t in range(TILES):
        ref[f, i, t] = value[:, t * LANES : (t + 1) * LANES]


def sheet_row(ref, i, sub):
    parts = [ref[SHEET, i, t, sub : sub + 1, :] for t in range(TILES)]
    return jnp.concatenate([jnp.broadcast_to(p, (LAYERS, LANES)) for p in parts], axis=1)


def prev_lane(v):
    return pltpu.roll(v, 1, 1)


def next_lane(v):
    return pltpu.roll(v, v.shape[1] - 1, 1)


def above(v):
    return pltpu.roll(v, 1, 0)


def below(v):
    return pltpu.roll(v, LAYERS - 1, 0)


def on_device():
    return lax.axis_index("half") == 0


def pack_kernel(
    grid, codes, contacts, sheets, field_ref, low_ref, high_ref, raw, raw_code, sem
):
    copies = []
    for t in range(2):
        cols = pl.ds(t * LANES, LANES)
        copies.append(
            pltpu.make_async_copy(grid.at[0, :, :, :, cols], raw.at[t], sem.at[2 * t])
        )
        copies.append(
            pltpu.make_async_copy(codes.at[0, :, :, cols], raw_code.at[t], sem.at[2 * t + 1])
        )
    for c in copies:
        c.start()
    lanes = lane_index()
    sub = layer_index(LANES)
    raw_rows = raw.reshape(2, 4, LAYERS * TX, LANES)
    code_rows = raw_code.reshape(2, LAYERS * TX, LANES)
    for c in copies:
        c.wait()
    for x in range(TX):
        slot = 16 * (x % 8)
        if x % 8 == 0:
            low = jnp.zeros((LAYERS, LANES), F32)
            high = jnp.zeros((LAYERS, LANES), F32)
        for f in range(6):
            vals = []
            for t in range(2):
                if f < 4:
                    v = raw_rows[t, f, pl.ds(x, LAYERS, stride=TX), :]
                elif f == CODE:
                    v = code_rows[t, pl.ds(x, LAYERS, stride=TX), :].astype(F32)
                else:
                    cols = slice(t * LANES, (t + 1) * LANES)
                    con = jnp.broadcast_to(contacts[x : x + 1, cols].astype(F32), (LAYERS, LANES))
                    she = jnp.broadcast_to(sheets[0, x : x + 1, cols], (LAYERS, LANES))
                    v = jnp.where(sub < 2, con, jnp.where(sub < 4, 1.0, she))
                field_ref[f, FIRST + x, t] = v
                vals.append(v)
            w = WIDTH[f]
            at = slot + SLOT[f]
            here = (lanes >= at) & (lanes < at + w)
            low = jnp.where(here, pltpu.roll(vals[0], at, 1) if at else vals[0], low)
            high = jnp.where(here, pltpu.roll(vals[1], (at + w) % LANES, 1), high)
        if x % 8 == 7:
            low_ref[x // 8] = low
            high_ref[x // 8] = high


def y_masks(lanes):
    gy = lax.axis_index("gy")
    has_right = gy < lax.axis_size("gy") - 1
    has_left = gy > 0
    right = {w: (lanes < w) & has_right for w in (2, 3)}
    left = {w: (lanes >= LANES - w) & has_left for w in (2, 3)}
    return left, right


def side_columns(left_ref, right_ref, f, x, masks):
    w = WIDTH[f]
    at = 16 * (x % 8) + SLOT[f]
    left, right = masks
    a = pltpu.roll(right_ref[x // 8], (LANES - at) % LANES, 1)
    b = pltpu.roll(left_ref[x // 8], (2 * LANES - at - w) % LANES, 1)
    return jnp.where(right[w], a, jnp.where(left[w], b, 0.0))


def edge_kernel(field_ref, left_ref, right_ref, low_ref, high_ref):
    lanes = lane_index()
    masks = y_masks(lanes)
    for items, out in ((LOW, low_ref), (HIGH, high_ref)):
        packed = jnp.zeros((LAYERS, LANES), F32)
        for n, (f, x) in enumerate(items):
            for t in range(2):
                out[2 * n + t] = field_ref[f, FIRST + x, t]
            side = side_columns(left_ref, right_ref, f, x, masks)
            here = (lanes >= 8 * n) & (lanes < 8 * n + 8)
            packed = jnp.where(here, pltpu.roll(side, 8 * n + 3, 1), packed)
        out[2 * ITEMS] = packed


def newton_row(src, fields, dst, i):
    width = TILES * LANES
    sub = layer_index(width)
    u, e, h = wide(src, 0, i), wide(fields[1], 1, i), wide(fields[1], 2, i)
    code = wide(fields[0], CODE, i)
    total = wide(src, 0, i - 1) + wide(src, 0, i + 1) + prev_lane(u) + next_lane(u)
    total = total + jnp.where(sub > 0, above(u), 0.0) + jnp.where(sub < LAYERS - 1, below(u), 0.0)
    weight = jnp.where((sub > 0) & (sub < LAYERS - 1), 6.0, 5.0)
    r = total - weight * u + 0.7 * (h - e + pick(code, DOPING))
    diag = weight + 0.7 * (jnp.abs(e) + jnp.abs(h))
    value = u + free_cells(fields[0], i, sub) * (0.8 * r / diag)
    put(dst, 0, i, value)


def free_cells(fields, i, sub):
    contact = sheet_row(fields, i, 0)
    inside = sheet_row(fields, i, 2)
    return jnp.where(sub == 0, inside * (1.0 - contact), inside)


def face(p, n):
    g = 0.5 * jnp.tanh(n[0] - p[0])
    a = (n[1] - p[1]) - (n[1] + p[1]) * g
    c = (n[2] - p[2]) + (n[2] + p[2]) * g
    return a, c, g


def x_face(uref, fref, i):
    p = (wide(uref, 0, i), wide(fref, 1, i), wide(fref, 2, i))
    n = (wide(uref, 0, i + 1), wide(fref, 1, i + 1), wide(fref, 2, i + 1))
    return face(p, n)


def relax_row(uref, fref, fields, i, before):
    width = TILES * LANES
    sub = layer_index(width)
    here = (wide(uref, 0, i), wide(fref, 1, i), wide(fref, 2, i))
    u, e, h = here
    k = wide(fref, 3, i)
    after = face(here, (wide(uref, 0, i + 1), wide(fref, 1, i + 1), wide(fref, 2, i + 1)))
    y_after = face(here, tuple(next_lane(v) for v in here))
    y_before = tuple(prev_lane(v) for v in y_after)
    l_after = face(here, tuple(below(v) for v in here))
    l_after = tuple(jnp.where(sub < LAYERS - 1, v, 0.0) for v in l_after)
    l_before = tuple(above(v) for v in l_after)
    net = [
        (after[n] - before[n]) + (y_after[n] - y_before[n]) + (l_after[n] - l_before[n])
        for n in range(3)
    ]
    square = [
        (after[n] * after[n] + before[n] * before[n])
        + (y_after[n] * y_after[n] + y_before[n] * y_before[n])
        + (l_after[n] * l_after[n] + l_before[n] * l_before[n])
        for n in range(2)
    ]
    weight = jnp.where((sub > 0) & (sub < LAYERS - 1), 6.0, 5.0)
    spread = wide(fref, 3, i - 1) + wide(fref, 3, i + 1) + prev_lane(k) + next_lane(k)
    spread = spread + jnp.where(sub > 0, above(k), 0.0)
    spread = spread + jnp.where(sub < LAYERS - 1, below(k), 0.0) - weight * k
    code = wide(fields, CODE, i)
    mob_e, mob_h = pick(code, MOB_ELEC), pick(code, MOB_HOLE)
    power = 0.05 * (mob_e * mob_e * square[0] + mob_h * mob_h * square[1])
    recombine = 0.3 * (e * h - 1.0) / (e * e + h * h + 2.0)
    step = 0.8 * free_cells(fields, i, sub)
    scale_e = step / (weight + net[2])
    scale_h = step / (weight - net[2])
    fixed = (
        e + scale_e * net[0],
        h + scale_h * net[1],
        k + step * (0.5 * spread - 0.5 * k) / (0.5 * weight + 0.5),
    )
    varying = (
        scale_e * recombine * pick(code, INV_ELEC),
        scale_h * recombine * pick(code, INV_HOLE),
        power,
    )
    return after, fixed, varying, step / (0.5 * weight + 0.5)


def relax_first(uref, fref, fields, dst, sheet_ref, i, before):
    after, fixed, varying, heat_step = relax_row(uref, fref, fields, i, before)
    s = sheet_row(fields, i, 4)
    slow = jnp.exp(-0.3 * s)
    fast = jnp.exp(0.3 * s)
    q = varying[2] * (slow * slow)
    put(dst, 1, i, fixed[0] - varying[0] * fast)
    put(dst, 2, i, fixed[1] - varying[1] * fast)
    put(dst, 3, i, fixed[2] + heat_step * (q + 0.5 * s))
    sheet_ref[pl.ds(i - 2, 1), :] = jnp.sum(q, axis=0, keepdims=True)
    return after


def thermal_row(
    src, anchor, fields, dst, i, halves=(0, 1), source=True, first=False, put_row=put
):
    width = TILES * LANES
    sub = layer_index(width)
    top = sub == 0
    cells = [wide(src, f, i) for f in range(4)]
    code = wide(fields, CODE, i)
    inside = sheet_row(fields, i, 2)
    spread = jnp.where(top, pick(code, SPREAD_TOP), pick(code, SPREAD_IN)) * inside
    held = jnp.where(top, pick(code, KEEP_TOP), pick(code, KEEP_IN)) * inside
    if source:
        heat = jnp.where(top, pick(code, SOURCE_TOP) * sheet_row(fields, i, 4), 0.0) * inside
    out = []
    for s in halves:
        for t in range(2):
            f = 2 * s + t
            v = cells[f]
            if s == 0:
                total = wide(src, 2 + t, i - 1) + cells[2 + t]
            else:
                total = cells[t] + wide(src, t, i + 1)
            other = cells[2 * s + 1 - t]
            total = total + other + (prev_lane(other) if t == 0 else next_lane(other))
            total = total + jnp.where(sub > 0, above(v), 0.0)
            total = total + jnp.where(sub < LAYERS - 1, below(v), 0.0)
            value = spread * total + 0.1 * v
            value = value + held * (v if first else wide(anchor, f, i))
            if source:
                value = value + heat
            out.append(value)
            put_row(dst, f, i, value)
    return out


def top_mean(cells):
    total = (cells[0] + cells[1]) + (cells[2] + cells[3])
    return 0.25 * total[0:1, :]


def inner_kernel(field_in, left_ref, right_ref, field_ref, next_ref, mid_ref, sheet_ref):
    lanes = lane_index()
    masks = y_masks(lanes)
    for x in range(TX):
        for f in range(6):
            field_ref[f, FIRST + x, 2] = side_columns(left_ref, right_ref, f, x, masks)

    @pl.when(on_device())
    def _():
        def newton(i, carry):
            newton_row(field_ref, (field_ref, field_ref), next_ref, i)
            return carry

        lax.fori_loop(FIRST + 1, FIRST + TX - 1, newton, 0)

        def relax(i, carry):
            return relax_first(next_ref, field_ref, field_ref, next_ref, sheet_ref, i, carry)

        lax.fori_loop(
            FIRST + 2, FIRST + TX - 2, relax, x_face(next_ref, field_ref, FIRST + 1)
        )

    @pl.when(jnp.logical_not(on_device()))
    def _():
        def one(i, carry):
            thermal_row(field_ref, field_ref, field_ref, mid_ref, i, first=True)
            return carry

        lax.fori_loop(FIRST + 1, FIRST + TX - 1, one, 0)

        def two(i, carry):
            cells = thermal_row(mid_ref, field_ref, field_ref, next_ref, i)
            sheet_ref[pl.ds(i - FIRST, 1), :] = top_mean(cells)
            return carry

        lax.fori_loop(FIRST + 2, FIRST + TX - 2, two, 0)


def rim_kernel(
    field_in, next_in, mid_in, sheet_in, up_ref, down_ref, field_ref, next_ref, mid_ref, sheet_ref
):
    lanes = lane_index()
    gx = lax.axis_index("gx")
    has_up = gx > 0
    has_down = gx < lax.axis_size("gx") - 1
    edge = {w: (lanes < w) | (lanes >= LANES - w) for w in (2, 3)}
    for items, src, ok, base in (
        (HIGH, up_ref, has_up, FIRST - TX),
        (LOW, down_ref, has_down, FIRST + TX),
    ):
        packed = src[2 * ITEMS]
        for n, (f, x) in enumerate(items):
            for t in range(2):
                field_ref[f, base + x, t] = jnp.where(ok, src[2 * n + t], 0.0)
            side = pltpu.roll(packed, LANES - 8 * n - 3, 1)
            field_ref[f, base + x, 2] = jnp.where(edge[WIDTH[f]] & ok, side, 0.0)

    @pl.when(on_device())
    def _():
        def newton(n, carry):
            newton_row(field_ref, (field_ref, field_ref), next_ref, FIRST - 2 + n)
            newton_row(field_ref, (field_ref, field_ref), next_ref, FIRST + TX - 1 + n)
            return carry

        lax.fori_loop(0, 3, newton, 0)

        def relax(n, carry):
            args = (next_ref, field_ref, field_ref, next_ref, sheet_ref)
            one = relax_first(*args, FIRST - 1 + n, carry[0])
            two = relax_first(*args, FIRST + TX - 2 + n, carry[1])
            return one, two

        start = (
            x_face(next_ref, field_ref, FIRST - 2),
            x_face(next_ref, field_ref, FIRST + TX - 3),
        )
        lax.fori_loop(0, 3, relax, start)

    @pl.when(jnp.logical_not(on_device()))
    def _():
        args = (field_ref, field_ref, field_ref, mid_ref)
        thermal_row(*args, FIRST - 2, halves=(1,), first=True)
        thermal_row(*args, FIRST + TX + 1, halves=(0,), first=True)
        for i in (FIRST - 1, FIRST, FIRST + TX - 1, FIRST + TX):
            thermal_row(*args, i, first=True)
        for n in range(3):
            for i in (FIRST - 1 + n, FIRST + TX - 2 + n):
                cells = thermal_row(mid_ref, field_ref, field_ref, next_ref, i)
                if FIRST <= i < FIRST + TX:
                    sheet_ref[pl.ds(i - FIRST, 1), :] = top_mean(cells)


def second_kernel(field_ref, next_ref, fixed_ref, varying_ref, source_ref, spread_ref, mid_ref):
    fixed_rows = fixed_ref.reshape(2, 4, LAYERS * TX, LANES)
    varying_rows = varying_ref.reshape(2, 3, LAYERS * TX, LANES)

    def native(ref, f, i, value):
        for t in range(2):
            rows = pl.ds(i - FIRST, LAYERS, stride=TX)
            ref[t, f, rows, :] = value[:, t * LANES : (t + 1) * LANES]

    @pl.when(on_device())
    def _():
        def newton(i, carry):
            newton_row(next_ref, (field_ref, next_ref), mid_ref, i)
            return carry

        lax.fori_loop(FIRST - 1, FIRST + TX + 1, newton, 0)

        def relax(i, before):
            after, fixed, varying, _ = relax_row(mid_ref, next_ref, field_ref, i, before)
            native(fixed_rows, 0, i, wide(mid_ref, 0, i))
            for n in range(3):
                native(fixed_rows, n + 1, i, fixed[n])
                native(varying_rows, n, i, varying[n])
            return after

        lax.fori_loop(FIRST, FIRST + TX, relax, x_face(mid_ref, next_ref, FIRST - 1))

    @pl.when(jnp.logical_not(on_device()))
    def _():
        args = (next_ref, next_ref, field_ref, mid_ref)
        thermal_row(*args, FIRST - 1, halves=(1,), source=False, first=True)
        thermal_row(*args, FIRST + TX, halves=(0,), source=False, first=True)

        def three(i, carry):
            thermal_row(*args, i, source=False, first=True)
            return carry

        lax.fori_loop(FIRST, FIRST + TX, three, 0)

        def four(i, carry):
            def keep(ref, f, i, value):
                native(fixed_rows, f, i, value)

            thermal_row(mid_ref, next_ref, field_ref, None, i, source=False, put_row=keep)
            return carry

        lax.fori_loop(FIRST, FIRST + TX, four, 0)

        def top(i, carry):
            code = jnp.concatenate([field_ref[CODE, i, t] for t in range(TILES)], axis=1)
            inside = jnp.concatenate(
                [field_ref[SHEET, i, t, 2:3, :] for t in range(TILES)], axis=1
            )
            source_ref[pl.ds(i - FIRST + 1, 1), :] = pick(code[0:1, :], SOURCE_TOP) * inside
            return carry

        lax.fori_loop(FIRST - 1, FIRST + TX + 1, top, 0)

        def sides(i, carry):
            code = jnp.concatenate([field_ref[CODE, i, t] for t in range(2)], axis=1)
            spread_ref[0, pl.ds(i - FIRST, 1), :] = pick(code[0:1, :], SPREAD_TOP)
            spread_ref[1, pl.ds(i - FIRST, 1), :] = pick(code[1:2, :], SPREAD_IN)
            return carry

        lax.fori_loop(FIRST, FIRST + TX, sides, 0)


def last_kernel(
    sheet_ref, fixed_ref, varying_ref, source_ref, spread_ref, contacts,
    state_out, sheet_out, done, delta, sem,
):
    def send(src, f, t, layers):
        dst = state_out.at[0, f, layers, :, pl.ds(t * LANES, LANES)]
        return pltpu.make_async_copy(src.at[t, f, layers], dst, sem.at[f, t])

    @pl.when(on_device())
    def _():
        every = pl.ds(0, LAYERS)
        copies = [send(fixed_ref, 0, t, every) for t in range(2)]
        for c in copies:
            c.start()
        for t in range(2):
            cols = slice(t * LANES, (t + 1) * LANES)
            s = sheet_ref[0:TX, cols]
            slow = jnp.exp(-0.3 * s)
            slow = slow * slow
            fast = jnp.exp(0.3 * s)
            total = jnp.zeros((TX, LANES), F32)
            for layer in range(LAYERS):
                for f in (1, 2):
                    done[t, f, layer] = (
                        fixed_ref[t, f, layer] - varying_ref[t, f - 1, layer] * fast
                    )
                q = varying_ref[t, 2, layer] * slow
                total = total + q
                step = 0.8 / 3.5 if 0 < layer < LAYERS - 1 else 0.8 / 3.0
                if layer == 0:
                    step = step * (1.0 - contacts[:, cols].astype(F32))
                done[t, 3, layer] = fixed_ref[t, 3, layer] + step * (q + 0.5 * s)
            sheet_out[0, :, cols] = total
            for f in (1, 2, 3):
                copies.append(send(done, f, t, every))
                copies[-1].start()
        for c in copies:
            c.wait()

    @pl.when(jnp.logical_not(on_device()))
    def _():
        rest = pl.ds(2, LAYERS - 2)
        copies = [send(fixed_ref, f, t, rest) for t in range(2) for f in range(4)]
        for c in copies:
            c.start()
        delta[...] = source_ref[...] * sheet_ref[...]
        middle = delta[1 : TX + 1, :]
        by_x = (delta[0:TX, :], delta[2 : TX + 2, :])
        by_y = (prev_lane(middle), next_lane(middle))
        more = []
        for t in range(2):
            cols = slice(t * LANES, (t + 1) * LANES)
            mid = middle[:, cols]
            total = jnp.zeros((TX, LANES), F32)
            for f in range(4):
                around = 2.0 * mid + by_x[f // 2][:, cols] + by_y[f % 2][:, cols]
                value = fixed_ref[t, f, 0] + 1.1 * mid + spread_ref[0, :, cols] * around
                done[t, f, 0] = value
                total = total + value
                done[t, f, 1] = fixed_ref[t, f, 1] + spread_ref[1, :, cols] * mid
                dst = state_out.at[0, f, pl.ds(0, 2), :, pl.ds(t * LANES, LANES)]
                more.append(
                    pltpu.make_async_copy(done.at[t, f, pl.ds(0, 2)], dst, sem.at[4 + f, t])
                )
                more[-1].start()
            sheet_out[0, :, cols] = 0.25 * total
        for c in copies + more:
            c.wait()


def per_device(grid_state, materials, contacts, received_sheets):
    nx, ny = lax.axis_size("gx"), lax.axis_size("gy")

    def shift(block, axis, count, by):
        return lax.ppermute(block, axis, [(i, (i + by) % count) for i in range(count)])

    tile = (LAYERS, LANES)
    field_shape = (6, ROWS, TILES) + tile
    state_shape = (4, ROWS, TILES) + tile
    fields, y_low, y_high = call(
        pack_kernel,
        [field_shape, (2,) + tile, (2,) + tile],
        [grid_state, materials, contacts, received_sheets],
        specs=[HBM, HBM, VMEM, VMEM],
        scratch=[
            pltpu.VMEM((2, 4, LAYERS, TX, LANES), F32),
            pltpu.VMEM((2, LAYERS, TX, LANES), jnp.int32),
            pltpu.SemaphoreType.DMA((4,)),
        ],
    )
    left = shift(y_high, "gy", ny, 1)
    right = shift(y_low, "gy", ny, -1)
    edge_shape = (2 * ITEMS + 1,) + tile
    x_low, x_high = call(edge_kernel, [edge_shape, edge_shape], [fields, left, right])
    up = shift(x_high, "gx", nx, 1)
    down = shift(x_low, "gx", nx, -1)
    fields, following, middle, sheet = call(
        inner_kernel,
        [field_shape, state_shape, state_shape, SHEET_SHAPE],
        [fields, left, right],
        aliases={0: 0},
        flops=1 << 22,
    )
    fields, following, middle, sheet = call(
        rim_kernel,
        [field_shape, state_shape, state_shape, SHEET_SHAPE],
        [fields, following, middle, sheet, up, down],
        aliases={0: 0, 1: 1, 2: 2, 3: 3},
    )
    swapped = lax.ppermute(sheet, "half", [(0, 1), (1, 0)])
    fixed, varying, source, spread = call(
        second_kernel,
        [
            (2, 4, LAYERS, TX, LANES),
            (2, 3, LAYERS, TX, LANES),
            SHEET_SHAPE,
            (2, TX, 2 * LANES),
        ],
        [fields, following],
        scratch=[pltpu.VMEM(state_shape, F32)],
        flops=1 << 22,
    )
    state, outgoing = call(
        last_kernel,
        [(1, 4, LAYERS, TX, 2 * LANES), (1, TX, 2 * LANES)],
        [swapped, fixed, varying, source, spread, contacts],
        out_specs=[HBM, VMEM],
        scratch=[
            pltpu.VMEM((2, 4, LAYERS, TX, LANES), F32),
            pltpu.VMEM(SHEET_SHAPE, F32),
            pltpu.SemaphoreType.DMA((8, 2)),
        ],
    )
    return state, outgoing


def solution(mesh):
    placed = (
        P("half", None, None, "gx", "gy"),
        P("half", None, "gx", "gy"),
        P("gx", "gy"),
        P("half", "gx", "gy"),
    )
    return jax.shard_map(
        per_device,
        mesh=mesh,
        in_specs=placed,
        out_specs=(P("half", None, None, "gx", "gy"), P("half", "gx", "gy")),
        check_vma=False,
    )
```

```python
import jax
import jax.numpy as jnp
from jax import lax
from jax.experimental import pallas as pl
from jax.experimental.pallas import tpu as pltpu
from jax.sharding import PartitionSpec as P

F32 = jnp.float32
LAYERS = 8
TX = 16
LANES = 128
TILES = 3
HALO = 3
ROWS = TX + 2 * HALO
FIRST = HALO

DOPING = (1.5, -1.5, 0.6, -0.6)
MOB_ELEC = (1.0, 0.35, 0.7, 0.5)
MOB_HOLE = (0.4, 0.8, 0.3, 0.6)
CONDUCT = (1.0, 0.15, 2.5, 0.5)
CAPACITY = (0.6, 1.2, 0.4, 0.9)
POWER_ELEC = tuple(0.05 * m * m for m in MOB_ELEC)
POWER_HOLE = tuple(0.05 * m * m for m in MOB_HOLE)
LOSS_ELEC = tuple(0.3 / m for m in MOB_ELEC)
LOSS_HOLE = tuple(0.3 / m for m in MOB_HOLE)
SPREAD_TOP = tuple(0.9 * k / (5.0 * k + c) for k, c in zip(CONDUCT, CAPACITY))
SPREAD_IN = tuple(0.9 * k / (6.0 * k + c) for k, c in zip(CONDUCT, CAPACITY))
SOURCE_TOP = tuple(0.45 / (5.0 * k + c) for k, c in zip(CONDUCT, CAPACITY))

CODE, FREE, SHEET = 4, 5, 6
FIELDS = 7
WIDTH = (3, 2, 2, 2, 2, 2, 2)
SLOT = (0, 3, 5, 7, 9, 11, 13)
LOW = [(f, r) for f in range(FIELDS) for r in range(WIDTH[f])]
HIGH = [(f, TX - WIDTH[f] + r) for f in range(FIELDS) for r in range(WIDTH[f])]
BULK = sum(1 for f, _ in LOW if f < FREE)
SIDE = 2 * BULK + 2
VMEM = pl.BlockSpec(memory_space=pltpu.VMEM)
HBM = pl.BlockSpec(memory_space=pltpu.HBM)
SHEET_SHAPE = (24, TILES * LANES)
INNER = 1 << 23
UNROLL_NEWTON, UNROLL_RELAX, UNROLL_HEAT = 2, 4, 2


def call(kernel, outs, ins, specs=None, out_specs=None, scratch=(), aliases=None, cost=1 << 20):
    return pl.pallas_call(
        kernel,
        out_shape=[
            jax.ShapeDtypeStruct(*(s if isinstance(s[0], tuple) else (s, F32))) for s in outs
        ],
        in_specs=specs or [VMEM] * len(ins),
        out_specs=out_specs or [VMEM] * len(outs),
        scratch_shapes=list(scratch),
        input_output_aliases=aliases or {},
        compiler_params=pltpu.CompilerParams(vmem_limit_bytes=12 << 20),
        cost_estimate=pl.CostEstimate(flops=0, bytes_accessed=cost, transcendentals=0),
    )(*ins)


def lane_index():
    return lax.broadcasted_iota(jnp.int32, (LAYERS, LANES), 1)


def layer_index(width):
    return lax.broadcasted_iota(jnp.int32, (LAYERS, width), 0)


def pick(code, table):
    low = jnp.where(code < 0.5, table[0], table[1])
    high = jnp.where(code < 2.5, table[2], table[3])
    return jnp.where(code < 1.5, low, high)


def wide(ref, f, i):
    return jnp.concatenate([ref[f, i, t] for t in range(TILES)], axis=1)


def put(ref, f, i, value):
    for t in range(TILES):
        ref[f, i, t] = value[:, t * LANES : (t + 1) * LANES]


def cut(v, tiles):
    return v if v.shape[1] == tiles * LANES else v[:, : tiles * LANES]


def recip(v):
    r = pl.reciprocal(v, approx=True)
    return r * (2.0 - v * r)


def prev_lane(v):
    return pltpu.roll(v, 1, 1)


def next_lane(v):
    return pltpu.roll(v, v.shape[1] - 1, 1)


def above(v):
    return pltpu.roll(v, 1, 0)


def below(v):
    return pltpu.roll(v, LAYERS - 1, 0)


def on_device():
    return lax.axis_index("half") == 0


def own_row(raw_rows, code_rows, contact_ref, sheet_ref, device, sub, f, x, t):
    cols = slice(t * LANES, (t + 1) * LANES)
    if f < 4:
        return raw_rows[t, f, pl.ds(x, LAYERS, stride=TX), :]
    if f == CODE:
        return code_rows[t, pl.ds(x, LAYERS, stride=TX), :].astype(F32)
    if f == FREE:
        held = jnp.broadcast_to(contact_ref[x : x + 1, cols], (LAYERS, LANES))
        return jnp.where((held == 1) & (sub == 0) & device, 0.0, 1.0)
    return jnp.broadcast_to(sheet_ref[0, x : x + 1, cols], (LAYERS, LANES))


def pack_kernel(
    grid, codes, contacts, sheets, raw, raw_code, raw_contact, raw_sheet, left_ref, right_ref, sem
):
    copies = [
        pltpu.make_async_copy(contacts, raw_contact, sem.at[4]),
        pltpu.make_async_copy(sheets, raw_sheet, sem.at[5]),
    ]
    for t in range(2):
        cols = pl.ds(t * LANES, LANES)
        copies.append(
            pltpu.make_async_copy(grid.at[0, :, :, :, cols], raw.at[t], sem.at[2 * t])
        )
        copies.append(
            pltpu.make_async_copy(codes.at[0, :, :, cols], raw_code.at[t], sem.at[2 * t + 1])
        )
    for c in copies:
        c.start()
    lanes = lane_index()
    raw_rows = raw.reshape(2, 4, LAYERS * TX, LANES)
    code_rows = raw_code.reshape(2, LAYERS * TX, LANES)
    args = (raw_rows, code_rows, raw_contact, raw_sheet, on_device(), layer_index(LANES))
    for c in copies:
        c.wait()
    for block in range(2):
        left = jnp.zeros((LAYERS, LANES), F32)
        right = jnp.zeros((LAYERS, LANES), F32)
        for row in range(8):
            for f in range(FIELDS):
                w = WIDTH[f]
                at = 16 * row + SLOT[f]
                here = (lanes >= at) & (lanes < at + w)
                low = own_row(*args, f, 8 * block + row, 0)
                high = own_row(*args, f, 8 * block + row, 1)
                left = jnp.where(here, pltpu.roll(low, at, 1) if at else low, left)
                right = jnp.where(here, pltpu.roll(high, (at + w) % LANES, 1), right)
        left_ref[block] = left
        right_ref[block] = right


def rows_kernel(raw, raw_code, raw_contact, raw_sheet, field_ref, low_ref, high_ref):
    sub = layer_index(LANES)
    raw_rows = raw.reshape(2, 4, LAYERS * TX, LANES)
    code_rows = raw_code.reshape(2, LAYERS * TX, LANES)
    args = (raw_rows, code_rows, raw_contact, raw_sheet, on_device(), sub)
    for f in range(FIELDS):
        for x in range(TX):
            for t in range(2):
                v = own_row(*args, f, x, t)
                field_ref[f, FIRST + x, t] = v
                for items, out in ((LOW, low_ref), (HIGH, high_ref)):
                    if f < FREE and (f, x) in items:
                        out[2 * items.index((f, x)) + t] = v
    for out, x in ((low_ref, 0), (high_ref, TX - 2)):
        for t in range(2):
            free = [field_ref[FREE, FIRST + x + n, t] for n in range(2)]
            sheet = [field_ref[SHEET, FIRST + x + n, t] for n in range(2)]
            v = jnp.where(sub == 0, free[0], pltpu.roll(free[1], 1, 0))
            v = jnp.where(sub < 2, v, 1.0)
            v = jnp.where(sub < 4, v, jnp.where(sub < 6, sheet[0], sheet[1]))
            out[2 * BULK + t] = v


def y_masks(lanes):
    gy = lax.axis_index("gy")
    has_right = gy < lax.axis_size("gy") - 1
    has_left = gy > 0
    right = {w: (lanes < w) & has_right for w in (2, 3)}
    left = {w: (lanes >= LANES - w) & has_left for w in (2, 3)}
    return left, right


def side_columns(left_ref, right_ref, f, x, masks):
    w = WIDTH[f]
    at = 16 * (x % 8) + SLOT[f]
    left, right = masks
    a = pltpu.roll(right_ref[x // 8], (LANES - at) % LANES, 1)
    b = pltpu.roll(left_ref[x // 8], (2 * LANES - at - w) % LANES, 1)
    return jnp.where(right[w], a, jnp.where(left[w], b, 0.0))


def corner_kernel(low_in, high_in, left_ref, right_ref, low_ref, high_ref):
    lanes = lane_index()
    masks = y_masks(lanes)
    for items, out in ((LOW, low_ref), (HIGH, high_ref)):
        packed = jnp.zeros((LAYERS, LANES), F32)
        for n, (f, x) in enumerate(items):
            side = side_columns(left_ref, right_ref, f, x, masks)
            here = (lanes >= 8 * n) & (lanes < 8 * n + 8)
            packed = jnp.where(here, pltpu.roll(side, 8 * n + 3, 1), packed)
        out[SIDE] = packed


def newton_row(uref, fref, fields, dst, i):
    width = TILES * LANES
    sub = layer_index(width)
    u, e, h = wide(uref, 0, i), wide(fref, 1, i), wide(fref, 2, i)
    code = wide(fields, CODE, i)
    total = wide(uref, 0, i - 1) + wide(uref, 0, i + 1) + prev_lane(u) + next_lane(u)
    total = total + jnp.where(sub > 0, above(u), 0.0) + jnp.where(sub < LAYERS - 1, below(u), 0.0)
    weight = jnp.where((sub > 0) & (sub < LAYERS - 1), 6.0, 5.0)
    r = total - weight * u + 0.7 * (h - e + pick(code, DOPING))
    diag = weight + 0.7 * (jnp.abs(e) + jnp.abs(h))
    put(dst, 0, i, u + (0.8 * wide(fields, FREE, i)) * (r * recip(diag)))


def face(p, n):
    g = 0.5 * jnp.tanh(n[0] - p[0])
    a = (n[1] - p[1]) - (n[1] + p[1]) * g
    c = (n[2] - p[2]) + (n[2] + p[2]) * g
    return a, c, g


def x_face(uref, fref, i, tiles=TILES):
    p = (wide(uref, 0, i), wide(fref, 1, i), wide(fref, 2, i))
    n = (wide(uref, 0, i + 1), wide(fref, 1, i + 1), wide(fref, 2, i + 1))
    return face([cut(v, tiles) for v in p], [cut(v, tiles) for v in n])


def relax_row(uref, fref, fields, i, before, tiles=TILES):
    sub = layer_index(tiles * LANES)
    here = (wide(uref, 0, i), wide(fref, 1, i), wide(fref, 2, i))
    k = wide(fref, 3, i)
    after = (wide(uref, 0, i + 1), wide(fref, 1, i + 1), wide(fref, 2, i + 1))
    y_after = face(here, tuple(next_lane(v) for v in here))
    y_before = tuple(cut(prev_lane(v), tiles) for v in y_after)
    y_after = tuple(cut(v, tiles) for v in y_after)
    spread = cut(prev_lane(k), tiles) + cut(next_lane(k), tiles)
    here = tuple(cut(v, tiles) for v in here)
    k = cut(k, tiles)
    u, e, h = here
    after = face(here, tuple(cut(v, tiles) for v in after))
    l_after = face(here, tuple(below(v) for v in here))
    l_after = tuple(jnp.where(sub < LAYERS - 1, v, 0.0) for v in l_after)
    l_before = tuple(above(v) for v in l_after)
    net = [
        (after[n] - before[n]) + (y_after[n] - y_before[n]) + (l_after[n] - l_before[n])
        for n in range(3)
    ]
    square = [
        (after[n] * after[n] + before[n] * before[n])
        + (y_after[n] * y_after[n] + y_before[n] * y_before[n])
        + (l_after[n] * l_after[n] + l_before[n] * l_before[n])
        for n in range(2)
    ]
    inner = (sub > 0) & (sub < LAYERS - 1)
    weight = jnp.where(inner, 6.0, 5.0)
    spread = spread + cut(wide(fref, 3, i - 1), tiles) + cut(wide(fref, 3, i + 1), tiles)
    spread = spread + jnp.where(sub > 0, above(k), 0.0)
    spread = spread + jnp.where(sub < LAYERS - 1, below(k), 0.0) - weight * k
    code = cut(wide(fields, CODE, i), tiles)
    free = cut(wide(fields, FREE, i), tiles)
    power = pick(code, POWER_ELEC) * square[0] + pick(code, POWER_HOLE) * square[1]
    recombine = (e * h - 1.0) * recip(e * e + h * h + 2.0)
    step = 0.8 * free
    scale_e = step * recip(weight + net[2])
    scale_h = step * recip(weight - net[2])
    heat_step = free * jnp.where(inner, 0.8 / 3.5, 0.8 / 3.0)
    fixed = (
        e + scale_e * net[0],
        h + scale_h * net[1],
        k + heat_step * (0.5 * spread - 0.5 * k),
    )
    varying = (
        scale_e * recombine * pick(code, LOSS_ELEC),
        scale_h * recombine * pick(code, LOSS_HOLE),
        power,
    )
    return after, fixed, varying, heat_step


def relax_first(uref, fref, fields, dst, sheet_ref, i, before):
    after, fixed, varying, heat_step = relax_row(uref, fref, fields, i, before)
    s = wide(fields, SHEET, i)
    slow = jnp.exp(-0.6 * s)
    fast = jnp.exp(0.3 * s)
    q = varying[2] * slow
    put(dst, 1, i, fixed[0] - varying[0] * fast)
    put(dst, 2, i, fixed[1] - varying[1] * fast)
    put(dst, 3, i, fixed[2] + heat_step * (q + 0.5 * s))
    sheet_ref[pl.ds(i - 2, 1), :] = jnp.sum(q, axis=0, keepdims=True)
    return after


def thermal_row(
    src, anchor, fields, dst, i, halves=(0, 1), source=True, first=False, put_row=put
):
    width = TILES * LANES
    sub = layer_index(width)
    top = sub == 0
    cells = [wide(src, f, i) for f in range(4)]
    code = wide(fields, CODE, i)
    spread = jnp.where(top, pick(code, SPREAD_TOP), pick(code, SPREAD_IN))
    held = 0.9 - jnp.where(top, 5.0, 6.0) * spread
    spread = spread * wide(fields, FREE, i)
    if source:
        heat = jnp.where(top, pick(code, SOURCE_TOP) * wide(fields, SHEET, i), 0.0)
    out = []
    for s in halves:
        for t in range(2):
            f = 2 * s + t
            v = cells[f]
            if s == 0:
                total = wide(src, 2 + t, i - 1) + cells[2 + t]
            else:
                total = cells[t] + wide(src, t, i + 1)
            other = cells[2 * s + 1 - t]
            total = total + other + (prev_lane(other) if t == 0 else next_lane(other))
            total = total + jnp.where(sub > 0, above(v), 0.0)
            total = total + jnp.where(sub < LAYERS - 1, below(v), 0.0)
            value = spread * total + 0.1 * v
            value = value + held * (v if first else wide(anchor, f, i))
            if source:
                value = value + heat
            out.append(value)
            put_row(dst, f, i, value)
    return out


def top_mean(cells):
    total = (cells[0] + cells[1]) + (cells[2] + cells[3])
    return 0.25 * total[0:1, :]


def inner_kernel(field_in, left_ref, right_ref, field_ref, next_ref, mid_ref, sheet_ref):
    lanes = lane_index()
    masks = y_masks(lanes)
    for x in range(TX):
        for f in range(FIELDS):
            field_ref[f, FIRST + x, 2] = side_columns(left_ref, right_ref, f, x, masks)

    @pl.when(on_device())
    def _():
        def newton(i, carry):
            newton_row(field_ref, field_ref, field_ref, mid_ref, i)
            return carry

        lax.fori_loop(FIRST + 1, FIRST + TX - 1, newton, 0, unroll=UNROLL_NEWTON)

        def relax(i, carry):
            return relax_first(mid_ref, field_ref, field_ref, next_ref, sheet_ref, i, carry)

        start = x_face(mid_ref, field_ref, FIRST + 1)
        lax.fori_loop(FIRST + 2, FIRST + TX - 2, relax, start, unroll=UNROLL_RELAX)

    @pl.when(jnp.logical_not(on_device()))
    def _():
        def one(i, carry):
            thermal_row(field_ref, field_ref, field_ref, mid_ref, i, first=True)
            return carry

        lax.fori_loop(FIRST + 1, FIRST + TX - 1, one, 0, unroll=UNROLL_HEAT)

        def two(i, carry):
            cells = thermal_row(mid_ref, field_ref, field_ref, next_ref, i)
            sheet_ref[pl.ds(i - FIRST, 1), :] = top_mean(cells)
            return carry

        lax.fori_loop(FIRST + 2, FIRST + TX - 2, two, 0, unroll=UNROLL_HEAT)


def rim_kernel(
    field_in, next_in, mid_in, sheet_in, up_ref, down_ref,
    field_ref, next_ref, mid_ref, sheet_ref,
):
    lanes = lane_index()
    sub = layer_index(LANES)
    gx = lax.axis_index("gx")
    has_up = gx > 0
    has_down = gx < lax.axis_size("gx") - 1
    edge = {w: (lanes < w) | (lanes >= LANES - w) for w in (2, 3)}
    for items, src, ok, base in (
        (HIGH, up_ref, has_up, FIRST - TX),
        (LOW, down_ref, has_down, FIRST + TX),
    ):
        packed = src[SIDE]
        for n, (f, x) in enumerate(items):
            for t in range(2):
                second = x % 2
                if f < FREE:
                    v = src[2 * n + t]
                elif f == FREE:
                    at = 2 * BULK + t
                    top = jnp.broadcast_to(src[at, second : second + 1, :], (LAYERS, LANES))
                    v = jnp.where(sub == 0, top, 1.0)
                else:
                    row = slice(4 + 2 * second, 5 + 2 * second)
                    v = jnp.broadcast_to(src[2 * BULK + t, row, :], (LAYERS, LANES))
                field_ref[f, base + x, t] = jnp.where(ok, v, 0.0)
            side = pltpu.roll(packed, LANES - 8 * n - 3, 1)
            field_ref[f, base + x, 2] = jnp.where(edge[WIDTH[f]] & ok, side, 0.0)

    @pl.when(on_device())
    def _():
        for n in range(3):
            for i in (FIRST - 2 + n, FIRST + TX - 1 + n):
                newton_row(field_ref, field_ref, field_ref, mid_ref, i)
        args = (mid_ref, field_ref, field_ref, next_ref, sheet_ref)
        one = x_face(mid_ref, field_ref, FIRST - 2)
        two = x_face(mid_ref, field_ref, FIRST + TX - 3)
        for n in range(3):
            one = relax_first(*args, FIRST - 1 + n, one)
            two = relax_first(*args, FIRST + TX - 2 + n, two)

    @pl.when(jnp.logical_not(on_device()))
    def _():
        args = (field_ref, field_ref, field_ref, mid_ref)
        thermal_row(*args, FIRST - 2, halves=(1,), first=True)
        thermal_row(*args, FIRST + TX + 1, halves=(0,), first=True)
        for i in (FIRST - 1, FIRST, FIRST + TX - 1, FIRST + TX):
            thermal_row(*args, i, first=True)
        for n in range(3):
            for i in (FIRST - 1 + n, FIRST + TX - 2 + n):
                cells = thermal_row(mid_ref, field_ref, field_ref, next_ref, i)
                if FIRST <= i < FIRST + TX:
                    sheet_ref[pl.ds(i - FIRST, 1), :] = top_mean(cells)


def second_kernel(
    field_ref, next_ref, first_ref, fixed_ref, varying_ref, source_ref, spread_ref, mid_ref
):
    fixed_rows = fixed_ref.reshape(2, 4, LAYERS * TX, LANES)
    varying_rows = varying_ref.reshape(2, 3, LAYERS * TX, LANES)

    def native(ref, f, i, value):
        for t in range(2):
            rows = pl.ds(i - FIRST, LAYERS, stride=TX)
            ref[t, f, rows, :] = value[:, t * LANES : (t + 1) * LANES]

    @pl.when(on_device())
    def _():
        def newton(i, carry):
            newton_row(first_ref, next_ref, field_ref, mid_ref, i)
            return carry

        lax.fori_loop(FIRST - 1, FIRST + TX + 1, newton, 0, unroll=UNROLL_NEWTON)

        def relax(i, before):
            after, fixed, varying, _ = relax_row(mid_ref, next_ref, field_ref, i, before, 2)
            for t in range(2):
                fixed_rows[t, 0, pl.ds(i - FIRST, LAYERS, stride=TX), :] = mid_ref[0, i, t]
            for n in range(3):
                native(fixed_rows, n + 1, i, fixed[n])
                native(varying_rows, n, i, varying[n])
            return after

        start = x_face(mid_ref, next_ref, FIRST - 1, 2)
        lax.fori_loop(FIRST, FIRST + TX, relax, start, unroll=UNROLL_RELAX)

    @pl.when(jnp.logical_not(on_device()))
    def _():
        args = (next_ref, next_ref, field_ref, mid_ref)
        thermal_row(*args, FIRST - 1, halves=(1,), source=False, first=True)
        thermal_row(*args, FIRST + TX, halves=(0,), source=False, first=True)

        def three(i, carry):
            thermal_row(*args, i, source=False, first=True)
            return carry

        lax.fori_loop(FIRST, FIRST + TX, three, 0, unroll=UNROLL_HEAT)

        def four(i, carry):
            def keep(ref, f, i, value):
                native(fixed_rows, f, i, value)

            thermal_row(mid_ref, next_ref, field_ref, None, i, source=False, put_row=keep)
            return carry

        lax.fori_loop(FIRST, FIRST + TX, four, 0, unroll=UNROLL_HEAT)

        def top(i, carry):
            code = jnp.concatenate([field_ref[CODE, i, t] for t in range(TILES)], axis=1)
            inside = wide(field_ref, FREE, i)[0:1, :]
            source_ref[pl.ds(i - FIRST + 1, 1), :] = pick(code[0:1, :], SOURCE_TOP) * inside
            return carry

        lax.fori_loop(FIRST - 1, FIRST + TX + 1, top, 0, unroll=3)

        def sides(i, carry):
            code = jnp.concatenate([field_ref[CODE, i, t] for t in range(2)], axis=1)
            spread_ref[0, pl.ds(i - FIRST, 1), :] = pick(code[0:1, :], SPREAD_TOP)
            spread_ref[1, pl.ds(i - FIRST, 1), :] = pick(code[1:2, :], SPREAD_IN)
            return carry

        lax.fori_loop(FIRST, FIRST + TX, sides, 0, unroll=4)


def last_kernel(
    sheet_ref, fixed_ref, varying_ref, source_ref, spread_ref, contacts,
    state_out, sheet_out, done, total_ref, delta, sem,
):
    def send(src, f, t, layers):
        dst = state_out.at[0, f, layers, :, pl.ds(t * LANES, LANES)]
        return pltpu.make_async_copy(src.at[t, f, layers], dst, sem.at[f, t])

    @pl.when(on_device())
    def _():
        every = pl.ds(0, LAYERS)
        copies = [send(fixed_ref, 0, t, every) for t in range(2)]
        for c in copies:
            c.start()
        for t in range(2):
            cols = slice(t * LANES, (t + 1) * LANES)
            s = sheet_ref[0:TX, cols]
            slow = jnp.exp(-0.6 * s)
            fast = jnp.exp(0.3 * s)
            total = jnp.zeros((TX, LANES), F32)
            for layer in range(LAYERS):
                for f in (1, 2):
                    done[t, f, layer] = (
                        fixed_ref[t, f, layer] - varying_ref[t, f - 1, layer] * fast
                    )
                q = varying_ref[t, 2, layer] * slow
                total = total + q
                step = 0.8 / 3.5 if 0 < layer < LAYERS - 1 else 0.8 / 3.0
                if layer == 0:
                    step = step * (1.0 - contacts[:, cols].astype(F32))
                done[t, 3, layer] = fixed_ref[t, 3, layer] + step * (q + 0.5 * s)
            total_ref[0, :, cols] = total
            for f in (1, 2, 3):
                copies.append(send(done, f, t, every))
                copies[-1].start()
        copies.append(pltpu.make_async_copy(total_ref, sheet_out, sem.at[8, 0]))
        copies[-1].start()
        for c in copies:
            c.wait()

    @pl.when(jnp.logical_not(on_device()))
    def _():
        rest = pl.ds(2, LAYERS - 2)
        copies = [send(fixed_ref, f, t, rest) for t in range(2) for f in range(4)]
        for c in copies:
            c.start()
        delta[...] = source_ref[...] * sheet_ref[...]
        middle = delta[1 : TX + 1, :]
        by_x = (delta[0:TX, :], delta[2 : TX + 2, :])
        by_y = (prev_lane(middle), next_lane(middle))
        more = []
        for t in range(2):
            cols = slice(t * LANES, (t + 1) * LANES)
            mid = middle[:, cols]
            total = jnp.zeros((TX, LANES), F32)
            for f in range(4):
                around = 2.0 * mid + by_x[f // 2][:, cols] + by_y[f % 2][:, cols]
                value = fixed_ref[t, f, 0] + 1.1 * mid + spread_ref[0, :, cols] * around
                done[t, f, 0] = value
                total = total + value
                done[t, f, 1] = fixed_ref[t, f, 1] + spread_ref[1, :, cols] * mid
                dst = state_out.at[0, f, pl.ds(0, 2), :, pl.ds(t * LANES, LANES)]
                more.append(
                    pltpu.make_async_copy(done.at[t, f, pl.ds(0, 2)], dst, sem.at[4 + f, t])
                )
                more[-1].start()
            total_ref[0, :, cols] = 0.25 * total
        more.append(pltpu.make_async_copy(total_ref, sheet_out, sem.at[8, 0]))
        more[-1].start()
        for c in copies + more:
            c.wait()


def per_device(grid_state, materials, contacts, received_sheets):
    nx, ny = lax.axis_size("gx"), lax.axis_size("gy")

    def shift(block, axis, count, by):
        return lax.ppermute(block, axis, [(i, (i + by) % count) for i in range(count)])

    tile = (LAYERS, LANES)
    field_shape = (FIELDS, ROWS, TILES) + tile
    state_shape = (4, ROWS, TILES) + tile
    y_shape, x_shape = (2,) + tile, (SIDE + 1,) + tile
    inputs = (grid_state, materials, contacts, received_sheets)
    inputs = [pltpu.with_memory_space_constraint(v, pltpu.HBM) for v in inputs]
    raw_shapes = [
        (2, 4, LAYERS, TX, LANES),
        ((2, LAYERS, TX, LANES), jnp.int32),
        ((TX, 2 * LANES), jnp.int32),
        (1, TX, 2 * LANES),
    ]
    *raw, y_low, y_high = call(
        pack_kernel,
        raw_shapes + [y_shape, y_shape],
        inputs,
        specs=[HBM] * 4,
        scratch=[pltpu.SemaphoreType.DMA((6,))],
    )
    fields, x_low, x_high = call(rows_kernel, [field_shape, x_shape, x_shape], raw)
    left = shift(y_high, "gy", ny, 1)
    right = shift(y_low, "gy", ny, -1)
    x_low, x_high = call(
        corner_kernel, [x_shape, x_shape], [x_low, x_high, left, right], aliases={0: 0, 1: 1}
    )
    up = shift(x_high, "gx", nx, 1)
    down = shift(x_low, "gx", nx, -1)
    fields, following, middle, sheet = call(
        inner_kernel,
        [field_shape, state_shape, state_shape, SHEET_SHAPE],
        [fields, left, right],
        aliases={0: 0},
        cost=INNER,
    )
    fields, following, middle, sheet = call(
        rim_kernel,
        [field_shape, state_shape, state_shape, SHEET_SHAPE],
        [fields, following, middle, sheet, up, down],
        aliases={0: 0, 1: 1, 2: 2, 3: 3},
    )
    swapped = lax.ppermute(sheet, "half", [(0, 1), (1, 0)])
    fixed, varying, source, spread = call(
        second_kernel,
        [
            (2, 4, LAYERS, TX, LANES),
            (2, 3, LAYERS, TX, LANES),
            SHEET_SHAPE,
            (2, TX, 2 * LANES),
        ],
        [fields, following, middle],
        scratch=[pltpu.VMEM(state_shape, F32)],
        cost=1 << 23,
    )
    state, outgoing = call(
        last_kernel,
        [(1, 4, LAYERS, TX, 2 * LANES), (1, TX, 2 * LANES)],
        [swapped, fixed, varying, source, spread, contacts],
        out_specs=[HBM, HBM],
        scratch=[
            pltpu.VMEM((2, 4, LAYERS, TX, LANES), F32),
            pltpu.VMEM((1, TX, 2 * LANES), F32),
            pltpu.VMEM(SHEET_SHAPE, F32),
            pltpu.SemaphoreType.DMA((9, 2)),
        ],
    )
    return state, outgoing


def solution(mesh):
    placed = (
        P("half", None, None, "gx", "gy"),
        P("half", None, "gx", "gy"),
        P("gx", "gy"),
        P("half", "gx", "gy"),
    )
    return jax.shard_map(
        per_device,
        mesh=mesh,
        in_specs=placed,
        out_specs=(P("half", None, None, "gx", "gy"), P("half", "gx", "gy")),
        check_vma=False,
    )
```

```python
import jax
import jax.numpy as jnp
from jax import lax
from jax.experimental import pallas as pl
from jax.experimental.pallas import tpu as pltpu
from jax.sharding import PartitionSpec as P

F32 = jnp.float32
LAYERS = 8
TX = 16
LANES = 128
TILES = 3
HALO = 3
ROWS = TX + 2 * HALO
FIRST = HALO

DOPING = (1.5, -1.5, 0.6, -0.6)
MOB_ELEC = (1.0, 0.35, 0.7, 0.5)
MOB_HOLE = (0.4, 0.8, 0.3, 0.6)
CONDUCT = (1.0, 0.15, 2.5, 0.5)
CAPACITY = (0.6, 1.2, 0.4, 0.9)
POWER_ELEC = tuple(0.05 * m * m for m in MOB_ELEC)
POWER_HOLE = tuple(0.05 * m * m for m in MOB_HOLE)
LOSS_ELEC = tuple(0.3 / m for m in MOB_ELEC)
LOSS_HOLE = tuple(0.3 / m for m in MOB_HOLE)
SPREAD_TOP = tuple(0.9 * k / (5.0 * k + c) for k, c in zip(CONDUCT, CAPACITY))
SPREAD_IN = tuple(0.9 * k / (6.0 * k + c) for k, c in zip(CONDUCT, CAPACITY))
SOURCE_TOP = tuple(0.45 / (5.0 * k + c) for k, c in zip(CONDUCT, CAPACITY))

CODE, FREE, SHEET = 4, 5, 6
FIELDS = 7
WIDTH = (3, 2, 2, 2, 2, 2, 2)
SLOT = (0, 3, 5, 7, 9, 11, 13)
LOW = [(f, r) for f in range(FIELDS) for r in range(WIDTH[f])]
HIGH = [(f, TX - WIDTH[f] + r) for f in range(FIELDS) for r in range(WIDTH[f])]
BULK = sum(1 for f, _ in LOW if f < FREE)
SIDE = 2 * BULK + 2
VMEM = pl.BlockSpec(memory_space=pltpu.VMEM)
HBM = pl.BlockSpec(memory_space=pltpu.HBM)
SHEET_SHAPE = (24, TILES * LANES)
INNER = 1 << 23
UNROLL_NEWTON, UNROLL_RELAX, UNROLL_HEAT = 2, 4, 2


def call(kernel, outs, ins, specs=None, out_specs=None, scratch=(), aliases=None, cost=1 << 20):
    return pl.pallas_call(
        kernel,
        out_shape=[
            jax.ShapeDtypeStruct(*(s if isinstance(s[0], tuple) else (s, F32))) for s in outs
        ],
        in_specs=specs or [VMEM] * len(ins),
        out_specs=out_specs or [VMEM] * len(outs),
        scratch_shapes=list(scratch),
        input_output_aliases=aliases or {},
        compiler_params=pltpu.CompilerParams(vmem_limit_bytes=12 << 20),
        cost_estimate=pl.CostEstimate(flops=0, bytes_accessed=cost, transcendentals=0),
    )(*ins)


def lane_index():
    return lax.broadcasted_iota(jnp.int32, (LAYERS, LANES), 1)


def layer_index(width):
    return lax.broadcasted_iota(jnp.int32, (LAYERS, width), 0)


def pick(code, table):
    low = jnp.where(code < 0.5, table[0], table[1])
    high = jnp.where(code < 2.5, table[2], table[3])
    return jnp.where(code < 1.5, low, high)


def wide(ref, f, i):
    return jnp.concatenate([ref[f, i, t] for t in range(TILES)], axis=1)


def put(ref, f, i, value):
    for t in range(TILES):
        ref[f, i, t] = value[:, t * LANES : (t + 1) * LANES]


def cut(v, tiles):
    return v if v.shape[1] == tiles * LANES else v[:, : tiles * LANES]


def recip(v):
    r = pl.reciprocal(v, approx=True)
    return r * (2.0 - v * r)


def prev_lane(v):
    return pltpu.roll(v, 1, 1)


def next_lane(v):
    return pltpu.roll(v, v.shape[1] - 1, 1)


def above(v):
    return pltpu.roll(v, 1, 0)


def below(v):
    return pltpu.roll(v, LAYERS - 1, 0)


def on_device():
    return lax.axis_index("half") == 0


def is_even(axis):
    return lax.axis_index(axis) % 2 == 0


def own_row(raw_rows, code_rows, contact_ref, sheet_ref, device, sub, f, x, t):
    cols = slice(t * LANES, (t + 1) * LANES)
    if f < 4:
        return raw_rows[t, f, pl.ds(x, LAYERS, stride=TX), :]
    if f == CODE:
        return code_rows[t, pl.ds(x, LAYERS, stride=TX), :].astype(F32)
    if f == FREE:
        held = jnp.broadcast_to(contact_ref[x : x + 1, cols], (LAYERS, LANES))
        return jnp.where((held == 1) & (sub == 0) & device, 0.0, 1.0)
    return jnp.broadcast_to(sheet_ref[0, x : x + 1, cols], (LAYERS, LANES))


def pack_kernel(
    grid, codes, contacts, sheets, raw, raw_code, raw_contact, raw_sheet, first_ref, second_ref, sem
):
    copies = [
        pltpu.make_async_copy(contacts, raw_contact, sem.at[4]),
        pltpu.make_async_copy(sheets, raw_sheet, sem.at[5]),
    ]
    for t in range(2):
        cols = pl.ds(t * LANES, LANES)
        copies.append(
            pltpu.make_async_copy(grid.at[0, :, :, :, cols], raw.at[t], sem.at[2 * t])
        )
        copies.append(
            pltpu.make_async_copy(codes.at[0, :, :, cols], raw_code.at[t], sem.at[2 * t + 1])
        )
    for c in copies:
        c.start()
    lanes = lane_index()
    even = is_even("gy")
    raw_rows = raw.reshape(2, 4, LAYERS * TX, LANES)
    code_rows = raw_code.reshape(2, LAYERS * TX, LANES)
    args = (raw_rows, code_rows, raw_contact, raw_sheet, on_device(), layer_index(LANES))
    for c in copies:
        c.wait()
    for block in range(2):
        left = jnp.zeros((LAYERS, LANES), F32)
        right = jnp.zeros((LAYERS, LANES), F32)
        for row in range(8):
            for f in range(FIELDS):
                w = WIDTH[f]
                at = 16 * row + SLOT[f]
                here = (lanes >= at) & (lanes < at + w)
                low = own_row(*args, f, 8 * block + row, 0)
                high = own_row(*args, f, 8 * block + row, 1)
                left = jnp.where(here, pltpu.roll(low, at, 1) if at else low, left)
                right = jnp.where(here, pltpu.roll(high, (at + w) % LANES, 1), right)
        first_ref[block] = jnp.where(even, right, left)
        second_ref[block] = jnp.where(even, left, right)


def rows_kernel(raw, raw_code, raw_contact, raw_sheet, field_ref, first_ref, second_ref):
    sub = layer_index(LANES)
    even = is_even("gx")
    raw_rows = raw.reshape(2, 4, LAYERS * TX, LANES)
    code_rows = raw_code.reshape(2, LAYERS * TX, LANES)
    args = (raw_rows, code_rows, raw_contact, raw_sheet, on_device(), sub)
    for f in range(FIELDS):
        for x in range(TX):
            for t in range(2):
                field_ref[f, FIRST + x, t] = own_row(*args, f, x, t)

    def both(x, t):
        free = [field_ref[FREE, FIRST + x + n, t] for n in range(2)]
        sheet = [field_ref[SHEET, FIRST + x + n, t] for n in range(2)]
        v = jnp.where(sub == 0, free[0], pltpu.roll(free[1], 1, 0))
        v = jnp.where(sub < 2, v, 1.0)
        return jnp.where(sub < 4, v, jnp.where(sub < 6, sheet[0], sheet[1]))

    for n in range(BULK + 1):
        for t in range(2):
            if n < BULK:
                f, x = LOW[n]
                low = field_ref[f, FIRST + x, t]
                high = field_ref[f, FIRST + HIGH[n][1], t]
            else:
                low, high = both(0, t), both(TX - 2, t)
            first_ref[2 * n + t] = jnp.where(even, high, low)
            second_ref[2 * n + t] = jnp.where(even, low, high)


def y_masks(lanes):
    gy = lax.axis_index("gy")
    has_right = gy < lax.axis_size("gy") - 1
    has_left = gy > 0
    right = {w: (lanes < w) & has_right for w in (2, 3)}
    left = {w: (lanes >= LANES - w) & has_left for w in (2, 3)}
    return left, right


def sides(first_ref, second_ref, axis):
    even = is_even(axis)
    first, second = first_ref[...], second_ref[...]
    return jnp.where(even, second, first), jnp.where(even, first, second)


def side_columns(before, after, f, x, masks):
    w = WIDTH[f]
    at = 16 * (x % 8) + SLOT[f]
    left, right = masks
    a = pltpu.roll(after[x // 8], (LANES - at) % LANES, 1)
    b = pltpu.roll(before[x // 8], (2 * LANES - at - w) % LANES, 1)
    return jnp.where(right[w], a, jnp.where(left[w], b, 0.0))


def corner_kernel(first_in, second_in, y_first, y_second, first_ref, second_ref):
    lanes = lane_index()
    masks = y_masks(lanes)
    before, after = sides(y_first, y_second, "gy")
    even = is_even("gx")
    packed = []
    for items in (LOW, HIGH):
        both = jnp.zeros((LAYERS, LANES), F32)
        for n, (f, x) in enumerate(items):
            side = side_columns(before, after, f, x, masks)
            here = (lanes >= 8 * n) & (lanes < 8 * n + 8)
            both = jnp.where(here, pltpu.roll(side, 8 * n + 3, 1), both)
        packed.append(both)
    first_ref[SIDE] = jnp.where(even, packed[1], packed[0])
    second_ref[SIDE] = jnp.where(even, packed[0], packed[1])


def newton_row(uref, fref, fields, dst, i):
    width = TILES * LANES
    sub = layer_index(width)
    u, e, h = wide(uref, 0, i), wide(fref, 1, i), wide(fref, 2, i)
    code = wide(fields, CODE, i)
    total = wide(uref, 0, i - 1) + wide(uref, 0, i + 1) + prev_lane(u) + next_lane(u)
    total = total + jnp.where(sub > 0, above(u), 0.0) + jnp.where(sub < LAYERS - 1, below(u), 0.0)
    weight = jnp.where((sub > 0) & (sub < LAYERS - 1), 6.0, 5.0)
    r = total - weight * u + 0.7 * (h - e + pick(code, DOPING))
    diag = weight + 0.7 * (jnp.abs(e) + jnp.abs(h))
    put(dst, 0, i, u + (0.8 * wide(fields, FREE, i)) * (r * recip(diag)))


def face(p, n):
    g = 0.5 * jnp.tanh(n[0] - p[0])
    a = (n[1] - p[1]) - (n[1] + p[1]) * g
    c = (n[2] - p[2]) + (n[2] + p[2]) * g
    return a, c, g


def x_face(uref, fref, i, tiles=TILES):
    p = (wide(uref, 0, i), wide(fref, 1, i), wide(fref, 2, i))
    n = (wide(uref, 0, i + 1), wide(fref, 1, i + 1), wide(fref, 2, i + 1))
    return face([cut(v, tiles) for v in p], [cut(v, tiles) for v in n])


def relax_row(uref, fref, fields, i, before, tiles=TILES):
    sub = layer_index(tiles * LANES)
    here = (wide(uref, 0, i), wide(fref, 1, i), wide(fref, 2, i))
    k = wide(fref, 3, i)
    after = (wide(uref, 0, i + 1), wide(fref, 1, i + 1), wide(fref, 2, i + 1))
    y_after = face(here, tuple(next_lane(v) for v in here))
    y_before = tuple(cut(prev_lane(v), tiles) for v in y_after)
    y_after = tuple(cut(v, tiles) for v in y_after)
    spread = cut(prev_lane(k), tiles) + cut(next_lane(k), tiles)
    here = tuple(cut(v, tiles) for v in here)
    k = cut(k, tiles)
    u, e, h = here
    after = face(here, tuple(cut(v, tiles) for v in after))
    l_after = face(here, tuple(below(v) for v in here))
    l_after = tuple(jnp.where(sub < LAYERS - 1, v, 0.0) for v in l_after)
    l_before = tuple(above(v) for v in l_after)
    net = [
        (after[n] - before[n]) + (y_after[n] - y_before[n]) + (l_after[n] - l_before[n])
        for n in range(3)
    ]
    square = [
        (after[n] * after[n] + before[n] * before[n])
        + (y_after[n] * y_after[n] + y_before[n] * y_before[n])
        + (l_after[n] * l_after[n] + l_before[n] * l_before[n])
        for n in range(2)
    ]
    inner = (sub > 0) & (sub < LAYERS - 1)
    weight = jnp.where(inner, 6.0, 5.0)
    spread = spread + cut(wide(fref, 3, i - 1), tiles) + cut(wide(fref, 3, i + 1), tiles)
    spread = spread + jnp.where(sub > 0, above(k), 0.0)
    spread = spread + jnp.where(sub < LAYERS - 1, below(k), 0.0) - weight * k
    code = cut(wide(fields, CODE, i), tiles)
    free = cut(wide(fields, FREE, i), tiles)
    power = pick(code, POWER_ELEC) * square[0] + pick(code, POWER_HOLE) * square[1]
    recombine = (e * h - 1.0) * recip(e * e + h * h + 2.0)
    step = 0.8 * free
    scale_e = step * recip(weight + net[2])
    scale_h = step * recip(weight - net[2])
    heat_step = free * jnp.where(inner, 0.8 / 3.5, 0.8 / 3.0)
    fixed = (
        e + scale_e * net[0],
        h + scale_h * net[1],
        k + heat_step * (0.5 * spread - 0.5 * k),
    )
    varying = (
        scale_e * recombine * pick(code, LOSS_ELEC),
        scale_h * recombine * pick(code, LOSS_HOLE),
        power,
    )
    return after, fixed, varying, heat_step


def relax_first(uref, fref, fields, dst, sheet_ref, i, before):
    after, fixed, varying, heat_step = relax_row(uref, fref, fields, i, before)
    s = wide(fields, SHEET, i)
    slow = jnp.exp(-0.6 * s)
    fast = jnp.exp(0.3 * s)
    q = varying[2] * slow
    put(dst, 1, i, fixed[0] - varying[0] * fast)
    put(dst, 2, i, fixed[1] - varying[1] * fast)
    put(dst, 3, i, fixed[2] + heat_step * (q + 0.5 * s))
    sheet_ref[pl.ds(i - 2, 1), :] = jnp.sum(q, axis=0, keepdims=True)
    return after


def thermal_row(
    src, anchor, fields, dst, i, halves=(0, 1), source=True, first=False, put_row=put
):
    width = TILES * LANES
    sub = layer_index(width)
    top = sub == 0
    cells = [wide(src, f, i) for f in range(4)]
    code = wide(fields, CODE, i)
    spread = jnp.where(top, pick(code, SPREAD_TOP), pick(code, SPREAD_IN))
    held = 0.9 - jnp.where(top, 5.0, 6.0) * spread
    spread = spread * wide(fields, FREE, i)
    if source:
        heat = jnp.where(top, pick(code, SOURCE_TOP) * wide(fields, SHEET, i), 0.0)
    out = []
    for s in halves:
        for t in range(2):
            f = 2 * s + t
            v = cells[f]
            if s == 0:
                total = wide(src, 2 + t, i - 1) + cells[2 + t]
            else:
                total = cells[t] + wide(src, t, i + 1)
            other = cells[2 * s + 1 - t]
            total = total + other + (prev_lane(other) if t == 0 else next_lane(other))
            total = total + jnp.where(sub > 0, above(v), 0.0)
            total = total + jnp.where(sub < LAYERS - 1, below(v), 0.0)
            value = spread * total + 0.1 * v
            value = value + held * (v if first else wide(anchor, f, i))
            if source:
                value = value + heat
            out.append(value)
            put_row(dst, f, i, value)
    return out


def top_mean(cells):
    total = (cells[0] + cells[1]) + (cells[2] + cells[3])
    return 0.25 * total[0:1, :]


def inner_kernel(field_in, y_first, y_second, field_ref, next_ref, mid_ref, sheet_ref):
    lanes = lane_index()
    masks = y_masks(lanes)
    before, after = sides(y_first, y_second, "gy")
    for x in range(TX):
        for f in range(FIELDS):
            field_ref[f, FIRST + x, 2] = side_columns(before, after, f, x, masks)

    @pl.when(on_device())
    def _():
        def newton(i, carry):
            newton_row(field_ref, field_ref, field_ref, mid_ref, i)
            return carry

        lax.fori_loop(FIRST + 1, FIRST + TX - 1, newton, 0, unroll=UNROLL_NEWTON)

        def relax(i, carry):
            return relax_first(mid_ref, field_ref, field_ref, next_ref, sheet_ref, i, carry)

        start = x_face(mid_ref, field_ref, FIRST + 1)
        lax.fori_loop(FIRST + 2, FIRST + TX - 2, relax, start, unroll=UNROLL_RELAX)

    @pl.when(jnp.logical_not(on_device()))
    def _():
        def one(i, carry):
            thermal_row(field_ref, field_ref, field_ref, mid_ref, i, first=True)
            return carry

        lax.fori_loop(FIRST + 1, FIRST + TX - 1, one, 0, unroll=UNROLL_HEAT)

        def two(i, carry):
            cells = thermal_row(mid_ref, field_ref, field_ref, next_ref, i)
            sheet_ref[pl.ds(i - FIRST, 1), :] = top_mean(cells)
            return carry

        lax.fori_loop(FIRST + 2, FIRST + TX - 2, two, 0, unroll=UNROLL_HEAT)


def rim_kernel(
    field_in, next_in, mid_in, sheet_in, x_first, x_second,
    field_ref, next_ref, mid_ref, sheet_ref,
):
    lanes = lane_index()
    sub = layer_index(LANES)
    gx = lax.axis_index("gx")
    has_up = gx > 0
    has_down = gx < lax.axis_size("gx") - 1
    edge = {w: (lanes < w) | (lanes >= LANES - w) for w in (2, 3)}
    up, down = sides(x_first, x_second, "gx")
    for items, src, ok, base in (
        (HIGH, up, has_up, FIRST - TX),
        (LOW, down, has_down, FIRST + TX),
    ):
        packed = src[SIDE]
        for n, (f, x) in enumerate(items):
            for t in range(2):
                second = x % 2
                if f < FREE:
                    v = src[2 * n + t]
                elif f == FREE:
                    top = src[2 * BULK + t][second : second + 1, :]
                    v = jnp.where(sub == 0, jnp.broadcast_to(top, (LAYERS, LANES)), 1.0)
                else:
                    row = src[2 * BULK + t][4 + 2 * second : 5 + 2 * second, :]
                    v = jnp.broadcast_to(row, (LAYERS, LANES))
                field_ref[f, base + x, t] = jnp.where(ok, v, 0.0)
            side = pltpu.roll(packed, LANES - 8 * n - 3, 1)
            field_ref[f, base + x, 2] = jnp.where(edge[WIDTH[f]] & ok, side, 0.0)

    @pl.when(on_device())
    def _():
        for n in range(3):
            for i in (FIRST - 2 + n, FIRST + TX - 1 + n):
                newton_row(field_ref, field_ref, field_ref, mid_ref, i)
        args = (mid_ref, field_ref, field_ref, next_ref, sheet_ref)
        one = x_face(mid_ref, field_ref, FIRST - 2)
        two = x_face(mid_ref, field_ref, FIRST + TX - 3)
        for n in range(3):
            one = relax_first(*args, FIRST - 1 + n, one)
            two = relax_first(*args, FIRST + TX - 2 + n, two)

    @pl.when(jnp.logical_not(on_device()))
    def _():
        args = (field_ref, field_ref, field_ref, mid_ref)
        thermal_row(*args, FIRST - 2, halves=(1,), first=True)
        thermal_row(*args, FIRST + TX + 1, halves=(0,), first=True)
        for i in (FIRST - 1, FIRST, FIRST + TX - 1, FIRST + TX):
            thermal_row(*args, i, first=True)
        for n in range(3):
            for i in (FIRST - 1 + n, FIRST + TX - 2 + n):
                cells = thermal_row(mid_ref, field_ref, field_ref, next_ref, i)
                if FIRST <= i < FIRST + TX:
                    sheet_ref[pl.ds(i - FIRST, 1), :] = top_mean(cells)


def second_kernel(
    field_ref, next_ref, first_ref, fixed_ref, varying_ref, source_ref, spread_ref, mid_ref
):
    fixed_rows = fixed_ref.reshape(2, 4, LAYERS * TX, LANES)
    varying_rows = varying_ref.reshape(2, 3, LAYERS * TX, LANES)

    def native(ref, f, i, value):
        for t in range(2):
            rows = pl.ds(i - FIRST, LAYERS, stride=TX)
            ref[t, f, rows, :] = value[:, t * LANES : (t + 1) * LANES]

    @pl.when(on_device())
    def _():
        def newton(i, carry):
            newton_row(first_ref, next_ref, field_ref, mid_ref, i)
            return carry

        lax.fori_loop(FIRST - 1, FIRST + TX + 1, newton, 0, unroll=UNROLL_NEWTON)

        def relax(i, before):
            after, fixed, varying, _ = relax_row(mid_ref, next_ref, field_ref, i, before, 2)
            for t in range(2):
                fixed_rows[t, 0, pl.ds(i - FIRST, LAYERS, stride=TX), :] = mid_ref[0, i, t]
            for n in range(3):
                native(fixed_rows, n + 1, i, fixed[n])
                native(varying_rows, n, i, varying[n])
            return after

        start = x_face(mid_ref, next_ref, FIRST - 1, 2)
        lax.fori_loop(FIRST, FIRST + TX, relax, start, unroll=UNROLL_RELAX)

    @pl.when(jnp.logical_not(on_device()))
    def _():
        args = (next_ref, next_ref, field_ref, mid_ref)
        thermal_row(*args, FIRST - 1, halves=(1,), source=False, first=True)
        thermal_row(*args, FIRST + TX, halves=(0,), source=False, first=True)

        def three(i, carry):
            thermal_row(*args, i, source=False, first=True)
            return carry

        lax.fori_loop(FIRST, FIRST + TX, three, 0, unroll=UNROLL_HEAT)

        def four(i, carry):
            def keep(ref, f, i, value):
                native(fixed_rows, f, i, value)

            thermal_row(mid_ref, next_ref, field_ref, None, i, source=False, put_row=keep)
            return carry

        lax.fori_loop(FIRST, FIRST + TX, four, 0, unroll=UNROLL_HEAT)

        def top(i, carry):
            code = jnp.concatenate([field_ref[CODE, i, t] for t in range(TILES)], axis=1)
            inside = wide(field_ref, FREE, i)[0:1, :]
            source_ref[pl.ds(i - FIRST + 1, 1), :] = pick(code[0:1, :], SOURCE_TOP) * inside
            return carry

        lax.fori_loop(FIRST - 1, FIRST + TX + 1, top, 0, unroll=3)

        def sides(i, carry):
            code = jnp.concatenate([field_ref[CODE, i, t] for t in range(2)], axis=1)
            spread_ref[0, pl.ds(i - FIRST, 1), :] = pick(code[0:1, :], SPREAD_TOP)
            spread_ref[1, pl.ds(i - FIRST, 1), :] = pick(code[1:2, :], SPREAD_IN)
            return carry

        lax.fori_loop(FIRST, FIRST + TX, sides, 0, unroll=4)


def last_kernel(
    sheet_ref, fixed_ref, varying_ref, source_ref, spread_ref, contacts,
    state_out, sheet_out, done, total_ref, delta, sem,
):
    def send(src, f, t, layers):
        dst = state_out.at[0, f, layers, :, pl.ds(t * LANES, LANES)]
        return pltpu.make_async_copy(src.at[t, f, layers], dst, sem.at[f, t])

    @pl.when(on_device())
    def _():
        every = pl.ds(0, LAYERS)
        copies = [send(fixed_ref, 0, t, every) for t in range(2)]
        for c in copies:
            c.start()
        for t in range(2):
            cols = slice(t * LANES, (t + 1) * LANES)
            s = sheet_ref[0:TX, cols]
            slow = jnp.exp(-0.6 * s)
            fast = jnp.exp(0.3 * s)
            total = jnp.zeros((TX, LANES), F32)
            for layer in range(LAYERS):
                for f in (1, 2):
                    done[t, f, layer] = (
                        fixed_ref[t, f, layer] - varying_ref[t, f - 1, layer] * fast
                    )
                q = varying_ref[t, 2, layer] * slow
                total = total + q
                step = 0.8 / 3.5 if 0 < layer < LAYERS - 1 else 0.8 / 3.0
                if layer == 0:
                    step = step * (1.0 - contacts[:, cols].astype(F32))
                done[t, 3, layer] = fixed_ref[t, 3, layer] + step * (q + 0.5 * s)
            total_ref[0, :, cols] = total
            for f in (1, 2, 3):
                copies.append(send(done, f, t, every))
                copies[-1].start()
        copies.append(pltpu.make_async_copy(total_ref, sheet_out, sem.at[8, 0]))
        copies[-1].start()
        for c in copies:
            c.wait()

    @pl.when(jnp.logical_not(on_device()))
    def _():
        rest = pl.ds(2, LAYERS - 2)
        copies = [send(fixed_ref, f, t, rest) for t in range(2) for f in range(4)]
        for c in copies:
            c.start()
        delta[...] = source_ref[...] * sheet_ref[...]
        middle = delta[1 : TX + 1, :]
        by_x = (delta[0:TX, :], delta[2 : TX + 2, :])
        by_y = (prev_lane(middle), next_lane(middle))
        more = []
        for t in range(2):
            cols = slice(t * LANES, (t + 1) * LANES)
            mid = middle[:, cols]
            total = jnp.zeros((TX, LANES), F32)
            for f in range(4):
                around = 2.0 * mid + by_x[f // 2][:, cols] + by_y[f % 2][:, cols]
                value = fixed_ref[t, f, 0] + 1.1 * mid + spread_ref[0, :, cols] * around
                done[t, f, 0] = value
                total = total + value
                done[t, f, 1] = fixed_ref[t, f, 1] + spread_ref[1, :, cols] * mid
                dst = state_out.at[0, f, pl.ds(0, 2), :, pl.ds(t * LANES, LANES)]
                more.append(
                    pltpu.make_async_copy(done.at[t, f, pl.ds(0, 2)], dst, sem.at[4 + f, t])
                )
                more[-1].start()
            total_ref[0, :, cols] = 0.25 * total
        more.append(pltpu.make_async_copy(total_ref, sheet_out, sem.at[8, 0]))
        more[-1].start()
        for c in copies + more:
            c.wait()


def per_device(grid_state, materials, contacts, received_sheets):
    nx, ny = lax.axis_size("gx"), lax.axis_size("gy")

    def swap(block, axis, parity):
        route = []
        for i in range(nx):
            for j in range(ny):
                at, count = (i, nx) if axis == "gx" else (j, ny)
                to = ((at - parity) ^ 1) + parity
                if axis == "gx":
                    p = (to, j) if 0 <= to < count else (i, j ^ 1)
                else:
                    p = (i, to) if 0 <= to < count else (i ^ 1, j)
                route.append((i * ny + j, p[0] * ny + p[1]))
        return lax.ppermute(block, ("gx", "gy"), route)

    tile = (LAYERS, LANES)
    field_shape = (FIELDS, ROWS, TILES) + tile
    state_shape = (4, ROWS, TILES) + tile
    y_shape, x_shape = (2,) + tile, (SIDE + 1,) + tile
    inputs = (grid_state, materials, contacts, received_sheets)
    inputs = [pltpu.with_memory_space_constraint(v, pltpu.HBM) for v in inputs]
    raw_shapes = [
        (2, 4, LAYERS, TX, LANES),
        ((2, LAYERS, TX, LANES), jnp.int32),
        ((TX, 2 * LANES), jnp.int32),
        (1, TX, 2 * LANES),
    ]
    *raw, y_first, y_second = call(
        pack_kernel,
        raw_shapes + [y_shape, y_shape],
        inputs,
        specs=[HBM] * 4,
        scratch=[pltpu.SemaphoreType.DMA((6,))],
    )
    fields, x_first, x_second = call(rows_kernel, [field_shape, x_shape, x_shape], raw)
    y_second = swap(y_second, "gy", 1)
    y_first = swap(y_first, "gy", 0)
    x_first, x_second = call(
        corner_kernel,
        [x_shape, x_shape],
        [x_first, x_second, y_first, y_second],
        aliases={0: 0, 1: 1},
    )
    x_second = swap(x_second, "gx", 1)
    x_first = swap(x_first, "gx", 0)
    fields, following, middle, sheet = call(
        inner_kernel,
        [field_shape, state_shape, state_shape, SHEET_SHAPE],
        [fields, y_first, y_second],
        aliases={0: 0},
        cost=INNER,
    )
    fields, following, middle, sheet = call(
        rim_kernel,
        [field_shape, state_shape, state_shape, SHEET_SHAPE],
        [fields, following, middle, sheet, x_first, x_second],
        aliases={0: 0, 1: 1, 2: 2, 3: 3},
    )
    swapped = lax.ppermute(sheet, "half", [(0, 1), (1, 0)])
    fixed, varying, source, spread = call(
        second_kernel,
        [
            (2, 4, LAYERS, TX, LANES),
            (2, 3, LAYERS, TX, LANES),
            SHEET_SHAPE,
            (2, TX, 2 * LANES),
        ],
        [fields, following, middle],
        scratch=[pltpu.VMEM(state_shape, F32)],
        cost=1 << 23,
    )
    state, outgoing = call(
        last_kernel,
        [(1, 4, LAYERS, TX, 2 * LANES), (1, TX, 2 * LANES)],
        [swapped, fixed, varying, source, spread, contacts],
        out_specs=[HBM, HBM],
        scratch=[
            pltpu.VMEM((2, 4, LAYERS, TX, LANES), F32),
            pltpu.VMEM((1, TX, 2 * LANES), F32),
            pltpu.VMEM(SHEET_SHAPE, F32),
            pltpu.SemaphoreType.DMA((9, 2)),
        ],
    )
    return state, outgoing


def solution(mesh):
    placed = (
        P("half", None, None, "gx", "gy"),
        P("half", None, "gx", "gy"),
        P("gx", "gy"),
        P("half", "gx", "gy"),
    )
    return jax.shard_map(
        per_device,
        mesh=mesh,
        in_specs=placed,
        out_specs=(P("half", None, None, "gx", "gy"), P("half", "gx", "gy")),
        check_vma=False,
    )
```

```python
import jax
import jax.numpy as jnp
from jax import lax
from jax.experimental import pallas as pl
from jax.experimental.pallas import tpu as pltpu
from jax.sharding import PartitionSpec as P

F32 = jnp.float32
LAYERS = 8
TX = 16
LANES = 128
TILES = 3
HALO = 3
ROWS = TX + 2 * HALO
FIRST = HALO

DOPING = (1.5, -1.5, 0.6, -0.6)
MOB_ELEC = (1.0, 0.35, 0.7, 0.5)
MOB_HOLE = (0.4, 0.8, 0.3, 0.6)
CONDUCT = (1.0, 0.15, 2.5, 0.5)
CAPACITY = (0.6, 1.2, 0.4, 0.9)
POWER_ELEC = tuple(0.05 * m * m for m in MOB_ELEC)
POWER_HOLE = tuple(0.05 * m * m for m in MOB_HOLE)
LOSS_ELEC = tuple(0.3 / m for m in MOB_ELEC)
LOSS_HOLE = tuple(0.3 / m for m in MOB_HOLE)
SPREAD_TOP = tuple(0.9 * k / (5.0 * k + c) for k, c in zip(CONDUCT, CAPACITY))
SPREAD_IN = tuple(0.9 * k / (6.0 * k + c) for k, c in zip(CONDUCT, CAPACITY))
SOURCE_TOP = tuple(0.45 / (5.0 * k + c) for k, c in zip(CONDUCT, CAPACITY))

CODE, FREE, SHEET = 4, 5, 6
FIELDS = 7
WIDTH = (3, 2, 2, 2, 2, 2, 2)
SLOT = (0, 3, 5, 7, 9, 11, 13)
LOW = [(f, r) for f in range(FIELDS) for r in range(WIDTH[f])]
HIGH = [(f, TX - WIDTH[f] + r) for f in range(FIELDS) for r in range(WIDTH[f])]
BULK = sum(1 for f, _ in LOW if f < FREE)
SIDE = 2 * BULK + 2
VMEM = pl.BlockSpec(memory_space=pltpu.VMEM)
HBM = pl.BlockSpec(memory_space=pltpu.HBM)
SHEET_SHAPE = (24, TILES * LANES)
INNER = 10**10
UNROLL_NEWTON, UNROLL_RELAX, UNROLL_HEAT = 2, 4, 2


def call(kernel, outs, ins, specs=None, out_specs=None, scratch=(), aliases=None, cost=1 << 20):
    return pl.pallas_call(
        kernel,
        out_shape=[
            jax.ShapeDtypeStruct(*(s if isinstance(s[0], tuple) else (s, F32))) for s in outs
        ],
        in_specs=specs or [VMEM] * len(ins),
        out_specs=out_specs or [VMEM] * len(outs),
        scratch_shapes=list(scratch),
        input_output_aliases=aliases or {},
        compiler_params=pltpu.CompilerParams(vmem_limit_bytes=12 << 20),
        cost_estimate=pl.CostEstimate(flops=cost, bytes_accessed=1 << 20, transcendentals=0),
    )(*ins)


def lane_index():
    return lax.broadcasted_iota(jnp.int32, (LAYERS, LANES), 1)


def layer_index(width):
    return lax.broadcasted_iota(jnp.int32, (LAYERS, width), 0)


def pick(code, table):
    low = jnp.where(code < 0.5, table[0], table[1])
    high = jnp.where(code < 2.5, table[2], table[3])
    return jnp.where(code < 1.5, low, high)


def wide(ref, f, i):
    return jnp.concatenate([ref[f, i, t] for t in range(TILES)], axis=1)


def put(ref, f, i, value):
    for t in range(TILES):
        ref[f, i, t] = value[:, t * LANES : (t + 1) * LANES]


def cut(v, tiles):
    return v if v.shape[1] == tiles * LANES else v[:, : tiles * LANES]


def recip(v):
    r = pl.reciprocal(v, approx=True)
    return r * (2.0 - v * r)


def prev_lane(v):
    return pltpu.roll(v, 1, 1)


def next_lane(v):
    return pltpu.roll(v, v.shape[1] - 1, 1)


def above(v):
    return pltpu.roll(v, 1, 0)


def below(v):
    return pltpu.roll(v, LAYERS - 1, 0)


def on_device():
    return lax.axis_index("half") == 0


def is_even(axis):
    return lax.axis_index(axis) % 2 == 0


def own_row(raw_rows, code_rows, contact_ref, sheet_ref, device, sub, f, x, t):
    cols = slice(t * LANES, (t + 1) * LANES)
    if f < 4:
        return raw_rows[t, f, pl.ds(x, LAYERS, stride=TX), :]
    if f == CODE:
        return code_rows[t, pl.ds(x, LAYERS, stride=TX), :].astype(F32)
    if f == FREE:
        held = jnp.broadcast_to(contact_ref[x : x + 1, cols], (LAYERS, LANES))
        return jnp.where((held == 1) & (sub == 0) & device, 0.0, 1.0)
    return jnp.broadcast_to(sheet_ref[0, x : x + 1, cols], (LAYERS, LANES))


def pack_kernel(
    grid, codes, contacts, sheets, raw, raw_code, raw_contact, raw_sheet, first_ref, second_ref, sem
):
    small = [
        pltpu.make_async_copy(contacts, raw_contact, sem.at[10]),
        pltpu.make_async_copy(sheets, raw_sheet, sem.at[11]),
    ]
    copies = []
    for t in range(2):
        cols = pl.ds(t * LANES, LANES)
        copies.append(
            [
                pltpu.make_async_copy(grid.at[0, f, :, :, cols], raw.at[t, f], sem.at[5 * t + f])
                for f in range(4)
            ]
        )
        copies[t].append(
            pltpu.make_async_copy(codes.at[0, :, :, cols], raw_code.at[t], sem.at[5 * t + 4])
        )
    for c in copies[0] + small + copies[1]:
        c.start()
    lanes = lane_index()
    even = is_even("gy")
    raw_rows = raw.reshape(2, 4, LAYERS * TX, LANES)
    code_rows = raw_code.reshape(2, LAYERS * TX, LANES)
    args = (raw_rows, code_rows, raw_contact, raw_sheet, on_device(), layer_index(LANES))
    for c in small:
        c.wait()
    packed = []
    for t in range(2):
        for c in copies[t]:
            c.wait()
        for block in range(2):
            side = jnp.zeros((LAYERS, LANES), F32)
            for row in range(8):
                for f in range(FIELDS):
                    w = WIDTH[f]
                    at = 16 * row + SLOT[f]
                    here = (lanes >= at) & (lanes < at + w)
                    v = own_row(*args, f, 8 * block + row, t)
                    by = (at + t * w) % LANES
                    side = jnp.where(here, pltpu.roll(v, by, 1) if by else v, side)
            packed.append(side)
    for block in range(2):
        left, right = packed[block], packed[2 + block]
        first_ref[block] = jnp.where(even, right, left)
        second_ref[block] = jnp.where(even, left, right)


def rows_kernel(raw, raw_code, raw_contact, raw_sheet, field_ref, first_ref, second_ref):
    sub = layer_index(LANES)
    even = is_even("gx")
    raw_rows = raw.reshape(2, 4, LAYERS * TX, LANES)
    code_rows = raw_code.reshape(2, LAYERS * TX, LANES)
    args = (raw_rows, code_rows, raw_contact, raw_sheet, on_device(), sub)
    for f in range(FIELDS):
        for x in range(TX):
            for t in range(2):
                field_ref[f, FIRST + x, t] = own_row(*args, f, x, t)

    def both(x, t):
        free = [field_ref[FREE, FIRST + x + n, t] for n in range(2)]
        sheet = [field_ref[SHEET, FIRST + x + n, t] for n in range(2)]
        v = jnp.where(sub == 0, free[0], pltpu.roll(free[1], 1, 0))
        v = jnp.where(sub < 2, v, 1.0)
        return jnp.where(sub < 4, v, jnp.where(sub < 6, sheet[0], sheet[1]))

    for n in range(BULK + 1):
        for t in range(2):
            if n < BULK:
                f, x = LOW[n]
                low = field_ref[f, FIRST + x, t]
                high = field_ref[f, FIRST + HIGH[n][1], t]
            else:
                low, high = both(0, t), both(TX - 2, t)
            first_ref[2 * n + t] = jnp.where(even, high, low)
            second_ref[2 * n + t] = jnp.where(even, low, high)


def y_masks(lanes):
    gy = lax.axis_index("gy")
    has_right = gy < lax.axis_size("gy") - 1
    has_left = gy > 0
    right = {w: (lanes < w) & has_right for w in (2, 3)}
    left = {w: (lanes >= LANES - w) & has_left for w in (2, 3)}
    return left, right


def sides(first_ref, second_ref, axis):
    even = is_even(axis)
    first, second = first_ref[...], second_ref[...]
    return jnp.where(even, second, first), jnp.where(even, first, second)


def side_columns(before, after, f, x, masks):
    w = WIDTH[f]
    at = 16 * (x % 8) + SLOT[f]
    left, right = masks
    a = pltpu.roll(after[x // 8], (LANES - at) % LANES, 1)
    b = pltpu.roll(before[x // 8], (2 * LANES - at - w) % LANES, 1)
    return jnp.where(right[w], a, jnp.where(left[w], b, 0.0))


def corner_kernel(first_in, y_first, y_second, first_ref, second_ref):
    lanes = lane_index()
    gy = lax.axis_index("gy")
    before, after = sides(y_first, y_second, "gy")
    before = jnp.where(gy > 0, before, 0.0)
    after = jnp.where(gy < lax.axis_size("gy") - 1, after, 0.0)
    even = is_even("gx")
    packed = []
    for items in (LOW, HIGH):
        both = jnp.zeros((LAYERS, LANES), F32)
        for n, (f, x) in enumerate(items):
            w = WIDTH[f]
            at = 16 * (x % 8) + SLOT[f]
            middle = 8 * n + 3
            for src, start in ((before, middle - w), (after, middle)):
                here = (lanes >= start) & (lanes < start + w)
                by = (start - at) % LANES
                v = src[x // 8]
                both = jnp.where(here, pltpu.roll(v, by, 1) if by else v, both)
        packed.append(both)
    first_ref[SIDE] = jnp.where(even, packed[1], packed[0])
    second_ref[...] = jnp.where(even, packed[0], packed[1])


def newton_row(uref, fref, fields, dst, i):
    width = TILES * LANES
    sub = layer_index(width)
    u, e, h = wide(uref, 0, i), wide(fref, 1, i), wide(fref, 2, i)
    code = wide(fields, CODE, i)
    total = wide(uref, 0, i - 1) + wide(uref, 0, i + 1) + prev_lane(u) + next_lane(u)
    total = total + jnp.where(sub > 0, above(u), 0.0) + jnp.where(sub < LAYERS - 1, below(u), 0.0)
    weight = jnp.where((sub > 0) & (sub < LAYERS - 1), 6.0, 5.0)
    r = total - weight * u + 0.7 * (h - e + pick(code, DOPING))
    diag = weight + 0.7 * (jnp.abs(e) + jnp.abs(h))
    put(dst, 0, i, u + (0.8 * wide(fields, FREE, i)) * (r * recip(diag)))


def face(p, n):
    g = 0.5 * jnp.tanh(n[0] - p[0])
    a = (n[1] - p[1]) - (n[1] + p[1]) * g
    c = (n[2] - p[2]) + (n[2] + p[2]) * g
    return a, c, g


def x_face(uref, fref, i, tiles=TILES):
    p = (wide(uref, 0, i), wide(fref, 1, i), wide(fref, 2, i))
    n = (wide(uref, 0, i + 1), wide(fref, 1, i + 1), wide(fref, 2, i + 1))
    return face([cut(v, tiles) for v in p], [cut(v, tiles) for v in n])


def relax_row(uref, fref, fields, i, before, tiles=TILES):
    sub = layer_index(tiles * LANES)
    here = (wide(uref, 0, i), wide(fref, 1, i), wide(fref, 2, i))
    k = wide(fref, 3, i)
    after = (wide(uref, 0, i + 1), wide(fref, 1, i + 1), wide(fref, 2, i + 1))
    y_after = face(here, tuple(next_lane(v) for v in here))
    y_before = tuple(cut(prev_lane(v), tiles) for v in y_after)
    y_after = tuple(cut(v, tiles) for v in y_after)
    spread = cut(prev_lane(k), tiles) + cut(next_lane(k), tiles)
    here = tuple(cut(v, tiles) for v in here)
    k = cut(k, tiles)
    u, e, h = here
    after = face(here, tuple(cut(v, tiles) for v in after))
    l_after = face(here, tuple(below(v) for v in here))
    l_after = tuple(jnp.where(sub < LAYERS - 1, v, 0.0) for v in l_after)
    l_before = tuple(above(v) for v in l_after)
    net = [
        (after[n] - before[n]) + (y_after[n] - y_before[n]) + (l_after[n] - l_before[n])
        for n in range(3)
    ]
    square = [
        (after[n] * after[n] + before[n] * before[n])
        + (y_after[n] * y_after[n] + y_before[n] * y_before[n])
        + (l_after[n] * l_after[n] + l_before[n] * l_before[n])
        for n in range(2)
    ]
    inner = (sub > 0) & (sub < LAYERS - 1)
    weight = jnp.where(inner, 6.0, 5.0)
    spread = spread + cut(wide(fref, 3, i - 1), tiles) + cut(wide(fref, 3, i + 1), tiles)
    spread = spread + jnp.where(sub > 0, above(k), 0.0)
    spread = spread + jnp.where(sub < LAYERS - 1, below(k), 0.0) - weight * k
    code = cut(wide(fields, CODE, i), tiles)
    free = cut(wide(fields, FREE, i), tiles)
    power = pick(code, POWER_ELEC) * square[0] + pick(code, POWER_HOLE) * square[1]
    recombine = (e * h - 1.0) * recip(e * e + h * h + 2.0)
    step = 0.8 * free
    scale_e = step * recip(weight + net[2])
    scale_h = step * recip(weight - net[2])
    heat_step = free * jnp.where(inner, 0.8 / 3.5, 0.8 / 3.0)
    fixed = (
        e + scale_e * net[0],
        h + scale_h * net[1],
        k + heat_step * (0.5 * spread - 0.5 * k),
    )
    varying = (
        scale_e * recombine * pick(code, LOSS_ELEC),
        scale_h * recombine * pick(code, LOSS_HOLE),
        power,
    )
    return after, fixed, varying, heat_step


def relax_first(uref, fref, fields, dst, sheet_ref, i, before):
    after, fixed, varying, heat_step = relax_row(uref, fref, fields, i, before)
    s = wide(fields, SHEET, i)
    slow = jnp.exp(-0.6 * s)
    fast = jnp.exp(0.3 * s)
    q = varying[2] * slow
    put(dst, 1, i, fixed[0] - varying[0] * fast)
    put(dst, 2, i, fixed[1] - varying[1] * fast)
    put(dst, 3, i, fixed[2] + heat_step * (q + 0.5 * s))
    sheet_ref[pl.ds(i - 2, 1), :] = jnp.sum(q, axis=0, keepdims=True)
    return after


def thermal_row(
    src, anchor, fields, dst, i, halves=(0, 1), source=True, first=False, put_row=put
):
    width = TILES * LANES
    sub = layer_index(width)
    top = sub == 0
    cells = [wide(src, f, i) for f in range(4)]
    code = wide(fields, CODE, i)
    spread = jnp.where(top, pick(code, SPREAD_TOP), pick(code, SPREAD_IN))
    held = 0.9 - jnp.where(top, 5.0, 6.0) * spread
    spread = spread * wide(fields, FREE, i)
    if source:
        heat = jnp.where(top, pick(code, SOURCE_TOP) * wide(fields, SHEET, i), 0.0)
    out = []
    for s in halves:
        for t in range(2):
            f = 2 * s + t
            v = cells[f]
            if s == 0:
                total = wide(src, 2 + t, i - 1) + cells[2 + t]
            else:
                total = cells[t] + wide(src, t, i + 1)
            other = cells[2 * s + 1 - t]
            total = total + other + (prev_lane(other) if t == 0 else next_lane(other))
            total = total + jnp.where(sub > 0, above(v), 0.0)
            total = total + jnp.where(sub < LAYERS - 1, below(v), 0.0)
            value = spread * total + 0.1 * v
            value = value + held * (v if first else wide(anchor, f, i))
            if source:
                value = value + heat
            out.append(value)
            put_row(dst, f, i, value)
    return out


def top_mean(cells):
    total = (cells[0] + cells[1]) + (cells[2] + cells[3])
    return 0.25 * total[0:1, :]


def inner_kernel(field_in, y_first, y_second, field_ref, next_ref, mid_ref, sheet_ref):
    lanes = lane_index()
    masks = y_masks(lanes)
    before, after = sides(y_first, y_second, "gy")
    for x in range(TX):
        for f in range(FIELDS):
            field_ref[f, FIRST + x, 2] = side_columns(before, after, f, x, masks)

    @pl.when(on_device())
    def _():
        def newton(i, carry):
            newton_row(field_ref, field_ref, field_ref, mid_ref, i)
            return carry

        lax.fori_loop(FIRST + 1, FIRST + TX - 1, newton, 0, unroll=UNROLL_NEWTON)

        def relax(i, carry):
            return relax_first(mid_ref, field_ref, field_ref, next_ref, sheet_ref, i, carry)

        start = x_face(mid_ref, field_ref, FIRST + 1)
        lax.fori_loop(FIRST + 2, FIRST + TX - 2, relax, start, unroll=UNROLL_RELAX)

    @pl.when(jnp.logical_not(on_device()))
    def _():
        def one(i, carry):
            thermal_row(field_ref, field_ref, field_ref, mid_ref, i, first=True)
            return carry

        lax.fori_loop(FIRST + 1, FIRST + TX - 1, one, 0, unroll=UNROLL_HEAT)

        def two(i, carry):
            cells = thermal_row(mid_ref, field_ref, field_ref, next_ref, i)
            sheet_ref[pl.ds(i - FIRST, 1), :] = top_mean(cells)
            return carry

        lax.fori_loop(FIRST + 2, FIRST + TX - 2, two, 0, unroll=UNROLL_HEAT)


def rim_kernel(
    field_in, next_in, mid_in, sheet_in, x_first, x_second, side_second,
    field_ref, next_ref, mid_ref, sheet_ref,
):
    lanes = lane_index()
    sub = layer_index(LANES)
    gx = lax.axis_index("gx")
    has_up = gx > 0
    has_down = gx < lax.axis_size("gx") - 1
    edge = {w: (lanes < w) | (lanes >= LANES - w) for w in (2, 3)}
    up, down = sides(x_first.at[0:SIDE], x_second, "gx")
    up_side, down_side = sides(x_first.at[SIDE], side_second, "gx")
    for items, src, packed, ok, base in (
        (HIGH, up, up_side, has_up, FIRST - TX),
        (LOW, down, down_side, has_down, FIRST + TX),
    ):
        for n, (f, x) in enumerate(items):
            for t in range(2):
                second = x % 2
                if f < FREE:
                    v = src[2 * n + t]
                elif f == FREE:
                    top = src[2 * BULK + t][second : second + 1, :]
                    v = jnp.where(sub == 0, jnp.broadcast_to(top, (LAYERS, LANES)), 1.0)
                else:
                    row = src[2 * BULK + t][4 + 2 * second : 5 + 2 * second, :]
                    v = jnp.broadcast_to(row, (LAYERS, LANES))
                field_ref[f, base + x, t] = jnp.where(ok, v, 0.0)
            side = pltpu.roll(packed, LANES - 8 * n - 3, 1)
            field_ref[f, base + x, 2] = jnp.where(edge[WIDTH[f]] & ok, side, 0.0)

    @pl.when(on_device())
    def _():
        for n in range(3):
            for i in (FIRST - 2 + n, FIRST + TX - 1 + n):
                newton_row(field_ref, field_ref, field_ref, mid_ref, i)
        args = (mid_ref, field_ref, field_ref, next_ref, sheet_ref)
        one = x_face(mid_ref, field_ref, FIRST - 2)
        two = x_face(mid_ref, field_ref, FIRST + TX - 3)
        for n in range(3):
            one = relax_first(*args, FIRST - 1 + n, one)
            two = relax_first(*args, FIRST + TX - 2 + n, two)

    @pl.when(jnp.logical_not(on_device()))
    def _():
        args = (field_ref, field_ref, field_ref, mid_ref)
        thermal_row(*args, FIRST - 2, halves=(1,), first=True)
        thermal_row(*args, FIRST + TX + 1, halves=(0,), first=True)
        for i in (FIRST - 1, FIRST, FIRST + TX - 1, FIRST + TX):
            thermal_row(*args, i, first=True)
        for n in range(3):
            for i in (FIRST - 1 + n, FIRST + TX - 2 + n):
                cells = thermal_row(mid_ref, field_ref, field_ref, next_ref, i)
                if FIRST <= i < FIRST + TX:
                    sheet_ref[pl.ds(i - FIRST, 1), :] = top_mean(cells)


def second_kernel(
    field_ref, next_ref, first_ref, fixed_ref, varying_ref, source_ref, spread_ref, mid_ref
):
    fixed_rows = fixed_ref.reshape(2, 4, LAYERS * TX, LANES)
    varying_rows = varying_ref.reshape(2, 3, LAYERS * TX, LANES)

    def native(ref, f, i, value):
        for t in range(2):
            rows = pl.ds(i - FIRST, LAYERS, stride=TX)
            ref[t, f, rows, :] = value[:, t * LANES : (t + 1) * LANES]

    @pl.when(on_device())
    def _():
        def newton(i, carry):
            newton_row(first_ref, next_ref, field_ref, mid_ref, i)
            return carry

        lax.fori_loop(FIRST - 1, FIRST + TX + 1, newton, 0, unroll=UNROLL_NEWTON)

        def relax(i, before):
            after, fixed, varying, _ = relax_row(mid_ref, next_ref, field_ref, i, before, 2)
            for t in range(2):
                fixed_rows[t, 0, pl.ds(i - FIRST, LAYERS, stride=TX), :] = mid_ref[0, i, t]
            for n in range(3):
                native(fixed_rows, n + 1, i, fixed[n])
                native(varying_rows, n, i, varying[n])
            return after

        start = x_face(mid_ref, next_ref, FIRST - 1, 2)
        lax.fori_loop(FIRST, FIRST + TX, relax, start, unroll=UNROLL_RELAX)

    @pl.when(jnp.logical_not(on_device()))
    def _():
        args = (next_ref, next_ref, field_ref, mid_ref)
        thermal_row(*args, FIRST - 1, halves=(1,), source=False, first=True)
        thermal_row(*args, FIRST + TX, halves=(0,), source=False, first=True)

        def three(i, carry):
            thermal_row(*args, i, source=False, first=True)
            return carry

        lax.fori_loop(FIRST, FIRST + TX, three, 0, unroll=UNROLL_HEAT)

        def four(i, carry):
            def keep(ref, f, i, value):
                native(fixed_rows, f, i, value)

            thermal_row(mid_ref, next_ref, field_ref, None, i, source=False, put_row=keep)
            return carry

        lax.fori_loop(FIRST, FIRST + TX, four, 0, unroll=UNROLL_HEAT)

        def top(i, carry):
            code = jnp.concatenate([field_ref[CODE, i, t] for t in range(TILES)], axis=1)
            inside = wide(field_ref, FREE, i)[0:1, :]
            source_ref[pl.ds(i - FIRST + 1, 1), :] = pick(code[0:1, :], SOURCE_TOP) * inside
            return carry

        lax.fori_loop(FIRST - 1, FIRST + TX + 1, top, 0, unroll=3)

        def sides(i, carry):
            code = jnp.concatenate([field_ref[CODE, i, t] for t in range(2)], axis=1)
            spread_ref[0, pl.ds(i - FIRST, 1), :] = pick(code[0:1, :], SPREAD_TOP)
            spread_ref[1, pl.ds(i - FIRST, 1), :] = pick(code[1:2, :], SPREAD_IN)
            return carry

        lax.fori_loop(FIRST, FIRST + TX, sides, 0, unroll=4)


def last_kernel(
    sheet_ref, fixed_ref, varying_ref, source_ref, spread_ref, contacts,
    state_out, sheet_out, done, total_ref, delta, sem,
):
    def send(src, f, t, layers):
        dst = state_out.at[0, f, layers, :, pl.ds(t * LANES, LANES)]
        return pltpu.make_async_copy(src.at[t, f, layers], dst, sem.at[f, t])

    @pl.when(on_device())
    def _():
        every = pl.ds(0, LAYERS)
        copies = [send(fixed_ref, 0, t, every) for t in range(2)]
        for c in copies:
            c.start()
        for t in range(2):
            cols = slice(t * LANES, (t + 1) * LANES)
            s = sheet_ref[0:TX, cols]
            slow = jnp.exp(-0.6 * s)
            fast = jnp.exp(0.3 * s)
            total = jnp.zeros((TX, LANES), F32)
            for layer in range(LAYERS):
                for f in (1, 2):
                    done[t, f, layer] = (
                        fixed_ref[t, f, layer] - varying_ref[t, f - 1, layer] * fast
                    )
                q = varying_ref[t, 2, layer] * slow
                total = total + q
                step = 0.8 / 3.5 if 0 < layer < LAYERS - 1 else 0.8 / 3.0
                if layer == 0:
                    step = step * (1.0 - contacts[:, cols].astype(F32))
                done[t, 3, layer] = fixed_ref[t, 3, layer] + step * (q + 0.5 * s)
            total_ref[0, :, cols] = total
            for f in (1, 2, 3):
                copies.append(send(done, f, t, every))
                copies[-1].start()
        copies.append(pltpu.make_async_copy(total_ref, sheet_out, sem.at[8, 0]))
        copies[-1].start()
        for c in copies:
            c.wait()

    @pl.when(jnp.logical_not(on_device()))
    def _():
        rest = pl.ds(2, LAYERS - 2)
        copies = [send(fixed_ref, f, t, rest) for t in range(2) for f in range(4)]
        for c in copies:
            c.start()
        delta[...] = source_ref[...] * sheet_ref[...]
        middle = delta[1 : TX + 1, :]
        by_x = (delta[0:TX, :], delta[2 : TX + 2, :])
        by_y = (prev_lane(middle), next_lane(middle))
        more = []
        for t in range(2):
            cols = slice(t * LANES, (t + 1) * LANES)
            mid = middle[:, cols]
            total = jnp.zeros((TX, LANES), F32)
            for f in range(4):
                around = 2.0 * mid + by_x[f // 2][:, cols] + by_y[f % 2][:, cols]
                value = fixed_ref[t, f, 0] + 1.1 * mid + spread_ref[0, :, cols] * around
                done[t, f, 0] = value
                total = total + value
                done[t, f, 1] = fixed_ref[t, f, 1] + spread_ref[1, :, cols] * mid
                dst = state_out.at[0, f, pl.ds(0, 2), :, pl.ds(t * LANES, LANES)]
                more.append(
                    pltpu.make_async_copy(done.at[t, f, pl.ds(0, 2)], dst, sem.at[4 + f, t])
                )
                more[-1].start()
            total_ref[0, :, cols] = 0.25 * total
        more.append(pltpu.make_async_copy(total_ref, sheet_out, sem.at[8, 0]))
        more[-1].start()
        for c in copies + more:
            c.wait()


def per_device(grid_state, materials, contacts, received_sheets):
    nx, ny = lax.axis_size("gx"), lax.axis_size("gy")

    def swap(block, axis, parity):
        route = []
        for i in range(nx):
            for j in range(ny):
                at, count = (i, nx) if axis == "gx" else (j, ny)
                to = ((at - parity) ^ 1) + parity
                if axis == "gx":
                    p = (to, j) if 0 <= to < count else (i, j ^ 1)
                else:
                    p = (i, to) if 0 <= to < count else (i ^ 1, j)
                route.append((i * ny + j, p[0] * ny + p[1]))
        return lax.ppermute(block, ("gx", "gy"), route)

    tile = (LAYERS, LANES)
    field_shape = (FIELDS, ROWS, TILES) + tile
    state_shape = (4, ROWS, TILES) + tile
    y_shape = (2,) + tile
    inputs = (grid_state, materials, contacts, received_sheets)
    inputs = [pltpu.with_memory_space_constraint(v, pltpu.HBM) for v in inputs]
    raw_shapes = [
        (2, 4, LAYERS, TX, LANES),
        ((2, LAYERS, TX, LANES), jnp.int32),
        ((TX, 2 * LANES), jnp.int32),
        (1, TX, 2 * LANES),
    ]
    *raw, y_first, y_second = call(
        pack_kernel,
        raw_shapes + [y_shape, y_shape],
        inputs,
        specs=[HBM] * 4,
        scratch=[pltpu.SemaphoreType.DMA((12,))],
    )
    fields, x_first, x_second = call(rows_kernel, [field_shape, (SIDE + 1,) + tile, (SIDE,) + tile], raw)
    y_second = swap(y_second, "gy", 1)
    y_first = swap(y_first, "gy", 0)
    x_second = swap(x_second, "gx", 1)
    x_first, side_second = call(
        corner_kernel,
        [(SIDE + 1,) + tile, tile],
        [x_first, y_first, y_second],
        aliases={0: 0},
    )
    side_second = swap(side_second, "gx", 1)
    x_first = swap(x_first, "gx", 0)
    fields, following, middle, sheet = call(
        inner_kernel,
        [field_shape, state_shape, state_shape, SHEET_SHAPE],
        [fields, y_first, y_second],
        aliases={0: 0},
        cost=INNER,
    )
    fields, following, middle, sheet = call(
        rim_kernel,
        [field_shape, state_shape, state_shape, SHEET_SHAPE],
        [fields, following, middle, sheet, x_first, x_second, side_second],
        aliases={0: 0, 1: 1, 2: 2, 3: 3},
    )
    swapped = lax.ppermute(sheet, "half", [(0, 1), (1, 0)])
    fixed, varying, source, spread = call(
        second_kernel,
        [
            (2, 4, LAYERS, TX, LANES),
            (2, 3, LAYERS, TX, LANES),
            SHEET_SHAPE,
            (2, TX, 2 * LANES),
        ],
        [fields, following, middle],
        scratch=[pltpu.VMEM(state_shape, F32)],
        cost=1 << 23,
    )
    state, outgoing = call(
        last_kernel,
        [(1, 4, LAYERS, TX, 2 * LANES), (1, TX, 2 * LANES)],
        [swapped, fixed, varying, source, spread, contacts],
        out_specs=[HBM, HBM],
        scratch=[
            pltpu.VMEM((2, 4, LAYERS, TX, LANES), F32),
            pltpu.VMEM((1, TX, 2 * LANES), F32),
            pltpu.VMEM(SHEET_SHAPE, F32),
            pltpu.SemaphoreType.DMA((9, 2)),
        ],
    )
    return state, outgoing


def solution(mesh):
    placed = (
        P("half", None, None, "gx", "gy"),
        P("half", None, "gx", "gy"),
        P("gx", "gy"),
        P("half", "gx", "gy"),
    )
    return jax.shard_map(
        per_device,
        mesh=mesh,
        in_specs=placed,
        out_specs=(P("half", None, None, "gx", "gy"), P("half", "gx", "gy")),
        check_vma=False,
    )
```

```python
import jax
import jax.numpy as jnp
from jax import lax
from jax.experimental import pallas as pl
from jax.experimental.pallas import tpu as pltpu
from jax.sharding import PartitionSpec as P

F32 = jnp.float32
LAYERS = 8
TX = 16
LANES = 128
TILES = 3
HALO = 3
ROWS = TX + 2 * HALO
FIRST = HALO

DOPING = (1.5, -1.5, 0.6, -0.6)
MOB_ELEC = (1.0, 0.35, 0.7, 0.5)
MOB_HOLE = (0.4, 0.8, 0.3, 0.6)
CONDUCT = (1.0, 0.15, 2.5, 0.5)
CAPACITY = (0.6, 1.2, 0.4, 0.9)
POWER_ELEC = tuple(0.05 * m * m for m in MOB_ELEC)
POWER_HOLE = tuple(0.05 * m * m for m in MOB_HOLE)
LOSS_ELEC = tuple(0.3 / m for m in MOB_ELEC)
LOSS_HOLE = tuple(0.3 / m for m in MOB_HOLE)
SPREAD_TOP = tuple(0.9 * k / (5.0 * k + c) for k, c in zip(CONDUCT, CAPACITY))
SPREAD_IN = tuple(0.9 * k / (6.0 * k + c) for k, c in zip(CONDUCT, CAPACITY))
SOURCE_TOP = tuple(0.45 / (5.0 * k + c) for k, c in zip(CONDUCT, CAPACITY))

CODE, FREE, SHEET = 4, 5, 6
FIELDS = 7
WIDTH = (3, 2, 2, 2, 2, 2, 2)
SLOT = (0, 3, 5, 7, 9, 11, 13)
LOW = [(f, r) for f in range(FIELDS) for r in range(WIDTH[f])]
HIGH = [(f, TX - WIDTH[f] + r) for f in range(FIELDS) for r in range(WIDTH[f])]
BULK = sum(1 for f, _ in LOW if f < FREE)
VMEM = pl.BlockSpec(memory_space=pltpu.VMEM)
HBM = pl.BlockSpec(memory_space=pltpu.HBM)
SHEET_SHAPE = (24, TILES * LANES)
INNER = 10**10
UNROLL_NEWTON, UNROLL_RELAX, UNROLL_HEAT = 2, 4, 2


def call(kernel, outs, ins, specs=None, out_specs=None, scratch=(), aliases=None, cost=1 << 20):
    return pl.pallas_call(
        kernel,
        out_shape=[
            jax.ShapeDtypeStruct(*(s if isinstance(s[0], tuple) else (s, F32))) for s in outs
        ],
        in_specs=specs or [VMEM] * len(ins),
        out_specs=out_specs or [VMEM] * len(outs),
        scratch_shapes=list(scratch),
        input_output_aliases=aliases or {},
        compiler_params=pltpu.CompilerParams(vmem_limit_bytes=12 << 20),
        cost_estimate=pl.CostEstimate(flops=cost, bytes_accessed=1 << 20, transcendentals=0),
    )(*ins)


def lane_index():
    return lax.broadcasted_iota(jnp.int32, (LAYERS, LANES), 1)


def layer_index(width):
    return lax.broadcasted_iota(jnp.int32, (LAYERS, width), 0)


def pick(code, table):
    low = jnp.where(code < 0.5, table[0], table[1])
    high = jnp.where(code < 2.5, table[2], table[3])
    return jnp.where(code < 1.5, low, high)


def wide(ref, f, i):
    return jnp.concatenate([ref[f, i, t] for t in range(TILES)], axis=1)


def put(ref, f, i, value):
    for t in range(TILES):
        ref[f, i, t] = value[:, t * LANES : (t + 1) * LANES]


def cut(v, tiles):
    return v if v.shape[1] == tiles * LANES else v[:, : tiles * LANES]


def recip(v):
    r = pl.reciprocal(v, approx=True)
    return r * (2.0 - v * r)


def prev_lane(v):
    return pltpu.roll(v, 1, 1)


def next_lane(v):
    return pltpu.roll(v, v.shape[1] - 1, 1)


def above(v):
    return pltpu.roll(v, 1, 0)


def below(v):
    return pltpu.roll(v, LAYERS - 1, 0)


def on_device():
    return lax.axis_index("half") == 0


def is_even(axis):
    return lax.axis_index(axis) % 2 == 0


def own_row(raw_rows, code_rows, contact_ref, sheet_ref, device, sub, f, x, t):
    cols = slice(t * LANES, (t + 1) * LANES)
    if f < 4:
        return raw_rows[t, f, pl.ds(x, LAYERS, stride=TX), :]
    if f == CODE:
        return code_rows[t, pl.ds(x, LAYERS, stride=TX), :].astype(F32)
    if f == FREE:
        held = jnp.broadcast_to(contact_ref[x : x + 1, cols], (LAYERS, LANES))
        return jnp.where((held == 1) & (sub == 0) & device, 0.0, 1.0)
    return jnp.broadcast_to(sheet_ref[0, x : x + 1, cols], (LAYERS, LANES))


def pack_kernel(
    grid, codes, contacts, sheets, raw, raw_code, raw_contact, raw_sheet, first_ref, second_ref, sem
):
    small = [
        pltpu.make_async_copy(contacts, raw_contact, sem.at[10]),
        pltpu.make_async_copy(sheets, raw_sheet, sem.at[11]),
    ]
    copies = []
    for t in range(2):
        cols = pl.ds(t * LANES, LANES)
        copies.append(
            [
                pltpu.make_async_copy(grid.at[0, f, :, :, cols], raw.at[t, f], sem.at[5 * t + f])
                for f in range(4)
            ]
        )
        copies[t].append(
            pltpu.make_async_copy(codes.at[0, :, :, cols], raw_code.at[t], sem.at[5 * t + 4])
        )
    for c in copies[0] + small + copies[1]:
        c.start()
    lanes = lane_index()
    even = is_even("gy")
    raw_rows = raw.reshape(2, 4, LAYERS * TX, LANES)
    code_rows = raw_code.reshape(2, LAYERS * TX, LANES)
    args = (raw_rows, code_rows, raw_contact, raw_sheet, on_device(), layer_index(LANES))
    for c in small:
        c.wait()
    packed = []
    for t in range(2):
        for c in copies[t]:
            c.wait()
        for block in range(2):
            side = jnp.zeros((LAYERS, LANES), F32)
            for row in range(8):
                for f in range(FIELDS):
                    w = WIDTH[f]
                    at = 16 * row + SLOT[f]
                    here = (lanes >= at) & (lanes < at + w)
                    v = own_row(*args, f, 8 * block + row, t)
                    by = (at + t * w) % LANES
                    side = jnp.where(here, pltpu.roll(v, by, 1) if by else v, side)
            packed.append(side)
    for block in range(2):
        left, right = packed[block], packed[2 + block]
        first_ref[block] = jnp.where(even, right, left)
        second_ref[block] = jnp.where(even, left, right)


def rows_kernel(raw, raw_code, raw_contact, raw_sheet, field_ref, first_ref, second_ref):
    sub = layer_index(LANES)
    even = is_even("gx")
    raw_rows = raw.reshape(2, 4, LAYERS * TX, LANES)
    code_rows = raw_code.reshape(2, LAYERS * TX, LANES)
    args = (raw_rows, code_rows, raw_contact, raw_sheet, on_device(), sub)
    for f in range(FIELDS):
        for x in range(TX):
            for t in range(2):
                field_ref[f, FIRST + x, t] = own_row(*args, f, x, t)

    def both(x, t):
        free = [field_ref[FREE, FIRST + x + n, t] for n in range(2)]
        sheet = [field_ref[SHEET, FIRST + x + n, t] for n in range(2)]
        v = jnp.where(sub == 0, free[0], pltpu.roll(free[1], 1, 0))
        v = jnp.where(sub < 2, v, 1.0)
        return jnp.where(sub < 4, v, jnp.where(sub < 6, sheet[0], sheet[1]))

    for n in range(BULK + 1):
        for t in range(2):
            if n < BULK:
                f, x = LOW[n]
                low = field_ref[f, FIRST + x, t]
                high = field_ref[f, FIRST + HIGH[n][1], t]
            else:
                low, high = both(0, t), both(TX - 2, t)
            first_ref[2 * n + t] = jnp.where(even, high, low)
            second_ref[2 * n + t] = jnp.where(even, low, high)


def y_masks(lanes):
    gy = lax.axis_index("gy")
    has_right = gy < lax.axis_size("gy") - 1
    has_left = gy > 0
    right = {w: (lanes < w) & has_right for w in (2, 3)}
    left = {w: (lanes >= LANES - w) & has_left for w in (2, 3)}
    return left, right


def sides(first_ref, second_ref, axis):
    even = is_even(axis)
    first, second = first_ref[...], second_ref[...]
    return jnp.where(even, second, first), jnp.where(even, first, second)


def side_columns(before, after, f, x, masks):
    w = WIDTH[f]
    at = 16 * (x % 8) + SLOT[f]
    left, right = masks
    a = pltpu.roll(after[x // 8], (LANES - at) % LANES, 1)
    b = pltpu.roll(before[x // 8], (2 * LANES - at - w) % LANES, 1)
    return jnp.where(right[w], a, jnp.where(left[w], b, 0.0))


def corner_kernel(y_first, y_second, first_ref, second_ref):
    lanes = lane_index()
    gy = lax.axis_index("gy")
    before, after = sides(y_first, y_second, "gy")
    before = jnp.where(gy > 0, before, 0.0)
    after = jnp.where(gy < lax.axis_size("gy") - 1, after, 0.0)
    even = is_even("gx")
    packed = []
    for items in (LOW, HIGH):
        both = jnp.zeros((LAYERS, LANES), F32)
        for n, (f, x) in enumerate(items):
            w = WIDTH[f]
            at = 16 * (x % 8) + SLOT[f]
            middle = 8 * n + 3
            for src, start in ((before, middle - w), (after, middle)):
                here = (lanes >= start) & (lanes < start + w)
                by = (start - at) % LANES
                v = src[x // 8]
                both = jnp.where(here, pltpu.roll(v, by, 1) if by else v, both)
        packed.append(both)
    first_ref[...] = jnp.where(even, packed[1], packed[0])
    second_ref[...] = jnp.where(even, packed[0], packed[1])


def newton_row(uref, fref, fields, dst, i):
    width = TILES * LANES
    sub = layer_index(width)
    u, e, h = wide(uref, 0, i), wide(fref, 1, i), wide(fref, 2, i)
    code = wide(fields, CODE, i)
    total = wide(uref, 0, i - 1) + wide(uref, 0, i + 1) + prev_lane(u) + next_lane(u)
    total = total + jnp.where(sub > 0, above(u), 0.0) + jnp.where(sub < LAYERS - 1, below(u), 0.0)
    weight = jnp.where((sub > 0) & (sub < LAYERS - 1), 6.0, 5.0)
    r = total - weight * u + 0.7 * (h - e + pick(code, DOPING))
    diag = weight + 0.7 * (jnp.abs(e) + jnp.abs(h))
    put(dst, 0, i, u + (0.8 * wide(fields, FREE, i)) * (r * recip(diag)))


def face(p, n):
    g = 0.5 * jnp.tanh(n[0] - p[0])
    a = (n[1] - p[1]) - (n[1] + p[1]) * g
    c = (n[2] - p[2]) + (n[2] + p[2]) * g
    return a, c, g


def x_face(uref, fref, i, tiles=TILES):
    p = (wide(uref, 0, i), wide(fref, 1, i), wide(fref, 2, i))
    n = (wide(uref, 0, i + 1), wide(fref, 1, i + 1), wide(fref, 2, i + 1))
    return face([cut(v, tiles) for v in p], [cut(v, tiles) for v in n])


def relax_row(uref, fref, fields, i, before, tiles=TILES):
    sub = layer_index(tiles * LANES)
    here = (wide(uref, 0, i), wide(fref, 1, i), wide(fref, 2, i))
    k = wide(fref, 3, i)
    after = (wide(uref, 0, i + 1), wide(fref, 1, i + 1), wide(fref, 2, i + 1))
    y_after = face(here, tuple(next_lane(v) for v in here))
    y_before = tuple(cut(prev_lane(v), tiles) for v in y_after)
    y_after = tuple(cut(v, tiles) for v in y_after)
    spread = cut(prev_lane(k), tiles) + cut(next_lane(k), tiles)
    here = tuple(cut(v, tiles) for v in here)
    k = cut(k, tiles)
    u, e, h = here
    after = face(here, tuple(cut(v, tiles) for v in after))
    l_after = face(here, tuple(below(v) for v in here))
    l_after = tuple(jnp.where(sub < LAYERS - 1, v, 0.0) for v in l_after)
    l_before = tuple(above(v) for v in l_after)
    net = [
        (after[n] - before[n]) + (y_after[n] - y_before[n]) + (l_after[n] - l_before[n])
        for n in range(3)
    ]
    square = [
        (after[n] * after[n] + before[n] * before[n])
        + (y_after[n] * y_after[n] + y_before[n] * y_before[n])
        + (l_after[n] * l_after[n] + l_before[n] * l_before[n])
        for n in range(2)
    ]
    inner = (sub > 0) & (sub < LAYERS - 1)
    weight = jnp.where(inner, 6.0, 5.0)
    spread = spread + cut(wide(fref, 3, i - 1), tiles) + cut(wide(fref, 3, i + 1), tiles)
    spread = spread + jnp.where(sub > 0, above(k), 0.0)
    spread = spread + jnp.where(sub < LAYERS - 1, below(k), 0.0) - weight * k
    code = cut(wide(fields, CODE, i), tiles)
    free = cut(wide(fields, FREE, i), tiles)
    power = pick(code, POWER_ELEC) * square[0] + pick(code, POWER_HOLE) * square[1]
    recombine = (e * h - 1.0) * recip(e * e + h * h + 2.0)
    step = 0.8 * free
    scale_e = step * recip(weight + net[2])
    scale_h = step * recip(weight - net[2])
    heat_step = free * jnp.where(inner, 0.8 / 3.5, 0.8 / 3.0)
    fixed = (
        e + scale_e * net[0],
        h + scale_h * net[1],
        k + heat_step * (0.5 * spread - 0.5 * k),
    )
    varying = (
        scale_e * recombine * pick(code, LOSS_ELEC),
        scale_h * recombine * pick(code, LOSS_HOLE),
        power,
    )
    return after, fixed, varying, heat_step


def relax_first(uref, fref, fields, dst, sheet_ref, i, before):
    after, fixed, varying, heat_step = relax_row(uref, fref, fields, i, before)
    s = wide(fields, SHEET, i)
    slow = jnp.exp(-0.6 * s)
    fast = jnp.exp(0.3 * s)
    q = varying[2] * slow
    put(dst, 1, i, fixed[0] - varying[0] * fast)
    put(dst, 2, i, fixed[1] - varying[1] * fast)
    put(dst, 3, i, fixed[2] + heat_step * (q + 0.5 * s))
    sheet_ref[pl.ds(i - 2, 1), :] = jnp.sum(q, axis=0, keepdims=True)
    return after


def thermal_row(
    src, anchor, fields, dst, i, halves=(0, 1), source=True, first=False, put_row=put
):
    width = TILES * LANES
    sub = layer_index(width)
    top = sub == 0
    cells = [wide(src, f, i) for f in range(4)]
    code = wide(fields, CODE, i)
    spread = jnp.where(top, pick(code, SPREAD_TOP), pick(code, SPREAD_IN))
    held = 0.9 - jnp.where(top, 5.0, 6.0) * spread
    spread = spread * wide(fields, FREE, i)
    if source:
        heat = jnp.where(top, pick(code, SOURCE_TOP) * wide(fields, SHEET, i), 0.0)
    out = []
    for s in halves:
        for t in range(2):
            f = 2 * s + t
            v = cells[f]
            if s == 0:
                total = wide(src, 2 + t, i - 1) + cells[2 + t]
            else:
                total = cells[t] + wide(src, t, i + 1)
            other = cells[2 * s + 1 - t]
            total = total + other + (prev_lane(other) if t == 0 else next_lane(other))
            total = total + jnp.where(sub > 0, above(v), 0.0)
            total = total + jnp.where(sub < LAYERS - 1, below(v), 0.0)
            value = spread * total + 0.1 * v
            value = value + held * (v if first else wide(anchor, f, i))
            if source:
                value = value + heat
            out.append(value)
            put_row(dst, f, i, value)
    return out


def top_mean(cells):
    total = (cells[0] + cells[1]) + (cells[2] + cells[3])
    return 0.25 * total[0:1, :]


def inner_kernel(field_in, y_first, y_second, field_ref, next_ref, mid_ref, sheet_ref):
    lanes = lane_index()
    masks = y_masks(lanes)
    before, after = sides(y_first, y_second, "gy")
    for x in range(TX):
        for f in range(FIELDS):
            field_ref[f, FIRST + x, 2] = side_columns(before, after, f, x, masks)

    @pl.when(on_device())
    def _():
        def newton(i, carry):
            newton_row(field_ref, field_ref, field_ref, mid_ref, i)
            return carry

        lax.fori_loop(FIRST + 1, FIRST + TX - 1, newton, 0, unroll=UNROLL_NEWTON)

        def relax(i, carry):
            return relax_first(mid_ref, field_ref, field_ref, next_ref, sheet_ref, i, carry)

        start = x_face(mid_ref, field_ref, FIRST + 1)
        lax.fori_loop(FIRST + 2, FIRST + TX - 2, relax, start, unroll=UNROLL_RELAX)

    @pl.when(jnp.logical_not(on_device()))
    def _():
        def one(i, carry):
            thermal_row(field_ref, field_ref, field_ref, mid_ref, i, first=True)
            return carry

        lax.fori_loop(FIRST + 1, FIRST + TX - 1, one, 0, unroll=UNROLL_HEAT)

        def two(i, carry):
            cells = thermal_row(mid_ref, field_ref, field_ref, next_ref, i)
            sheet_ref[pl.ds(i - FIRST, 1), :] = top_mean(cells)
            return carry

        lax.fori_loop(FIRST + 2, FIRST + TX - 2, two, 0, unroll=UNROLL_HEAT)


def rim_kernel(
    field_in, next_in, mid_in, sheet_in, x_first, x_second, side_second, side_first,
    field_ref, next_ref, mid_ref, sheet_ref,
):
    lanes = lane_index()
    sub = layer_index(LANES)
    gx = lax.axis_index("gx")
    has_up = gx > 0
    has_down = gx < lax.axis_size("gx") - 1
    edge = {w: (lanes < w) | (lanes >= LANES - w) for w in (2, 3)}
    up, down = sides(x_first, x_second, "gx")
    up_side, down_side = sides(side_first, side_second, "gx")
    for items, src, packed, ok, base in (
        (HIGH, up, up_side, has_up, FIRST - TX),
        (LOW, down, down_side, has_down, FIRST + TX),
    ):
        for n, (f, x) in enumerate(items):
            for t in range(2):
                second = x % 2
                if f < FREE:
                    v = src[2 * n + t]
                elif f == FREE:
                    top = src[2 * BULK + t][second : second + 1, :]
                    v = jnp.where(sub == 0, jnp.broadcast_to(top, (LAYERS, LANES)), 1.0)
                else:
                    row = src[2 * BULK + t][4 + 2 * second : 5 + 2 * second, :]
                    v = jnp.broadcast_to(row, (LAYERS, LANES))
                field_ref[f, base + x, t] = jnp.where(ok, v, 0.0)
            side = pltpu.roll(packed, LANES - 8 * n - 3, 1)
            field_ref[f, base + x, 2] = jnp.where(edge[WIDTH[f]] & ok, side, 0.0)

    @pl.when(on_device())
    def _():
        for n in range(3):
            for i in (FIRST - 2 + n, FIRST + TX - 1 + n):
                newton_row(field_ref, field_ref, field_ref, mid_ref, i)
        args = (mid_ref, field_ref, field_ref, next_ref, sheet_ref)
        one = x_face(mid_ref, field_ref, FIRST - 2)
        two = x_face(mid_ref, field_ref, FIRST + TX - 3)
        for n in range(3):
            one = relax_first(*args, FIRST - 1 + n, one)
            two = relax_first(*args, FIRST + TX - 2 + n, two)

    @pl.when(jnp.logical_not(on_device()))
    def _():
        args = (field_ref, field_ref, field_ref, mid_ref)
        thermal_row(*args, FIRST - 2, halves=(1,), first=True)
        thermal_row(*args, FIRST + TX + 1, halves=(0,), first=True)
        for i in (FIRST - 1, FIRST, FIRST + TX - 1, FIRST + TX):
            thermal_row(*args, i, first=True)
        for n in range(3):
            for i in (FIRST - 1 + n, FIRST + TX - 2 + n):
                cells = thermal_row(mid_ref, field_ref, field_ref, next_ref, i)
                if FIRST <= i < FIRST + TX:
                    sheet_ref[pl.ds(i - FIRST, 1), :] = top_mean(cells)


def second_kernel(
    field_ref, next_ref, first_ref, fixed_ref, varying_ref, source_ref, spread_ref, mid_ref
):
    fixed_rows = fixed_ref.reshape(2, 4, LAYERS * TX, LANES)
    varying_rows = varying_ref.reshape(2, 3, LAYERS * TX, LANES)

    def native(ref, f, i, value):
        for t in range(2):
            rows = pl.ds(i - FIRST, LAYERS, stride=TX)
            ref[t, f, rows, :] = value[:, t * LANES : (t + 1) * LANES]

    @pl.when(on_device())
    def _():
        def newton(i, carry):
            newton_row(first_ref, next_ref, field_ref, mid_ref, i)
            return carry

        lax.fori_loop(FIRST - 1, FIRST + TX + 1, newton, 0, unroll=UNROLL_NEWTON)

        def relax(i, before):
            after, fixed, varying, _ = relax_row(mid_ref, next_ref, field_ref, i, before, 2)
            for t in range(2):
                fixed_rows[t, 0, pl.ds(i - FIRST, LAYERS, stride=TX), :] = mid_ref[0, i, t]
            for n in range(3):
                native(fixed_rows, n + 1, i, fixed[n])
                native(varying_rows, n, i, varying[n])
            return after

        start = x_face(mid_ref, next_ref, FIRST - 1, 2)
        lax.fori_loop(FIRST, FIRST + TX, relax, start, unroll=UNROLL_RELAX)

    @pl.when(jnp.logical_not(on_device()))
    def _():
        args = (next_ref, next_ref, field_ref, mid_ref)
        thermal_row(*args, FIRST - 1, halves=(1,), source=False, first=True)
        thermal_row(*args, FIRST + TX, halves=(0,), source=False, first=True)

        def three(i, carry):
            thermal_row(*args, i, source=False, first=True)
            return carry

        lax.fori_loop(FIRST, FIRST + TX, three, 0, unroll=UNROLL_HEAT)

        def four(i, carry):
            def keep(ref, f, i, value):
                native(fixed_rows, f, i, value)

            thermal_row(mid_ref, next_ref, field_ref, None, i, source=False, put_row=keep)
            return carry

        lax.fori_loop(FIRST, FIRST + TX, four, 0, unroll=UNROLL_HEAT)

        def top(i, carry):
            code = jnp.concatenate([field_ref[CODE, i, t] for t in range(TILES)], axis=1)
            inside = wide(field_ref, FREE, i)[0:1, :]
            source_ref[pl.ds(i - FIRST + 1, 1), :] = pick(code[0:1, :], SOURCE_TOP) * inside
            return carry

        lax.fori_loop(FIRST - 1, FIRST + TX + 1, top, 0, unroll=3)

        def sides(i, carry):
            code = jnp.concatenate([field_ref[CODE, i, t] for t in range(2)], axis=1)
            spread_ref[0, pl.ds(i - FIRST, 1), :] = pick(code[0:1, :], SPREAD_TOP)
            spread_ref[1, pl.ds(i - FIRST, 1), :] = pick(code[1:2, :], SPREAD_IN)
            return carry

        lax.fori_loop(FIRST, FIRST + TX, sides, 0, unroll=4)


def last_kernel(
    sheet_ref, fixed_ref, varying_ref, source_ref, spread_ref, contacts,
    state_out, sheet_out, done, total_ref, delta, sem,
):
    def send(src, f, t, layers):
        dst = state_out.at[0, f, layers, :, pl.ds(t * LANES, LANES)]
        return pltpu.make_async_copy(src.at[t, f, layers], dst, sem.at[f, t])

    @pl.when(on_device())
    def _():
        every = pl.ds(0, LAYERS)
        copies = [send(fixed_ref, 0, t, every) for t in range(2)]
        for c in copies:
            c.start()
        for t in range(2):
            cols = slice(t * LANES, (t + 1) * LANES)
            s = sheet_ref[0:TX, cols]
            slow = jnp.exp(-0.6 * s)
            fast = jnp.exp(0.3 * s)
            total = jnp.zeros((TX, LANES), F32)
            for layer in range(LAYERS):
                for f in (1, 2):
                    done[t, f, layer] = (
                        fixed_ref[t, f, layer] - varying_ref[t, f - 1, layer] * fast
                    )
                q = varying_ref[t, 2, layer] * slow
                total = total + q
                step = 0.8 / 3.5 if 0 < layer < LAYERS - 1 else 0.8 / 3.0
                if layer == 0:
                    step = step * (1.0 - contacts[:, cols].astype(F32))
                done[t, 3, layer] = fixed_ref[t, 3, layer] + step * (q + 0.5 * s)
            total_ref[0, :, cols] = total
            for f in (1, 2, 3):
                copies.append(send(done, f, t, every))
                copies[-1].start()
        copies.append(pltpu.make_async_copy(total_ref, sheet_out, sem.at[8, 0]))
        copies[-1].start()
        for c in copies:
            c.wait()

    @pl.when(jnp.logical_not(on_device()))
    def _():
        rest = pl.ds(2, LAYERS - 2)
        copies = [send(fixed_ref, f, t, rest) for t in range(2) for f in range(4)]
        for c in copies:
            c.start()
        delta[...] = source_ref[...] * sheet_ref[...]
        middle = delta[1 : TX + 1, :]
        by_x = (delta[0:TX, :], delta[2 : TX + 2, :])
        by_y = (prev_lane(middle), next_lane(middle))
        more = []
        for t in range(2):
            cols = slice(t * LANES, (t + 1) * LANES)
            mid = middle[:, cols]
            total = jnp.zeros((TX, LANES), F32)
            for f in range(4):
                around = 2.0 * mid + by_x[f // 2][:, cols] + by_y[f % 2][:, cols]
                value = fixed_ref[t, f, 0] + 1.1 * mid + spread_ref[0, :, cols] * around
                done[t, f, 0] = value
                total = total + value
                done[t, f, 1] = fixed_ref[t, f, 1] + spread_ref[1, :, cols] * mid
                dst = state_out.at[0, f, pl.ds(0, 2), :, pl.ds(t * LANES, LANES)]
                more.append(
                    pltpu.make_async_copy(done.at[t, f, pl.ds(0, 2)], dst, sem.at[4 + f, t])
                )
                more[-1].start()
            total_ref[0, :, cols] = 0.25 * total
        more.append(pltpu.make_async_copy(total_ref, sheet_out, sem.at[8, 0]))
        more[-1].start()
        for c in copies + more:
            c.wait()


def per_device(grid_state, materials, contacts, received_sheets):
    nx, ny = lax.axis_size("gx"), lax.axis_size("gy")

    def swap(block, axis, parity):
        route = []
        for i in range(nx):
            for j in range(ny):
                at, count = (i, nx) if axis == "gx" else (j, ny)
                to = ((at - parity) ^ 1) + parity
                if axis == "gx":
                    p = (to, j) if 0 <= to < count else (i, j ^ 1)
                else:
                    p = (i, to) if 0 <= to < count else (i ^ 1, j)
                route.append((i * ny + j, p[0] * ny + p[1]))
        return lax.ppermute(block, ("gx", "gy"), route)

    tile = (LAYERS, LANES)
    field_shape = (FIELDS, ROWS, TILES) + tile
    state_shape = (4, ROWS, TILES) + tile
    y_shape, x_shape = (2,) + tile, (2 * BULK + 2,) + tile
    inputs = (grid_state, materials, contacts, received_sheets)
    inputs = [pltpu.with_memory_space_constraint(v, pltpu.HBM) for v in inputs]
    raw_shapes = [
        (2, 4, LAYERS, TX, LANES),
        ((2, LAYERS, TX, LANES), jnp.int32),
        ((TX, 2 * LANES), jnp.int32),
        (1, TX, 2 * LANES),
    ]
    *raw, y_first, y_second = call(
        pack_kernel,
        raw_shapes + [y_shape, y_shape],
        inputs,
        specs=[HBM] * 4,
        scratch=[pltpu.SemaphoreType.DMA((12,))],
    )
    fields, x_first, x_second = call(rows_kernel, [field_shape, x_shape, x_shape], raw)
    y_second = swap(y_second, "gy", 1)
    y_first = swap(y_first, "gy", 0)
    x_second = swap(x_second, "gx", 1)
    x_first = swap(x_first, "gx", 0)
    side_first, side_second = call(corner_kernel, [tile, tile], [y_first, y_second])
    side_second = swap(side_second, "gx", 1)
    side_first = swap(side_first, "gx", 0)
    fields, following, middle, sheet = call(
        inner_kernel,
        [field_shape, state_shape, state_shape, SHEET_SHAPE],
        [fields, y_first, y_second],
        aliases={0: 0},
        cost=INNER,
    )
    fields, following, middle, sheet = call(
        rim_kernel,
        [field_shape, state_shape, state_shape, SHEET_SHAPE],
        [fields, following, middle, sheet, x_first, x_second, side_second, side_first],
        aliases={0: 0, 1: 1, 2: 2, 3: 3},
    )
    swapped = lax.ppermute(sheet, "half", [(0, 1), (1, 0)])
    fixed, varying, source, spread = call(
        second_kernel,
        [
            (2, 4, LAYERS, TX, LANES),
            (2, 3, LAYERS, TX, LANES),
            SHEET_SHAPE,
            (2, TX, 2 * LANES),
        ],
        [fields, following, middle],
        scratch=[pltpu.VMEM(state_shape, F32)],
        cost=1 << 23,
    )
    state, outgoing = call(
        last_kernel,
        [(1, 4, LAYERS, TX, 2 * LANES), (1, TX, 2 * LANES)],
        [swapped, fixed, varying, source, spread, contacts],
        out_specs=[HBM, HBM],
        scratch=[
            pltpu.VMEM((2, 4, LAYERS, TX, LANES), F32),
            pltpu.VMEM((1, TX, 2 * LANES), F32),
            pltpu.VMEM(SHEET_SHAPE, F32),
            pltpu.SemaphoreType.DMA((9, 2)),
        ],
    )
    return state, outgoing


def solution(mesh):
    placed = (
        P("half", None, None, "gx", "gy"),
        P("half", None, "gx", "gy"),
        P("gx", "gy"),
        P("half", "gx", "gy"),
    )
    return jax.shard_map(
        per_device,
        mesh=mesh,
        in_specs=placed,
        out_specs=(P("half", None, None, "gx", "gy"), P("half", "gx", "gy")),
        check_vma=False,
    )
```

```python
import jax
import jax.numpy as jnp
from jax import lax
from jax.experimental import pallas as pl
from jax.experimental.pallas import tpu as pltpu
from jax.sharding import PartitionSpec as P

F32 = jnp.float32
LAYERS = 8
TX = 16
LANES = 128
TILES = 3
HALO = 3
ROWS = TX + 2 * HALO
FIRST = HALO

DOPING = (1.5, -1.5, 0.6, -0.6)
MOB_ELEC = (1.0, 0.35, 0.7, 0.5)
MOB_HOLE = (0.4, 0.8, 0.3, 0.6)
CONDUCT = (1.0, 0.15, 2.5, 0.5)
CAPACITY = (0.6, 1.2, 0.4, 0.9)
POWER_ELEC = tuple(0.05 * m * m for m in MOB_ELEC)
POWER_HOLE = tuple(0.05 * m * m for m in MOB_HOLE)
LOSS_ELEC = tuple(0.3 / m for m in MOB_ELEC)
LOSS_HOLE = tuple(0.3 / m for m in MOB_HOLE)
SPREAD_TOP = tuple(0.9 * k / (5.0 * k + c) for k, c in zip(CONDUCT, CAPACITY))
SPREAD_IN = tuple(0.9 * k / (6.0 * k + c) for k, c in zip(CONDUCT, CAPACITY))
SOURCE_TOP = tuple(0.45 / (5.0 * k + c) for k, c in zip(CONDUCT, CAPACITY))

CODE, FREE, SHEET = 4, 5, 6
FIELDS = 7
WIDTH = (3, 2, 2, 2, 2, 2, 2)
SLOT = (0, 3, 5, 7, 9, 11, 13)
LOW = [(f, r) for f in range(FIELDS) for r in range(WIDTH[f])]
HIGH = [(f, TX - WIDTH[f] + r) for f in range(FIELDS) for r in range(WIDTH[f])]
BULK = sum(1 for f, _ in LOW if f < FREE)
VMEM = pl.BlockSpec(memory_space=pltpu.VMEM)
HBM = pl.BlockSpec(memory_space=pltpu.HBM)
SHEET_SHAPE = (24, TILES * LANES)
INNER = 10**10
UNROLL_NEWTON, UNROLL_RELAX, UNROLL_HEAT = 2, 4, 2


def call(kernel, outs, ins, specs=None, out_specs=None, scratch=(), aliases=None, cost=1 << 20):
    return pl.pallas_call(
        kernel,
        out_shape=[
            jax.ShapeDtypeStruct(*(s if isinstance(s[0], tuple) else (s, F32))) for s in outs
        ],
        in_specs=specs or [VMEM] * len(ins),
        out_specs=out_specs or [VMEM] * len(outs),
        scratch_shapes=list(scratch),
        input_output_aliases=aliases or {},
        compiler_params=pltpu.CompilerParams(vmem_limit_bytes=12 << 20),
        cost_estimate=pl.CostEstimate(flops=cost, bytes_accessed=1 << 20, transcendentals=0),
    )(*ins)


def lane_index():
    return lax.broadcasted_iota(jnp.int32, (LAYERS, LANES), 1)


def layer_index(width):
    return lax.broadcasted_iota(jnp.int32, (LAYERS, width), 0)


def pick(code, table):
    low = jnp.where(code < 0.5, table[0], table[1])
    high = jnp.where(code < 2.5, table[2], table[3])
    return jnp.where(code < 1.5, low, high)


def wide(ref, f, i):
    return jnp.concatenate([ref[f, i, t] for t in range(TILES)], axis=1)


def put(ref, f, i, value):
    for t in range(TILES):
        ref[f, i, t] = value[:, t * LANES : (t + 1) * LANES]


def cut(v, tiles):
    return v if v.shape[1] == tiles * LANES else v[:, : tiles * LANES]


def recip(v):
    r = pl.reciprocal(v, approx=True)
    return r * (2.0 - v * r)


def prev_lane(v):
    return pltpu.roll(v, 1, 1)


def next_lane(v):
    return pltpu.roll(v, v.shape[1] - 1, 1)


def above(v):
    return pltpu.roll(v, 1, 0)


def below(v):
    return pltpu.roll(v, LAYERS - 1, 0)


def on_device():
    return lax.axis_index("half") == 0


def is_even(axis):
    return lax.axis_index(axis) % 2 == 0


def own_row(raw_rows, code_rows, contact_ref, sheet_ref, device, sub, f, x, t):
    cols = slice(t * LANES, (t + 1) * LANES)
    if f < 4:
        return raw_rows[t, f, pl.ds(x, LAYERS, stride=TX), :]
    if f == CODE:
        return code_rows[t, pl.ds(x, LAYERS, stride=TX), :].astype(F32)
    if f == FREE:
        held = jnp.broadcast_to(contact_ref[x : x + 1, cols], (LAYERS, LANES))
        return jnp.where((held == 1) & (sub == 0) & device, 0.0, 1.0)
    return jnp.broadcast_to(sheet_ref[0, x : x + 1, cols], (LAYERS, LANES))


def pack_kernel(
    grid, codes, contacts, sheets, raw, raw_code, raw_contact, raw_sheet, first_ref, second_ref, sem
):
    small = [
        pltpu.make_async_copy(contacts, raw_contact, sem.at[10]),
        pltpu.make_async_copy(sheets, raw_sheet, sem.at[11]),
    ]
    copies = []
    for t in range(2):
        cols = pl.ds(t * LANES, LANES)
        copies.append(
            [
                pltpu.make_async_copy(grid.at[0, f, :, :, cols], raw.at[t, f], sem.at[5 * t + f])
                for f in range(4)
            ]
        )
        copies[t].append(
            pltpu.make_async_copy(codes.at[0, :, :, cols], raw_code.at[t], sem.at[5 * t + 4])
        )
    for c in copies[0] + small + copies[1]:
        c.start()
    lanes = lane_index()
    even = is_even("gy")
    raw_rows = raw.reshape(2, 4, LAYERS * TX, LANES)
    code_rows = raw_code.reshape(2, LAYERS * TX, LANES)
    args = (raw_rows, code_rows, raw_contact, raw_sheet, on_device(), layer_index(LANES))
    for c in small:
        c.wait()
    packed = []
    for t in range(2):
        for c in copies[t]:
            c.wait()
        for block in range(2):
            side = jnp.zeros((LAYERS, LANES), F32)
            for row in range(8):
                for f in range(FIELDS):
                    w = WIDTH[f]
                    at = 16 * row + SLOT[f]
                    here = (lanes >= at) & (lanes < at + w)
                    v = own_row(*args, f, 8 * block + row, t)
                    by = (at + t * w) % LANES
                    side = jnp.where(here, pltpu.roll(v, by, 1) if by else v, side)
            packed.append(side)
    for block in range(2):
        left, right = packed[block], packed[2 + block]
        first_ref[block] = jnp.where(even, right, left)
        second_ref[block] = jnp.where(even, left, right)


def rows_kernel(raw, raw_code, raw_contact, raw_sheet, field_ref, first_ref, second_ref):
    sub = layer_index(LANES)
    even = is_even("gx")
    raw_rows = raw.reshape(2, 4, LAYERS * TX, LANES)
    code_rows = raw_code.reshape(2, LAYERS * TX, LANES)
    args = (raw_rows, code_rows, raw_contact, raw_sheet, on_device(), sub)
    for f in range(FIELDS):
        for x in range(TX):
            for t in range(2):
                field_ref[f, FIRST + x, t] = own_row(*args, f, x, t)

    def both(x, t):
        free = [field_ref[FREE, FIRST + x + n, t] for n in range(2)]
        sheet = [field_ref[SHEET, FIRST + x + n, t] for n in range(2)]
        v = jnp.where(sub == 0, free[0], pltpu.roll(free[1], 1, 0))
        v = jnp.where(sub < 2, v, 1.0)
        return jnp.where(sub < 4, v, jnp.where(sub < 6, sheet[0], sheet[1]))

    for n in range(BULK + 1):
        for t in range(2):
            if n < BULK:
                f, x = LOW[n]
                low = field_ref[f, FIRST + x, t]
                high = field_ref[f, FIRST + HIGH[n][1], t]
            else:
                low, high = both(0, t), both(TX - 2, t)
            first_ref[2 * n + t] = jnp.where(even, high, low)
            second_ref[2 * n + t] = jnp.where(even, low, high)


def y_masks(lanes):
    gy = lax.axis_index("gy")
    has_right = gy < lax.axis_size("gy") - 1
    has_left = gy > 0
    right = {w: (lanes < w) & has_right for w in (2, 3)}
    left = {w: (lanes >= LANES - w) & has_left for w in (2, 3)}
    return left, right


def sides(first_ref, second_ref, axis):
    even = is_even(axis)
    first, second = first_ref[...], second_ref[...]
    return jnp.where(even, second, first), jnp.where(even, first, second)


def side_columns(before, after, f, x, masks):
    w = WIDTH[f]
    at = 16 * (x % 8) + SLOT[f]
    left, right = masks
    a = pltpu.roll(after[x // 8], (LANES - at) % LANES, 1)
    b = pltpu.roll(before[x // 8], (2 * LANES - at - w) % LANES, 1)
    return jnp.where(right[w], a, jnp.where(left[w], b, 0.0))


def corner_kernel(y_first, y_second, first_ref, second_ref):
    lanes = lane_index()
    gy = lax.axis_index("gy")
    before, after = sides(y_first, y_second, "gy")
    before = jnp.where(gy > 0, before, 0.0)
    after = jnp.where(gy < lax.axis_size("gy") - 1, after, 0.0)
    even = is_even("gx")
    packed = []
    for items in (LOW, HIGH):
        both = jnp.zeros((LAYERS, LANES), F32)
        for n, (f, x) in enumerate(items):
            w = WIDTH[f]
            at = 16 * (x % 8) + SLOT[f]
            middle = 8 * n + 3
            for src, start in ((before, middle - w), (after, middle)):
                here = (lanes >= start) & (lanes < start + w)
                by = (start - at) % LANES
                v = src[x // 8]
                both = jnp.where(here, pltpu.roll(v, by, 1) if by else v, both)
        packed.append(both)
    first_ref[...] = jnp.where(even, packed[1], packed[0])
    second_ref[...] = jnp.where(even, packed[0], packed[1])


def newton_row(uref, fref, fields, dst, i):
    width = TILES * LANES
    sub = layer_index(width)
    u, e, h = wide(uref, 0, i), wide(fref, 1, i), wide(fref, 2, i)
    code = wide(fields, CODE, i)
    total = wide(uref, 0, i - 1) + wide(uref, 0, i + 1) + prev_lane(u) + next_lane(u)
    total = total + jnp.where(sub > 0, above(u), 0.0) + jnp.where(sub < LAYERS - 1, below(u), 0.0)
    weight = jnp.where((sub > 0) & (sub < LAYERS - 1), 6.0, 5.0)
    r = total - weight * u + 0.7 * (h - e + pick(code, DOPING))
    diag = weight + 0.7 * (jnp.abs(e) + jnp.abs(h))
    put(dst, 0, i, u + (0.8 * wide(fields, FREE, i)) * (r * recip(diag)))


def face(p, n):
    g = 0.5 * jnp.tanh(n[0] - p[0])
    a = (n[1] - p[1]) - (n[1] + p[1]) * g
    c = (n[2] - p[2]) + (n[2] + p[2]) * g
    return a, c, g


def x_face(uref, fref, i, tiles=TILES):
    p = (wide(uref, 0, i), wide(fref, 1, i), wide(fref, 2, i))
    n = (wide(uref, 0, i + 1), wide(fref, 1, i + 1), wide(fref, 2, i + 1))
    return face([cut(v, tiles) for v in p], [cut(v, tiles) for v in n])


def relax_row(uref, fref, fields, i, before, tiles=TILES):
    sub = layer_index(tiles * LANES)
    here = (wide(uref, 0, i), wide(fref, 1, i), wide(fref, 2, i))
    k = wide(fref, 3, i)
    after = (wide(uref, 0, i + 1), wide(fref, 1, i + 1), wide(fref, 2, i + 1))
    y_after = face(here, tuple(next_lane(v) for v in here))
    y_before = tuple(cut(prev_lane(v), tiles) for v in y_after)
    y_after = tuple(cut(v, tiles) for v in y_after)
    spread = cut(prev_lane(k), tiles) + cut(next_lane(k), tiles)
    here = tuple(cut(v, tiles) for v in here)
    k = cut(k, tiles)
    u, e, h = here
    after = face(here, tuple(cut(v, tiles) for v in after))
    l_after = face(here, tuple(below(v) for v in here))
    l_after = tuple(jnp.where(sub < LAYERS - 1, v, 0.0) for v in l_after)
    l_before = tuple(above(v) for v in l_after)
    net = [
        (after[n] - before[n]) + (y_after[n] - y_before[n]) + (l_after[n] - l_before[n])
        for n in range(3)
    ]
    square = [
        (after[n] * after[n] + before[n] * before[n])
        + (y_after[n] * y_after[n] + y_before[n] * y_before[n])
        + (l_after[n] * l_after[n] + l_before[n] * l_before[n])
        for n in range(2)
    ]
    inner = (sub > 0) & (sub < LAYERS - 1)
    weight = jnp.where(inner, 6.0, 5.0)
    spread = spread + cut(wide(fref, 3, i - 1), tiles) + cut(wide(fref, 3, i + 1), tiles)
    spread = spread + jnp.where(sub > 0, above(k), 0.0)
    spread = spread + jnp.where(sub < LAYERS - 1, below(k), 0.0) - weight * k
    code = cut(wide(fields, CODE, i), tiles)
    free = cut(wide(fields, FREE, i), tiles)
    power = pick(code, POWER_ELEC) * square[0] + pick(code, POWER_HOLE) * square[1]
    recombine = (e * h - 1.0) * recip(e * e + h * h + 2.0)
    step = 0.8 * free
    scale_e = step * recip(weight + net[2])
    scale_h = step * recip(weight - net[2])
    heat_step = free * jnp.where(inner, 0.8 / 3.5, 0.8 / 3.0)
    fixed = (
        e + scale_e * net[0],
        h + scale_h * net[1],
        k + heat_step * (0.5 * spread - 0.5 * k),
    )
    varying = (
        scale_e * recombine * pick(code, LOSS_ELEC),
        scale_h * recombine * pick(code, LOSS_HOLE),
        power,
    )
    return after, fixed, varying, heat_step


def relax_first(uref, fref, fields, dst, sheet_ref, i, before):
    after, fixed, varying, heat_step = relax_row(uref, fref, fields, i, before)
    s = wide(fields, SHEET, i)
    slow = jnp.exp(-0.6 * s)
    fast = jnp.exp(0.3 * s)
    q = varying[2] * slow
    put(dst, 1, i, fixed[0] - varying[0] * fast)
    put(dst, 2, i, fixed[1] - varying[1] * fast)
    put(dst, 3, i, fixed[2] + heat_step * (q + 0.5 * s))
    sheet_ref[pl.ds(i - 2, 1), :] = jnp.sum(q, axis=0, keepdims=True)
    return after


def thermal_row(
    src, anchor, fields, dst, i, halves=(0, 1), source=True, first=False, put_row=put
):
    width = TILES * LANES
    sub = layer_index(width)
    top = sub == 0
    cells = [wide(src, f, i) for f in range(4)]
    code = wide(fields, CODE, i)
    spread = jnp.where(top, pick(code, SPREAD_TOP), pick(code, SPREAD_IN))
    held = 0.9 - jnp.where(top, 5.0, 6.0) * spread
    spread = spread * wide(fields, FREE, i)
    if source:
        heat = jnp.where(top, pick(code, SOURCE_TOP) * wide(fields, SHEET, i), 0.0)
    out = []
    for s in halves:
        for t in range(2):
            f = 2 * s + t
            v = cells[f]
            if s == 0:
                total = wide(src, 2 + t, i - 1) + cells[2 + t]
            else:
                total = cells[t] + wide(src, t, i + 1)
            other = cells[2 * s + 1 - t]
            total = total + other + (prev_lane(other) if t == 0 else next_lane(other))
            total = total + jnp.where(sub > 0, above(v), 0.0)
            total = total + jnp.where(sub < LAYERS - 1, below(v), 0.0)
            value = spread * total + 0.1 * v
            value = value + held * (v if first else wide(anchor, f, i))
            if source:
                value = value + heat
            out.append(value)
            put_row(dst, f, i, value)
    return out


def top_mean(cells):
    total = (cells[0] + cells[1]) + (cells[2] + cells[3])
    return 0.25 * total[0:1, :]


def inner_kernel(field_in, y_first, y_second, field_ref, next_ref, mid_ref, sheet_ref):
    lanes = lane_index()
    masks = y_masks(lanes)
    before, after = sides(y_first, y_second, "gy")
    for x in range(TX):
        for f in range(FIELDS):
            field_ref[f, FIRST + x, 2] = side_columns(before, after, f, x, masks)

    @pl.when(on_device())
    def _():
        def newton(i, carry):
            newton_row(field_ref, field_ref, field_ref, mid_ref, i)
            return carry

        lax.fori_loop(FIRST + 1, FIRST + TX - 1, newton, 0, unroll=UNROLL_NEWTON)

        def relax(i, carry):
            return relax_first(mid_ref, field_ref, field_ref, next_ref, sheet_ref, i, carry)

        start = x_face(mid_ref, field_ref, FIRST + 1)
        lax.fori_loop(FIRST + 2, FIRST + TX - 2, relax, start, unroll=UNROLL_RELAX)

    @pl.when(jnp.logical_not(on_device()))
    def _():
        def one(i, carry):
            thermal_row(field_ref, field_ref, field_ref, mid_ref, i, first=True)
            return carry

        lax.fori_loop(FIRST + 1, FIRST + TX - 1, one, 0, unroll=UNROLL_HEAT)

        def two(i, carry):
            cells = thermal_row(mid_ref, field_ref, field_ref, next_ref, i)
            sheet_ref[pl.ds(i - FIRST, 1), :] = top_mean(cells)
            return carry

        lax.fori_loop(FIRST + 2, FIRST + TX - 2, two, 0, unroll=UNROLL_HEAT)


def rim_kernel(
    field_in, next_in, mid_in, sheet_in, x_first, x_second, side_second, side_first,
    field_ref, next_ref, mid_ref, sheet_ref,
):
    lanes = lane_index()
    sub = layer_index(LANES)
    gx = lax.axis_index("gx")
    has_up = gx > 0
    has_down = gx < lax.axis_size("gx") - 1
    edge = {w: (lanes < w) | (lanes >= LANES - w) for w in (2, 3)}
    even = is_even("gx")

    def up(n):
        return jnp.where(even, x_second[n], x_first[n])

    def down(n):
        return jnp.where(even, x_first[n], x_second[n])

    up_side, down_side = sides(side_first, side_second, "gx")
    for items, src, packed, ok, base in (
        (HIGH, up, up_side, has_up, FIRST - TX),
        (LOW, down, down_side, has_down, FIRST + TX),
    ):
        for n, (f, x) in enumerate(items):
            for t in range(2):
                second = x % 2
                if f < FREE:
                    v = src(2 * n + t)
                elif f == FREE:
                    top = src(2 * BULK + t)[second : second + 1, :]
                    v = jnp.where(sub == 0, jnp.broadcast_to(top, (LAYERS, LANES)), 1.0)
                else:
                    row = src(2 * BULK + t)[4 + 2 * second : 5 + 2 * second, :]
                    v = jnp.broadcast_to(row, (LAYERS, LANES))
                field_ref[f, base + x, t] = jnp.where(ok, v, 0.0)
            side = pltpu.roll(packed, LANES - 8 * n - 3, 1)
            field_ref[f, base + x, 2] = jnp.where(edge[WIDTH[f]] & ok, side, 0.0)

    @pl.when(on_device())
    def _():
        for n in range(3):
            for i in (FIRST - 2 + n, FIRST + TX - 1 + n):
                newton_row(field_ref, field_ref, field_ref, mid_ref, i)
        args = (mid_ref, field_ref, field_ref, next_ref, sheet_ref)
        one = x_face(mid_ref, field_ref, FIRST - 2)
        two = x_face(mid_ref, field_ref, FIRST + TX - 3)
        for n in range(3):
            one = relax_first(*args, FIRST - 1 + n, one)
            two = relax_first(*args, FIRST + TX - 2 + n, two)

    @pl.when(jnp.logical_not(on_device()))
    def _():
        args = (field_ref, field_ref, field_ref, mid_ref)
        thermal_row(*args, FIRST - 2, halves=(1,), first=True)
        thermal_row(*args, FIRST + TX + 1, halves=(0,), first=True)
        for i in (FIRST - 1, FIRST, FIRST + TX - 1, FIRST + TX):
            thermal_row(*args, i, first=True)
        for n in range(3):
            for i in (FIRST - 1 + n, FIRST + TX - 2 + n):
                cells = thermal_row(mid_ref, field_ref, field_ref, next_ref, i)
                if FIRST <= i < FIRST + TX:
                    sheet_ref[pl.ds(i - FIRST, 1), :] = top_mean(cells)


def second_kernel(
    field_ref, next_ref, first_ref, fixed_ref, varying_ref, source_ref, spread_ref, mid_ref
):
    fixed_rows = fixed_ref.reshape(2, 4, LAYERS * TX, LANES)
    varying_rows = varying_ref.reshape(2, 3, LAYERS * TX, LANES)

    def native(ref, f, i, value):
        for t in range(2):
            rows = pl.ds(i - FIRST, LAYERS, stride=TX)
            ref[t, f, rows, :] = value[:, t * LANES : (t + 1) * LANES]

    @pl.when(on_device())
    def _():
        def newton(i, carry):
            newton_row(first_ref, next_ref, field_ref, mid_ref, i)
            return carry

        lax.fori_loop(FIRST - 1, FIRST + TX + 1, newton, 0, unroll=UNROLL_NEWTON)

        def relax(i, before):
            after, fixed, varying, _ = relax_row(mid_ref, next_ref, field_ref, i, before, 2)
            for t in range(2):
                fixed_rows[t, 0, pl.ds(i - FIRST, LAYERS, stride=TX), :] = mid_ref[0, i, t]
            for n in range(3):
                native(fixed_rows, n + 1, i, fixed[n])
                native(varying_rows, n, i, varying[n])
            return after

        start = x_face(mid_ref, next_ref, FIRST - 1, 2)
        lax.fori_loop(FIRST, FIRST + TX, relax, start, unroll=UNROLL_RELAX)

    @pl.when(jnp.logical_not(on_device()))
    def _():
        args = (next_ref, next_ref, field_ref, mid_ref)
        thermal_row(*args, FIRST - 1, halves=(1,), source=False, first=True)
        thermal_row(*args, FIRST + TX, halves=(0,), source=False, first=True)

        def three(i, carry):
            thermal_row(*args, i, source=False, first=True)
            return carry

        lax.fori_loop(FIRST, FIRST + TX, three, 0, unroll=UNROLL_HEAT)

        def four(i, carry):
            def keep(ref, f, i, value):
                native(fixed_rows, f, i, value)

            thermal_row(mid_ref, next_ref, field_ref, None, i, source=False, put_row=keep)
            return carry

        lax.fori_loop(FIRST, FIRST + TX, four, 0, unroll=UNROLL_HEAT)

        def top(i, carry):
            code = jnp.concatenate([field_ref[CODE, i, t] for t in range(TILES)], axis=1)
            inside = wide(field_ref, FREE, i)[0:1, :]
            source_ref[pl.ds(i - FIRST + 1, 1), :] = pick(code[0:1, :], SOURCE_TOP) * inside
            return carry

        lax.fori_loop(FIRST - 1, FIRST + TX + 1, top, 0, unroll=3)

        def sides(i, carry):
            code = jnp.concatenate([field_ref[CODE, i, t] for t in range(2)], axis=1)
            spread_ref[0, pl.ds(i - FIRST, 1), :] = pick(code[0:1, :], SPREAD_TOP)
            spread_ref[1, pl.ds(i - FIRST, 1), :] = pick(code[1:2, :], SPREAD_IN)
            return carry

        lax.fori_loop(FIRST, FIRST + TX, sides, 0, unroll=4)


def last_kernel(
    sheet_ref, fixed_ref, varying_ref, source_ref, spread_ref, contacts,
    state_out, sheet_out, done, total_ref, delta, sem,
):
    def send(src, f, t, layers):
        dst = state_out.at[0, f, layers, :, pl.ds(t * LANES, LANES)]
        return pltpu.make_async_copy(src.at[t, f, layers], dst, sem.at[f, t])

    @pl.when(on_device())
    def _():
        every = pl.ds(0, LAYERS)
        copies = [send(fixed_ref, 0, t, every) for t in range(2)]
        for c in copies:
            c.start()
        s = sheet_ref[0:TX, 0 : 2 * LANES]
        slow = jnp.exp(-0.6 * s)
        fast = jnp.exp(0.3 * s)
        for f in (1, 2, 3):
            for t in range(2):
                cols = slice(t * LANES, (t + 1) * LANES)
                total = jnp.zeros((TX, LANES), F32)
                for layer in range(LAYERS):
                    fixed, varying = fixed_ref[t, f, layer], varying_ref[t, f - 1, layer]
                    if f < 3:
                        done[f, layer, :, cols] = fixed - varying * fast[:, cols]
                        continue
                    q = varying * slow[:, cols]
                    total = total + q
                    step = 0.8 / 3.5 if 0 < layer < LAYERS - 1 else 0.8 / 3.0
                    if layer == 0:
                        step = step * (1.0 - contacts[:, cols].astype(F32))
                    done[f, layer, :, cols] = fixed + step * (q + 0.5 * s[:, cols])
                if f == 3:
                    total_ref[0, :, cols] = total
            copies.append(pltpu.make_async_copy(done.at[f], state_out.at[0, f], sem.at[f, 0]))
            copies[-1].start()
        copies.append(pltpu.make_async_copy(total_ref, sheet_out, sem.at[8, 0]))
        copies[-1].start()
        for c in copies:
            c.wait()

    @pl.when(jnp.logical_not(on_device()))
    def _():
        rest = pl.ds(2, LAYERS - 2)
        copies = [send(fixed_ref, f, t, rest) for t in range(2) for f in range(4)]
        for c in copies:
            c.start()
        delta[...] = source_ref[...] * sheet_ref[...]
        middle = delta[1 : TX + 1, :]
        by_x = (delta[0:TX, :], delta[2 : TX + 2, :])
        by_y = (prev_lane(middle), next_lane(middle))
        more = []
        totals = [jnp.zeros((TX, LANES), F32)] * 2
        for f in range(4):
            for t in range(2):
                cols = slice(t * LANES, (t + 1) * LANES)
                mid = middle[:, cols]
                around = 2.0 * mid + by_x[f // 2][:, cols] + by_y[f % 2][:, cols]
                value = fixed_ref[t, f, 0] + 1.1 * mid + spread_ref[0, :, cols] * around
                done[f, 0, :, cols] = value
                totals[t] = totals[t] + value
                done[f, 1, :, cols] = fixed_ref[t, f, 1] + spread_ref[1, :, cols] * mid
            two = pl.ds(0, 2)
            more.append(
                pltpu.make_async_copy(done.at[f, two], state_out.at[0, f, two], sem.at[4 + f, 0])
            )
            more[-1].start()
        for t in range(2):
            total_ref[0, :, t * LANES : (t + 1) * LANES] = 0.25 * totals[t]
        more.append(pltpu.make_async_copy(total_ref, sheet_out, sem.at[8, 0]))
        more[-1].start()
        for c in copies + more:
            c.wait()


def per_device(grid_state, materials, contacts, received_sheets):
    nx, ny = lax.axis_size("gx"), lax.axis_size("gy")

    def swap(block, axis, parity):
        route = []
        for i in range(nx):
            for j in range(ny):
                at, count = (i, nx) if axis == "gx" else (j, ny)
                to = ((at - parity) ^ 1) + parity
                if axis == "gx":
                    p = (to, j) if 0 <= to < count else (i, j ^ 1)
                else:
                    p = (i, to) if 0 <= to < count else (i ^ 1, j)
                route.append((i * ny + j, p[0] * ny + p[1]))
        return lax.ppermute(block, ("gx", "gy"), route)

    tile = (LAYERS, LANES)
    field_shape = (FIELDS, ROWS, TILES) + tile
    state_shape = (4, ROWS, TILES) + tile
    y_shape, x_shape = (2,) + tile, (2 * BULK + 2,) + tile
    inputs = (grid_state, materials, contacts, received_sheets)
    inputs = [pltpu.with_memory_space_constraint(v, pltpu.HBM) for v in inputs]
    raw_shapes = [
        (2, 4, LAYERS, TX, LANES),
        ((2, LAYERS, TX, LANES), jnp.int32),
        ((TX, 2 * LANES), jnp.int32),
        (1, TX, 2 * LANES),
    ]
    *raw, y_first, y_second = call(
        pack_kernel,
        raw_shapes + [y_shape, y_shape],
        inputs,
        specs=[HBM] * 4,
        scratch=[pltpu.SemaphoreType.DMA((12,))],
    )
    fields, x_first, x_second = call(rows_kernel, [field_shape, x_shape, x_shape], raw)
    y_second = swap(y_second, "gy", 1)
    y_first = swap(y_first, "gy", 0)
    x_second = swap(x_second, "gx", 1)
    x_first = swap(x_first, "gx", 0)
    side_first, side_second = call(corner_kernel, [tile, tile], [y_first, y_second])
    side_second = swap(side_second, "gx", 1)
    side_first = swap(side_first, "gx", 0)
    fields, following, middle, sheet = call(
        inner_kernel,
        [field_shape, state_shape, state_shape, SHEET_SHAPE],
        [fields, y_first, y_second],
        aliases={0: 0},
        cost=INNER,
    )
    fields, following, middle, sheet = call(
        rim_kernel,
        [field_shape, state_shape, state_shape, SHEET_SHAPE],
        [fields, following, middle, sheet, x_first, x_second, side_second, side_first],
        aliases={0: 0, 1: 1, 2: 2, 3: 3},
    )
    swapped = lax.ppermute(sheet, "half", [(0, 1), (1, 0)])
    fixed, varying, source, spread = call(
        second_kernel,
        [
            (2, 4, LAYERS, TX, LANES),
            (2, 3, LAYERS, TX, LANES),
            SHEET_SHAPE,
            (2, TX, 2 * LANES),
        ],
        [fields, following, middle],
        scratch=[pltpu.VMEM(state_shape, F32)],
        cost=1 << 23,
    )
    state, outgoing = call(
        last_kernel,
        [(1, 4, LAYERS, TX, 2 * LANES), (1, TX, 2 * LANES)],
        [swapped, fixed, varying, source, spread, contacts],
        out_specs=[HBM, HBM],
        scratch=[
            pltpu.VMEM((4, LAYERS, TX, 2 * LANES), F32),
            pltpu.VMEM((1, TX, 2 * LANES), F32),
            pltpu.VMEM(SHEET_SHAPE, F32),
            pltpu.SemaphoreType.DMA((9, 2)),
        ],
    )
    return state, outgoing


def solution(mesh):
    placed = (
        P("half", None, None, "gx", "gy"),
        P("half", None, "gx", "gy"),
        P("gx", "gy"),
        P("half", "gx", "gy"),
    )
    return jax.shard_map(
        per_device,
        mesh=mesh,
        in_specs=placed,
        out_specs=(P("half", None, None, "gx", "gy"), P("half", "gx", "gy")),
        check_vma=False,
    )
```

```python
import jax
import jax.numpy as jnp
from jax import lax
from jax.experimental import pallas as pl
from jax.experimental.pallas import tpu as pltpu
from jax.sharding import PartitionSpec as P

F32 = jnp.float32
LAYERS = 8
TX = 16
LANES = 128
TILES = 3
HALO = 3
ROWS = TX + 2 * HALO
FIRST = HALO

DOPING = (1.5, -1.5, 0.6, -0.6)
MOB_ELEC = (1.0, 0.35, 0.7, 0.5)
MOB_HOLE = (0.4, 0.8, 0.3, 0.6)
CONDUCT = (1.0, 0.15, 2.5, 0.5)
CAPACITY = (0.6, 1.2, 0.4, 0.9)
POWER_ELEC = tuple(0.05 * m * m for m in MOB_ELEC)
POWER_HOLE = tuple(0.05 * m * m for m in MOB_HOLE)
LOSS_ELEC = tuple(0.3 / m for m in MOB_ELEC)
LOSS_HOLE = tuple(0.3 / m for m in MOB_HOLE)
SPREAD_TOP = tuple(0.9 * k / (5.0 * k + c) for k, c in zip(CONDUCT, CAPACITY))
SPREAD_IN = tuple(0.9 * k / (6.0 * k + c) for k, c in zip(CONDUCT, CAPACITY))
SOURCE_TOP = tuple(0.45 / (5.0 * k + c) for k, c in zip(CONDUCT, CAPACITY))

CODE, FREE, SHEET = 4, 5, 6
FIELDS = 7
WIDTH = (3, 2, 2, 2, 2, 2, 2)
SLOT = (0, 3, 5, 7, 9, 11, 13)
LOW = [(f, r) for f in range(FIELDS) for r in range(WIDTH[f])]
HIGH = [(f, TX - WIDTH[f] + r) for f in range(FIELDS) for r in range(WIDTH[f])]
BULK = sum(1 for f, _ in LOW if f < FREE)
VMEM = pl.BlockSpec(memory_space=pltpu.VMEM)
HBM = pl.BlockSpec(memory_space=pltpu.HBM)
SHEET_SHAPE = (24, TILES * LANES)
INNER = 10**10
UNROLL_NEWTON, UNROLL_RELAX, UNROLL_HEAT = 2, 4, 2


def call(kernel, outs, ins, specs=None, out_specs=None, scratch=(), aliases=None, cost=1 << 20):
    return pl.pallas_call(
        kernel,
        out_shape=[
            jax.ShapeDtypeStruct(*(s if isinstance(s[0], tuple) else (s, F32))) for s in outs
        ],
        in_specs=specs or [VMEM] * len(ins),
        out_specs=out_specs or [VMEM] * len(outs),
        scratch_shapes=list(scratch),
        input_output_aliases=aliases or {},
        compiler_params=pltpu.CompilerParams(vmem_limit_bytes=12 << 20),
        cost_estimate=pl.CostEstimate(flops=cost, bytes_accessed=1 << 20, transcendentals=0),
    )(*ins)


def lane_index():
    return lax.broadcasted_iota(jnp.int32, (LAYERS, LANES), 1)


def layer_index(width):
    return lax.broadcasted_iota(jnp.int32, (LAYERS, width), 0)


def pick(code, table):
    low = jnp.where(code < 0.5, table[0], table[1])
    high = jnp.where(code < 2.5, table[2], table[3])
    return jnp.where(code < 1.5, low, high)


def wide(ref, f, i):
    return jnp.concatenate([ref[f, i, t] for t in range(TILES)], axis=1)


def put(ref, f, i, value):
    for t in range(TILES):
        ref[f, i, t] = value[:, t * LANES : (t + 1) * LANES]


def cut(v, tiles):
    return v if v.shape[1] == tiles * LANES else v[:, : tiles * LANES]


def recip(v):
    r = pl.reciprocal(v, approx=True)
    return r * (2.0 - v * r)


def prev_lane(v):
    return pltpu.roll(v, 1, 1)


def next_lane(v):
    return pltpu.roll(v, v.shape[1] - 1, 1)


def above(v):
    return pltpu.roll(v, 1, 0)


def below(v):
    return pltpu.roll(v, LAYERS - 1, 0)


def on_device():
    return lax.axis_index("half") == 0


def is_even(axis):
    return lax.axis_index(axis) % 2 == 0


def own_row(raw_rows, code_rows, contact_ref, sheet_ref, device, sub, f, x, t):
    cols = slice(t * LANES, (t + 1) * LANES)
    if f < 4:
        return raw_rows[t, f, pl.ds(x, LAYERS, stride=TX), :]
    if f == CODE:
        return code_rows[t, pl.ds(x, LAYERS, stride=TX), :].astype(F32)
    if f == FREE:
        held = jnp.broadcast_to(contact_ref[x : x + 1, cols], (LAYERS, LANES))
        return jnp.where((held == 1) & (sub == 0) & device, 0.0, 1.0)
    return jnp.broadcast_to(sheet_ref[0, x : x + 1, cols], (LAYERS, LANES))


def pack_kernel(
    grid, codes, contacts, sheets, raw, raw_code, raw_contact, raw_sheet, first_ref, second_ref, sem
):
    small = [
        pltpu.make_async_copy(contacts, raw_contact, sem.at[10]),
        pltpu.make_async_copy(sheets, raw_sheet, sem.at[11]),
    ]
    copies = []
    for t in range(2):
        cols = pl.ds(t * LANES, LANES)
        copies.append(
            [
                pltpu.make_async_copy(grid.at[0, f, :, :, cols], raw.at[t, f], sem.at[5 * t + f])
                for f in range(4)
            ]
        )
        copies[t].append(
            pltpu.make_async_copy(codes.at[0, :, :, cols], raw_code.at[t], sem.at[5 * t + 4])
        )
    for c in copies[0] + small + copies[1]:
        c.start()
    lanes = lane_index()
    even = is_even("gy")
    raw_rows = raw.reshape(2, 4, LAYERS * TX, LANES)
    code_rows = raw_code.reshape(2, LAYERS * TX, LANES)
    args = (raw_rows, code_rows, raw_contact, raw_sheet, on_device(), layer_index(LANES))
    for c in small:
        c.wait()
    packed = []
    for t in range(2):
        for c in copies[t]:
            c.wait()
        for block in range(2):
            side = jnp.zeros((LAYERS, LANES), F32)
            for row in range(8):
                for f in range(FIELDS):
                    w = WIDTH[f]
                    at = 16 * row + SLOT[f]
                    here = (lanes >= at) & (lanes < at + w)
                    v = own_row(*args, f, 8 * block + row, t)
                    by = (at + t * w) % LANES
                    side = jnp.where(here, pltpu.roll(v, by, 1) if by else v, side)
            packed.append(side)
    for block in range(2):
        left, right = packed[block], packed[2 + block]
        first_ref[block] = jnp.where(even, right, left)
        second_ref[block] = jnp.where(even, left, right)


def rows_kernel(raw, raw_code, raw_contact, raw_sheet, field_ref, first_ref, second_ref):
    sub = layer_index(LANES)
    even = is_even("gx")
    raw_rows = raw.reshape(2, 4, LAYERS * TX, LANES)
    code_rows = raw_code.reshape(2, LAYERS * TX, LANES)
    args = (raw_rows, code_rows, raw_contact, raw_sheet, on_device(), sub)
    for f in range(FIELDS):
        for x in range(TX):
            for t in range(2):
                field_ref[f, FIRST + x, t] = own_row(*args, f, x, t)

    def both(x, t):
        free = [field_ref[FREE, FIRST + x + n, t] for n in range(2)]
        sheet = [field_ref[SHEET, FIRST + x + n, t] for n in range(2)]
        v = jnp.where(sub == 0, free[0], pltpu.roll(free[1], 1, 0))
        v = jnp.where(sub < 2, v, 1.0)
        return jnp.where(sub < 4, v, jnp.where(sub < 6, sheet[0], sheet[1]))

    for n in range(BULK + 1):
        for t in range(2):
            if n < BULK:
                f, x = LOW[n]
                low = field_ref[f, FIRST + x, t]
                high = field_ref[f, FIRST + HIGH[n][1], t]
            else:
                low, high = both(0, t), both(TX - 2, t)
            first_ref[2 * n + t] = jnp.where(even, high, low)
            second_ref[2 * n + t] = jnp.where(even, low, high)


def y_masks(lanes):
    gy = lax.axis_index("gy")
    has_right = gy < lax.axis_size("gy") - 1
    has_left = gy > 0
    right = {w: (lanes < w) & has_right for w in (2, 3)}
    left = {w: (lanes >= LANES - w) & has_left for w in (2, 3)}
    return left, right


def sides(first_ref, second_ref, axis):
    even = is_even(axis)
    first, second = first_ref[...], second_ref[...]
    return jnp.where(even, second, first), jnp.where(even, first, second)


def side_columns(before, after, f, x, masks):
    w = WIDTH[f]
    at = 16 * (x % 8) + SLOT[f]
    left, right = masks
    a = pltpu.roll(after[x // 8], (LANES - at) % LANES, 1)
    b = pltpu.roll(before[x // 8], (2 * LANES - at - w) % LANES, 1)
    return jnp.where(right[w], a, jnp.where(left[w], b, 0.0))


def corner_kernel(y_second, y_first, first_ref, second_ref):
    lanes = lane_index()
    gy = lax.axis_index("gy")
    before, after = sides(y_first, y_second, "gy")
    before = jnp.where(gy > 0, before, 0.0)
    after = jnp.where(gy < lax.axis_size("gy") - 1, after, 0.0)
    even = is_even("gx")
    packed = []
    for items in (LOW, HIGH):
        both = jnp.zeros((LAYERS, LANES), F32)
        for n, (f, x) in enumerate(items):
            w = WIDTH[f]
            at = 16 * (x % 8) + SLOT[f]
            middle = 8 * n + 3
            for src, start in ((before, middle - w), (after, middle)):
                here = (lanes >= start) & (lanes < start + w)
                by = (start - at) % LANES
                v = src[x // 8]
                both = jnp.where(here, pltpu.roll(v, by, 1) if by else v, both)
        packed.append(both)
    first_ref[...] = jnp.where(even, packed[1], packed[0])
    second_ref[...] = jnp.where(even, packed[0], packed[1])


def newton_row(uref, fref, fields, dst, i):
    width = TILES * LANES
    sub = layer_index(width)
    u, e, h = wide(uref, 0, i), wide(fref, 1, i), wide(fref, 2, i)
    code = wide(fields, CODE, i)
    total = wide(uref, 0, i - 1) + wide(uref, 0, i + 1) + prev_lane(u) + next_lane(u)
    total = total + jnp.where(sub > 0, above(u), 0.0) + jnp.where(sub < LAYERS - 1, below(u), 0.0)
    weight = jnp.where((sub > 0) & (sub < LAYERS - 1), 6.0, 5.0)
    r = total - weight * u + 0.7 * (h - e + pick(code, DOPING))
    diag = weight + 0.7 * (jnp.abs(e) + jnp.abs(h))
    put(dst, 0, i, u + (0.8 * wide(fields, FREE, i)) * (r * recip(diag)))


def face(p, n):
    g = 0.5 * jnp.tanh(n[0] - p[0])
    a = (n[1] - p[1]) - (n[1] + p[1]) * g
    c = (n[2] - p[2]) + (n[2] + p[2]) * g
    return a, c, g


def x_face(uref, fref, i, tiles=TILES):
    p = (wide(uref, 0, i), wide(fref, 1, i), wide(fref, 2, i))
    n = (wide(uref, 0, i + 1), wide(fref, 1, i + 1), wide(fref, 2, i + 1))
    return face([cut(v, tiles) for v in p], [cut(v, tiles) for v in n])


def relax_row(uref, fref, fields, i, before, tiles=TILES):
    sub = layer_index(tiles * LANES)
    here = (wide(uref, 0, i), wide(fref, 1, i), wide(fref, 2, i))
    k = wide(fref, 3, i)
    after = (wide(uref, 0, i + 1), wide(fref, 1, i + 1), wide(fref, 2, i + 1))
    y_after = face(here, tuple(next_lane(v) for v in here))
    y_before = tuple(cut(prev_lane(v), tiles) for v in y_after)
    y_after = tuple(cut(v, tiles) for v in y_after)
    spread = cut(prev_lane(k), tiles) + cut(next_lane(k), tiles)
    here = tuple(cut(v, tiles) for v in here)
    k = cut(k, tiles)
    u, e, h = here
    after = face(here, tuple(cut(v, tiles) for v in after))
    l_after = face(here, tuple(below(v) for v in here))
    l_after = tuple(jnp.where(sub < LAYERS - 1, v, 0.0) for v in l_after)
    l_before = tuple(above(v) for v in l_after)
    net = [
        (after[n] - before[n]) + (y_after[n] - y_before[n]) + (l_after[n] - l_before[n])
        for n in range(3)
    ]
    square = [
        (after[n] * after[n] + before[n] * before[n])
        + (y_after[n] * y_after[n] + y_before[n] * y_before[n])
        + (l_after[n] * l_after[n] + l_before[n] * l_before[n])
        for n in range(2)
    ]
    inner = (sub > 0) & (sub < LAYERS - 1)
    weight = jnp.where(inner, 6.0, 5.0)
    spread = spread + cut(wide(fref, 3, i - 1), tiles) + cut(wide(fref, 3, i + 1), tiles)
    spread = spread + jnp.where(sub > 0, above(k), 0.0)
    spread = spread + jnp.where(sub < LAYERS - 1, below(k), 0.0) - weight * k
    code = cut(wide(fields, CODE, i), tiles)
    free = cut(wide(fields, FREE, i), tiles)
    power = pick(code, POWER_ELEC) * square[0] + pick(code, POWER_HOLE) * square[1]
    recombine = (e * h - 1.0) * recip(e * e + h * h + 2.0)
    step = 0.8 * free
    scale_e = step * recip(weight + net[2])
    scale_h = step * recip(weight - net[2])
    heat_step = free * jnp.where(inner, 0.8 / 3.5, 0.8 / 3.0)
    fixed = (
        e + scale_e * net[0],
        h + scale_h * net[1],
        k + heat_step * (0.5 * spread - 0.5 * k),
    )
    varying = (
        scale_e * recombine * pick(code, LOSS_ELEC),
        scale_h * recombine * pick(code, LOSS_HOLE),
        power,
    )
    return after, fixed, varying, heat_step


def relax_first(uref, fref, fields, dst, sheet_ref, i, before):
    after, fixed, varying, heat_step = relax_row(uref, fref, fields, i, before)
    s = wide(fields, SHEET, i)
    slow = jnp.exp(-0.6 * s)
    fast = jnp.exp(0.3 * s)
    q = varying[2] * slow
    put(dst, 1, i, fixed[0] - varying[0] * fast)
    put(dst, 2, i, fixed[1] - varying[1] * fast)
    put(dst, 3, i, fixed[2] + heat_step * (q + 0.5 * s))
    sheet_ref[pl.ds(i - 2, 1), :] = jnp.sum(q, axis=0, keepdims=True)
    return after


def thermal_row(
    src, anchor, fields, dst, i, halves=(0, 1), source=True, first=False, put_row=put
):
    width = TILES * LANES
    sub = layer_index(width)
    top = sub == 0
    cells = [wide(src, f, i) for f in range(4)]
    code = wide(fields, CODE, i)
    spread = jnp.where(top, pick(code, SPREAD_TOP), pick(code, SPREAD_IN))
    held = 0.9 - jnp.where(top, 5.0, 6.0) * spread
    spread = spread * wide(fields, FREE, i)
    if source:
        heat = jnp.where(top, pick(code, SOURCE_TOP) * wide(fields, SHEET, i), 0.0)
    out = []
    for s in halves:
        for t in range(2):
            f = 2 * s + t
            v = cells[f]
            if s == 0:
                total = wide(src, 2 + t, i - 1) + cells[2 + t]
            else:
                total = cells[t] + wide(src, t, i + 1)
            other = cells[2 * s + 1 - t]
            total = total + other + (prev_lane(other) if t == 0 else next_lane(other))
            total = total + jnp.where(sub > 0, above(v), 0.0)
            total = total + jnp.where(sub < LAYERS - 1, below(v), 0.0)
            value = spread * total + 0.1 * v
            value = value + held * (v if first else wide(anchor, f, i))
            if source:
                value = value + heat
            out.append(value)
            put_row(dst, f, i, value)
    return out


def top_mean(cells):
    total = (cells[0] + cells[1]) + (cells[2] + cells[3])
    return 0.25 * total[0:1, :]


def inner_kernel(field_in, y_second, y_first, field_ref, next_ref, mid_ref, sheet_ref):
    lanes = lane_index()
    masks = y_masks(lanes)
    before, after = sides(y_first, y_second, "gy")
    for x in range(TX):
        for f in range(FIELDS):
            field_ref[f, FIRST + x, 2] = side_columns(before, after, f, x, masks)

    @pl.when(on_device())
    def _():
        def newton(i, carry):
            newton_row(field_ref, field_ref, field_ref, mid_ref, i)
            return carry

        lax.fori_loop(FIRST + 1, FIRST + TX - 1, newton, 0, unroll=UNROLL_NEWTON)

        def relax(i, carry):
            return relax_first(mid_ref, field_ref, field_ref, next_ref, sheet_ref, i, carry)

        start = x_face(mid_ref, field_ref, FIRST + 1)
        lax.fori_loop(FIRST + 2, FIRST + TX - 2, relax, start, unroll=UNROLL_RELAX)

    @pl.when(jnp.logical_not(on_device()))
    def _():
        def one(i, carry):
            thermal_row(field_ref, field_ref, field_ref, mid_ref, i, first=True)
            return carry

        lax.fori_loop(FIRST + 1, FIRST + TX - 1, one, 0, unroll=UNROLL_HEAT)

        def two(i, carry):
            cells = thermal_row(mid_ref, field_ref, field_ref, next_ref, i)
            sheet_ref[pl.ds(i - FIRST, 1), :] = top_mean(cells)
            return carry

        lax.fori_loop(FIRST + 2, FIRST + TX - 2, two, 0, unroll=UNROLL_HEAT)


def rim_kernel(
    field_in, next_in, mid_in, sheet_in, x_first, x_second, side_second, side_first,
    field_ref, next_ref, mid_ref, sheet_ref,
):
    lanes = lane_index()
    sub = layer_index(LANES)
    gx = lax.axis_index("gx")
    has_up = gx > 0
    has_down = gx < lax.axis_size("gx") - 1
    edge = {w: (lanes < w) | (lanes >= LANES - w) for w in (2, 3)}
    up, down = sides(x_first, x_second, "gx")
    up_side, down_side = sides(side_first, side_second, "gx")
    for items, src, packed, ok, base in (
        (HIGH, up, up_side, has_up, FIRST - TX),
        (LOW, down, down_side, has_down, FIRST + TX),
    ):
        for n, (f, x) in enumerate(items):
            for t in range(2):
                second = x % 2
                if f < FREE:
                    v = src[2 * n + t]
                elif f == FREE:
                    top = src[2 * BULK + t][second : second + 1, :]
                    v = jnp.where(sub == 0, jnp.broadcast_to(top, (LAYERS, LANES)), 1.0)
                else:
                    row = src[2 * BULK + t][4 + 2 * second : 5 + 2 * second, :]
                    v = jnp.broadcast_to(row, (LAYERS, LANES))
                field_ref[f, base + x, t] = jnp.where(ok, v, 0.0)
            side = pltpu.roll(packed, LANES - 8 * n - 3, 1)
            field_ref[f, base + x, 2] = jnp.where(edge[WIDTH[f]] & ok, side, 0.0)

    @pl.when(on_device())
    def _():
        for n in range(3):
            for i in (FIRST - 2 + n, FIRST + TX - 1 + n):
                newton_row(field_ref, field_ref, field_ref, mid_ref, i)
        args = (mid_ref, field_ref, field_ref, next_ref, sheet_ref)
        one = x_face(mid_ref, field_ref, FIRST - 2)
        two = x_face(mid_ref, field_ref, FIRST + TX - 3)
        for n in range(3):
            one = relax_first(*args, FIRST - 1 + n, one)
            two = relax_first(*args, FIRST + TX - 2 + n, two)

    @pl.when(jnp.logical_not(on_device()))
    def _():
        args = (field_ref, field_ref, field_ref, mid_ref)
        thermal_row(*args, FIRST - 2, halves=(1,), first=True)
        thermal_row(*args, FIRST + TX + 1, halves=(0,), first=True)
        for i in (FIRST - 1, FIRST, FIRST + TX - 1, FIRST + TX):
            thermal_row(*args, i, first=True)
        for n in range(3):
            for i in (FIRST - 1 + n, FIRST + TX - 2 + n):
                cells = thermal_row(mid_ref, field_ref, field_ref, next_ref, i)
                if FIRST <= i < FIRST + TX:
                    sheet_ref[pl.ds(i - FIRST, 1), :] = top_mean(cells)


def second_kernel(
    field_ref, next_ref, first_ref, fixed_ref, varying_ref, source_ref, spread_ref, mid_ref
):
    fixed_rows = fixed_ref.reshape(2, 4, LAYERS * TX, LANES)
    varying_rows = varying_ref.reshape(2, 3, LAYERS * TX, LANES)

    def native(ref, f, i, value):
        for t in range(2):
            rows = pl.ds(i - FIRST, LAYERS, stride=TX)
            ref[t, f, rows, :] = value[:, t * LANES : (t + 1) * LANES]

    @pl.when(on_device())
    def _():
        def newton(i, carry):
            newton_row(first_ref, next_ref, field_ref, mid_ref, i)
            return carry

        lax.fori_loop(FIRST - 1, FIRST + TX + 1, newton, 0, unroll=UNROLL_NEWTON)

        def relax(i, before):
            after, fixed, varying, _ = relax_row(mid_ref, next_ref, field_ref, i, before, 2)
            for t in range(2):
                fixed_rows[t, 0, pl.ds(i - FIRST, LAYERS, stride=TX), :] = mid_ref[0, i, t]
            for n in range(3):
                native(fixed_rows, n + 1, i, fixed[n])
                native(varying_rows, n, i, varying[n])
            return after

        start = x_face(mid_ref, next_ref, FIRST - 1, 2)
        lax.fori_loop(FIRST, FIRST + TX, relax, start, unroll=UNROLL_RELAX)

    @pl.when(jnp.logical_not(on_device()))
    def _():
        args = (next_ref, next_ref, field_ref, mid_ref)
        thermal_row(*args, FIRST - 1, halves=(1,), source=False, first=True)
        thermal_row(*args, FIRST + TX, halves=(0,), source=False, first=True)

        def three(i, carry):
            thermal_row(*args, i, source=False, first=True)
            return carry

        lax.fori_loop(FIRST, FIRST + TX, three, 0, unroll=UNROLL_HEAT)

        def four(i, carry):
            def keep(ref, f, i, value):
                native(fixed_rows, f, i, value)

            thermal_row(mid_ref, next_ref, field_ref, None, i, source=False, put_row=keep)
            return carry

        lax.fori_loop(FIRST, FIRST + TX, four, 0, unroll=UNROLL_HEAT)

        def top(i, carry):
            code = jnp.concatenate([field_ref[CODE, i, t] for t in range(TILES)], axis=1)
            inside = wide(field_ref, FREE, i)[0:1, :]
            source_ref[pl.ds(i - FIRST + 1, 1), :] = pick(code[0:1, :], SOURCE_TOP) * inside
            return carry

        lax.fori_loop(FIRST - 1, FIRST + TX + 1, top, 0, unroll=3)

        def sides(i, carry):
            code = jnp.concatenate([field_ref[CODE, i, t] for t in range(2)], axis=1)
            spread_ref[0, pl.ds(i - FIRST, 1), :] = pick(code[0:1, :], SPREAD_TOP)
            spread_ref[1, pl.ds(i - FIRST, 1), :] = pick(code[1:2, :], SPREAD_IN)
            return carry

        lax.fori_loop(FIRST, FIRST + TX, sides, 0, unroll=4)


def last_kernel(
    sheet_ref, fixed_ref, varying_ref, source_ref, spread_ref, contacts,
    state_out, sheet_out, done, total_ref, delta, sem,
):
    def send(src, f, t, layers):
        dst = state_out.at[0, f, layers, :, pl.ds(t * LANES, LANES)]
        return pltpu.make_async_copy(src.at[t, f, layers], dst, sem.at[f, t])

    @pl.when(on_device())
    def _():
        every = pl.ds(0, LAYERS)
        copies = [send(fixed_ref, 0, t, every) for t in range(2)]
        for c in copies:
            c.start()
        for t in range(2):
            cols = slice(t * LANES, (t + 1) * LANES)
            s = sheet_ref[0:TX, cols]
            slow = jnp.exp(-0.6 * s)
            fast = jnp.exp(0.3 * s)
            total = jnp.zeros((TX, LANES), F32)
            for layer in range(LAYERS):
                for f in (1, 2):
                    done[t, f, layer] = (
                        fixed_ref[t, f, layer] - varying_ref[t, f - 1, layer] * fast
                    )
                q = varying_ref[t, 2, layer] * slow
                total = total + q
                step = 0.8 / 3.5 if 0 < layer < LAYERS - 1 else 0.8 / 3.0
                if layer == 0:
                    step = step * (1.0 - contacts[:, cols].astype(F32))
                done[t, 3, layer] = fixed_ref[t, 3, layer] + step * (q + 0.5 * s)
            total_ref[0, :, cols] = total
            for f in (1, 2, 3):
                copies.append(send(done, f, t, every))
                copies[-1].start()
        copies.append(pltpu.make_async_copy(total_ref, sheet_out, sem.at[8, 0]))
        copies[-1].start()
        for c in copies:
            c.wait()

    @pl.when(jnp.logical_not(on_device()))
    def _():
        rest = pl.ds(2, LAYERS - 2)
        copies = [send(fixed_ref, f, t, rest) for t in range(2) for f in range(4)]
        for c in copies:
            c.start()
        delta[...] = source_ref[...] * sheet_ref[...]
        middle = delta[1 : TX + 1, :]
        by_x = (delta[0:TX, :], delta[2 : TX + 2, :])
        by_y = (prev_lane(middle), next_lane(middle))
        more = []
        for t in range(2):
            cols = slice(t * LANES, (t + 1) * LANES)
            mid = middle[:, cols]
            total = jnp.zeros((TX, LANES), F32)
            for f in range(4):
                around = 2.0 * mid + by_x[f // 2][:, cols] + by_y[f % 2][:, cols]
                value = fixed_ref[t, f, 0] + 1.1 * mid + spread_ref[0, :, cols] * around
                done[t, f, 0] = value
                total = total + value
                done[t, f, 1] = fixed_ref[t, f, 1] + spread_ref[1, :, cols] * mid
                dst = state_out.at[0, f, pl.ds(0, 2), :, pl.ds(t * LANES, LANES)]
                more.append(
                    pltpu.make_async_copy(done.at[t, f, pl.ds(0, 2)], dst, sem.at[4 + f, t])
                )
                more[-1].start()
            total_ref[0, :, cols] = 0.25 * total
        more.append(pltpu.make_async_copy(total_ref, sheet_out, sem.at[8, 0]))
        more[-1].start()
        for c in copies + more:
            c.wait()


def per_device(grid_state, materials, contacts, received_sheets):
    nx, ny = lax.axis_size("gx"), lax.axis_size("gy")

    def swap(block, axis, parity):
        route = []
        for i in range(nx):
            for j in range(ny):
                at, count = (i, nx) if axis == "gx" else (j, ny)
                to = ((at - parity) ^ 1) + parity
                if axis == "gx":
                    p = (to, j) if 0 <= to < count else (i, j ^ 1)
                else:
                    p = (i, to) if 0 <= to < count else (i ^ 1, j)
                route.append((i * ny + j, p[0] * ny + p[1]))
        return lax.ppermute(block, ("gx", "gy"), route)

    tile = (LAYERS, LANES)
    field_shape = (FIELDS, ROWS, TILES) + tile
    state_shape = (4, ROWS, TILES) + tile
    y_shape, x_shape = (2,) + tile, (2 * BULK + 2,) + tile
    inputs = (grid_state, materials, contacts, received_sheets)
    inputs = [pltpu.with_memory_space_constraint(v, pltpu.HBM) for v in inputs]
    raw_shapes = [
        (2, 4, LAYERS, TX, LANES),
        ((2, LAYERS, TX, LANES), jnp.int32),
        ((TX, 2 * LANES), jnp.int32),
        (1, TX, 2 * LANES),
    ]
    *raw, y_first, y_second = call(
        pack_kernel,
        raw_shapes + [y_shape, y_shape],
        inputs,
        specs=[HBM] * 4,
        scratch=[pltpu.SemaphoreType.DMA((12,))],
    )
    fields, x_first, x_second = call(rows_kernel, [field_shape, x_shape, x_shape], raw)
    y_second = swap(y_second, "gy", 1)
    y_first = swap(y_first, "gy", 0)
    x_second = swap(x_second, "gx", 1)
    x_first = swap(x_first, "gx", 0)
    side_first, side_second = call(corner_kernel, [tile, tile], [y_second, y_first])
    side_second = swap(side_second, "gx", 1)
    side_first = swap(side_first, "gx", 0)
    fields, following, middle, sheet = call(
        inner_kernel,
        [field_shape, state_shape, state_shape, SHEET_SHAPE],
        [fields, y_second, y_first],
        aliases={0: 0},
        cost=INNER,
    )
    fields, following, middle, sheet = call(
        rim_kernel,
        [field_shape, state_shape, state_shape, SHEET_SHAPE],
        [fields, following, middle, sheet, x_first, x_second, side_second, side_first],
        aliases={0: 0, 1: 1, 2: 2, 3: 3},
    )
    swapped = lax.ppermute(sheet, "half", [(0, 1), (1, 0)])
    fixed, varying, source, spread = call(
        second_kernel,
        [
            (2, 4, LAYERS, TX, LANES),
            (2, 3, LAYERS, TX, LANES),
            SHEET_SHAPE,
            (2, TX, 2 * LANES),
        ],
        [fields, following, middle],
        scratch=[pltpu.VMEM(state_shape, F32)],
        cost=1 << 23,
    )
    state, outgoing = call(
        last_kernel,
        [(1, 4, LAYERS, TX, 2 * LANES), (1, TX, 2 * LANES)],
        [swapped, fixed, varying, source, spread, contacts],
        out_specs=[HBM, HBM],
        scratch=[
            pltpu.VMEM((2, 4, LAYERS, TX, LANES), F32),
            pltpu.VMEM((1, TX, 2 * LANES), F32),
            pltpu.VMEM(SHEET_SHAPE, F32),
            pltpu.SemaphoreType.DMA((9, 2)),
        ],
    )
    return state, outgoing


def solution(mesh):
    placed = (
        P("half", None, None, "gx", "gy"),
        P("half", None, "gx", "gy"),
        P("gx", "gy"),
        P("half", "gx", "gy"),
    )
    return jax.shard_map(
        per_device,
        mesh=mesh,
        in_specs=placed,
        out_specs=(P("half", None, None, "gx", "gy"), P("half", "gx", "gy")),
        check_vma=False,
    )
```
